32 devices in a mesh: rows: 16 (over z, y, x), grp: 2 (over core).
Axes of the slice: x: 2, y: 2, z: 4, core: 2. Of those that a mesh axis runs over, the one named last changes fastest.
Arguments:
- nodes_in: bfloat16 [131072, 384], P(('rows', 'grp')), may hold values from -6 to 6
- out_grad: bfloat16 [131072, 384], P(('rows', 'grp')), may hold values from -6 to 6
- neighbours: int32 [131072, 27], P(('rows', 'grp')), may hold values from -1 to 128, as said below
- node_mask: int32 [131072], P(('rows', 'grp')), may hold values from 0 to 1
- master: float32 [1785856], P(('rows', 'grp')), may hold values from -1.6 to 1.6
- first_moment: float32 [1785856], P(('rows', 'grp')), may hold values from -128 to 128
- second_moment: float32 [1785856], P(('rows', 'grp')), may hold values from 1703.936 to 6946.816
Outputs:
- output: bfloat16 [131072, 384], P(('rows', 'grp'))
- node_grad: float32 [131072, 384], P(('rows', 'grp'))
- new_master: float32 [1785856], P(('rows', 'grp'))
- new_first: float32 [1785856], P(('rows', 'grp'))
- new_second: float32 [1785856], P(('rows', 'grp'))
- new_low: bfloat16 [1785856], P(('rows', 'grp'))
- final_bias_grad: float32 [384], replicated
The draws below stay inside these ranges and needn't reach their ends.
Inputs may be any that keep to these rules, and one draw needn't show every extreme that they name: `neighbours`: entry 13 of every row is 64. Every other entry is either -1 or 64 plus the signed distance in node order from the row's node to a node within 64 positions. Entries 0 and 26 are 0 and 128 wherever those nodes exist.
All inputs are finite; a program needn't handle non-finite values.
Results may differ from the reference program's by a relative error of at most 0.012.
Values may be sent and summed in bfloat16 or wider, within the bound.
A program may use at most 448 MiB of HBM per device.

```python
import math
import jax
import jax.numpy as jnp
from jax import lax

C = 384
HEADS = 12
HD = 32
F = 1536
TOK_DEV = 4096
WINDOW_NODES = 32
WINDOW_DILATION = 4
HALO = 64
STEP = 5
NODES = 131072
PARAMS = 1785856
N_ROWS = 16
N_GRP = 2


def layout_drawn(channels, hidden_units):
    return [('batch_gain', (channels,)), ('batch_shift', (channels,)), ('first_gain', (channels,)), ('first_shift', (channels,)), ('query_bias', (channels,)), ('value_bias', (channels,)), ('output_bias', (channels,)), ('second_gain', (channels,)), ('second_shift', (channels,)), ('hidden_bias', (hidden_units,)), ('final_bias', (channels,)), ('conv_weight', (27, channels)), ('joint_weight', (channels, 3 * channels)), ('output_weight', (channels, channels)), ('hidden_weight', (channels, hidden_units)), ('final_weight', (hidden_units, channels))]


def draw_neighbours(key, part):
    first_key = jax.random.fold_in(key, 11)
    second_key = jax.random.fold_in(key, 12)
    column = lax.broadcasted_iota(jnp.int32, (NODES, 27), 1)
    position = lax.broadcasted_iota(jnp.int32, (NODES, 27), 0)
    offsets = jax.random.randint(first_key, (NODES, 27), -HALO, HALO + 1)
    offsets = jnp.where(column == 0, -HALO, jnp.where(column == 26, HALO, jnp.where(column == 13, 0, offsets)))
    kept = jax.random.randint(second_key, (NODES, 27), 0, 4) > 0
    kept = kept | (column == 0) | (column == 13) | (column == 26)
    target = position + offsets
    inside = kept & (target >= 0) & (target < NODES)
    return jnp.where(inside, offsets + HALO, -1).astype(jnp.int32)


def draw_node_mask(key, part):
    roll = jax.random.randint(jax.random.fold_in(key, 21), (NODES,), 0, 1000)
    position = jnp.arange(NODES, dtype=jnp.int32)
    threshold = 300 + 600 * position // NODES
    return (roll < threshold).astype(jnp.int32)


def draw_master(key, part):
    bases = []
    scales = []
    for segment_name, segment_shape in layout_drawn(C, F):
        entries = math.prod(segment_shape)
        if segment_name in ('batch_gain', 'first_gain', 'second_gain'):
            base_value, scale_value = (1.0, 0.15)
        elif segment_name == 'conv_weight':
            base_value, scale_value = (0.0, 27.0 ** (-0.5))
        elif segment_name == 'output_weight':
            base_value, scale_value = (0.0, 3.0 * C ** (-0.5))
        elif segment_name == 'final_weight':
            base_value, scale_value = (0.0, F ** (-0.5))
        elif segment_name in ('joint_weight', 'hidden_weight'):
            base_value, scale_value = (0.0, C ** (-0.5))
        else:
            base_value, scale_value = (0.0, 0.3)
        bases.append(jnp.full((entries,), base_value, jnp.float32))
        scales.append(jnp.full((entries,), scale_value, jnp.float32))
    used = sum((math.prod(segment_shape) for segment_name, segment_shape in layout_drawn(C, F)))
    bases.append(jnp.zeros((PARAMS - used,), jnp.float32))
    scales.append(jnp.full((PARAMS - used,), 0.05, jnp.float32))
    base_all = jnp.concatenate(bases)
    scale_all = jnp.concatenate(scales)
    noise_key = jax.random.fold_in(key, 31)
    noise = jnp.clip(jax.random.normal(noise_key, (PARAMS,), jnp.float32), -3.0, 3.0)
    return base_all + scale_all * noise


def shard_levels(stream_key, shape, shards, least, largest):
    def one(dim, blocks):
        draws = jax.random.uniform(jax.random.fold_in(jax.random.fold_in(stream_key, 6), dim), (blocks,), jnp.float32, least / len(shards), largest / len(shards))
        return jnp.repeat(jnp.exp(draws), shape[dim] // blocks).reshape((-1,) + (1,) * (len(shape) - dim - 1))

    loudness = one(*shards[0])
    for cut in shards[1:]:
        loudness = loudness * one(*cut)
    return loudness


def scatter_about(stream_key, shape, scale, reach, cuts=(), kind=jnp.bfloat16):
    values = scale * jax.random.normal(stream_key, shape, jnp.float32)
    if cuts:
        values = values * shard_levels(stream_key, shape, cuts, -0.22, 0.18)
    return jnp.clip(values, -reach, reach).astype(kind)


def setup_inputs(seed: int = 0) -> dict:
    splits = jax.random.split(jax.random.key(seed), 8)
    return {
        "nodes_in": scatter_about(splits[0], (NODES, C), 1.0, 6.0, ((0, 32),)),
        "out_grad": scatter_about(splits[1], (NODES, C), 1.0, 6.0, ((0, 32),)),
        "neighbours": draw_neighbours(jax.random.fold_in(splits[7], 71), 0),
        "node_mask": draw_node_mask(jax.random.fold_in(splits[7], 71), 0),
        "master": draw_master(jax.random.fold_in(splits[7], 71), 0),
        "first_moment": scatter_about(splits[5], (PARAMS,), (0.055 * NODES ** 0.5), 128.0, ((0, 32),), jnp.float32),
        "second_moment": jnp.clip(jnp.exp(math.log(6946.816) - 1.40534252 * jax.random.uniform(splits[6], (PARAMS,), jnp.float32) ** shard_levels(splits[6], (PARAMS,), ((0, 32),), -0.2, 0.2)), 1703.936, 6946.816),
    }


eps_norm = 1e-05
highest = lax.Precision.HIGHEST

@jax.custom_vjp
def low(v):
    return lax.optimization_barrier(v.astype(jnp.bfloat16)).astype(jnp.float32)

@jax.custom_vjp
def low_back(v):
    return v

def low_keep(v):
    return (low(v), None)

def low_pass(kept, grad):
    return (grad,)

def back_keep(v):
    return (v, None)

def back_low(kept, grad):
    return (low(grad),)
low.defvjp(low_keep, low_pass)
low_back.defvjp(back_keep, back_low)

def layout(channels, hidden_units):
    return [('batch_gain', (channels,)), ('batch_shift', (channels,)), ('first_gain', (channels,)), ('first_shift', (channels,)), ('query_bias', (channels,)), ('value_bias', (channels,)), ('output_bias', (channels,)), ('second_gain', (channels,)), ('second_shift', (channels,)), ('hidden_bias', (hidden_units,)), ('final_bias', (channels,)), ('conv_weight', (27, channels)), ('joint_weight', (channels, 3 * channels)), ('output_weight', (channels, channels)), ('hidden_weight', (channels, hidden_units)), ('final_weight', (hidden_units, channels))]

def unpack(flat, channels, hidden_units):
    pieces = {}
    offset = 0
    for segment_name, segment_shape in layout(channels, hidden_units):
        entries = math.prod(segment_shape)
        pieces[segment_name] = flat[offset:offset + entries].reshape(segment_shape)
        offset += entries
    return pieces

def layer_norm(value_rows, norm_gain, norm_shift):
    center = value_rows - lax.optimization_barrier(jnp.mean(value_rows, axis=-1, keepdims=True))
    spread = lax.optimization_barrier(jnp.mean(center * center, axis=-1, keepdims=True))
    return center * lax.rsqrt(spread + eps_norm) * norm_gain + norm_shift

def alternate(value_rows):
    trailing_rows = value_rows.shape[1:]
    launch_grid = value_rows.reshape((value_rows.shape[0] // (WINDOW_NODES * WINDOW_DILATION), WINDOW_NODES, WINDOW_DILATION) + trailing_rows)
    return jnp.swapaxes(launch_grid, 1, 2).reshape(value_rows.shape)

def restore(value_rows):
    trailing_rows = value_rows.shape[1:]
    launch_grid = value_rows.reshape((value_rows.shape[0] // (WINDOW_NODES * WINDOW_DILATION), WINDOW_DILATION, WINDOW_NODES) + trailing_rows)
    return jnp.swapaxes(launch_grid, 1, 2).reshape(value_rows.shape)

def window_block(queries, window_keys, window_values, key_live):
    scores = jnp.einsum('wqhd,wkhd->whqk', queries, window_keys, precision=highest) * HD ** (-0.5)
    scores = low_back(scores)
    scores = jnp.where(key_live[:, None, None, :] > 0, scores, -1000000000.0)
    row_max = lax.optimization_barrier(jnp.max(scores, axis=-1, keepdims=True))
    expo = jnp.exp(scores - row_max)
    attention_weights = low(expo / lax.optimization_barrier(jnp.sum(expo, axis=-1, keepdims=True)))
    return jnp.einsum('whqk,wkhd->wqhd', attention_weights, window_values, precision=highest)

def reference(nodes_in, out_grad, neighbours, node_mask, master, first_moment, second_moment):
    device_count = N_ROWS * N_GRP
    live_rows = node_mask.astype(jnp.float32)[:, None]
    mask_windows = alternate(node_mask).reshape(device_count, TOK_DEV // WINDOW_NODES, WINDOW_NODES)
    shard_starts = jnp.arange(device_count, dtype=jnp.int32) * TOK_DEV

    def forward(node_values, flat):
        weights = unpack(low(flat), C, F)

        def conv_block(block_args):
            neighbour_block, shard_start = block_args
            row_place = shard_start + jnp.arange(TOK_DEV, dtype=jnp.int32)[:, None]
            target = row_place + neighbour_block - HALO
            present_bool = neighbour_block >= 0
            safe_index = jnp.where(present_bool, target, 0).astype(jnp.int32)
            present = present_bool.astype(jnp.float32)[:, :, None]
            gathered = node_values[safe_index] * present
            return lax.optimization_barrier(jnp.sum(gathered * weights['conv_weight'][None], axis=1))
        convolved = lax.map(jax.checkpoint(conv_block), (neighbours.reshape(device_count, TOK_DEV, 27), shard_starts))
        convolved = low_back(convolved.reshape(NODES, C))
        live_total = jnp.sum(live_rows)
        average = lax.optimization_barrier(jnp.sum(live_rows * convolved, axis=0)) / live_total
        variance = lax.optimization_barrier(jnp.sum(live_rows * convolved * convolved, axis=0)) / live_total - average * average
        centered = (convolved - average) * lax.rsqrt(variance + eps_norm)
        first_sum = node_values + (centered * weights['batch_gain'] + weights['batch_shift'])
        attend_input = low(layer_norm(first_sum, weights['first_gain'], weights['first_shift']))
        joint_bias = jnp.concatenate([weights['query_bias'], jnp.zeros((C,), jnp.float32), weights['value_bias']])
        projected = jnp.dot(attend_input, weights['joint_weight'], precision=highest) + joint_bias
        projected = low_back(low(projected))
        windowed = alternate(projected)
        block_shape = (device_count, TOK_DEV // WINDOW_NODES, WINDOW_NODES, HEADS, HD)
        queries = windowed[:, :C].reshape(block_shape)
        window_keys = windowed[:, C:2 * C].reshape(block_shape)
        window_values = windowed[:, 2 * C:].reshape(block_shape)
        checked = jax.checkpoint(window_block)
        attended = lax.map(lambda group_args: checked(*group_args), (queries, window_keys, window_values, mask_windows))
        attended = restore(low_back(low(attended.reshape(NODES, C))))
        branch = jnp.dot(attended, weights['output_weight'], precision=highest) + weights['output_bias']
        second_sum = first_sum + low_back(branch)

        def hidden_block(rows_block):
            hidden_input = low(layer_norm(rows_block, weights['second_gain'], weights['second_shift']))
            hidden_pre = low_back(jnp.dot(hidden_input, weights['hidden_weight'], precision=highest) + weights['hidden_bias'])
            activated = low(jax.nn.gelu(hidden_pre))
            return rows_block + (jnp.dot(activated, weights['final_weight'], precision=highest) + weights['final_bias'])
        result = lax.map(jax.checkpoint(hidden_block), second_sum.reshape(device_count, TOK_DEV, C))
        return result.reshape(NODES, C)
    result, pullback = jax.vjp(forward, nodes_in.astype(jnp.float32), master)
    node_grad, flat_grads = pullback(out_grad.astype(jnp.float32))
    position = jnp.arange(PARAMS, dtype=jnp.int32)
    step_rate = jnp.where(position < 10 * C + F, 0.2, 0.03)
    new_first = 0.9 * first_moment + 0.1 * flat_grads
    new_second = 0.95 * second_moment + 0.05 * flat_grads * flat_grads
    first_hat = new_first / (1.0 - 0.9 ** STEP)
    second_hat = new_second / (1.0 - 0.95 ** STEP)
    new_master = master - step_rate * (first_hat / (jnp.sqrt(second_hat) + 1e-08) + 0.01 * master)
    final_bias_grad = flat_grads[9 * C + F:10 * C + F]
    return (result.astype(jnp.bfloat16), node_grad, new_master, new_first, new_second, new_master.astype(jnp.bfloat16), final_bias_grad)
```

```python
import functools

import jax
import jax.numpy as jnp
from jax import lax
from jax.experimental import pallas as pl
from jax.experimental.pallas import tpu as pltpu
from jax.sharding import PartitionSpec as P

C = 384
HEADS = 12
HD = 32
F = 1536
HALO = 64
STEP = 5
EPS = 1e-5
AXES = ("rows", "grp")
F32 = jnp.float32
BF = jnp.bfloat16

BLK = 128
T = 256
ROW_CONV = (10 * C + F) // 128
ROW_JOINT = ROW_CONV + 27 * C // 128
ROW_OUT = ROW_JOINT + C * 3 * C // 128
ROW_HIDDEN = ROW_OUT + C * C // 128
ROW_FINAL = ROW_HIDDEN + C * F // 128
ROW_END = ROW_FINAL + C * F // 128
VMEM = pltpu.CompilerParams(vmem_limit_bytes=60 * 1024 * 1024)


def nn(a, b):
    return jnp.dot(a, b, preferred_element_type=F32)


def nt(a, b):
    return lax.dot_general(a, b, (((1,), (1,)), ((), ())), preferred_element_type=F32)


def whole(*shape):
    return pl.BlockSpec(shape, lambda i: (0,) * len(shape), pipeline_mode=pl.Buffered(1))


def rows_of(width, size):
    return pl.BlockSpec((size, width), lambda i: (i, 0))


def unpack_kernel(flat_ref, wj, wjt, wo, wot, wh, wht, wf, wft, wide):
    wide[...] = flat_ref[...].astype(F32)
    for first, out, out_t in (
        (ROW_JOINT, wj, wjt),
        (ROW_OUT, wo, wot),
        (ROW_HIDDEN, wh, wht),
        (ROW_FINAL, wf, wft),
    ):
        rows, cols = out.shape
        per = cols // 128
        for k in range(per):
            for r in range(0, rows, C):
                piece = wide[pl.ds(first + r * per + k, C, stride=per), :]
                out[r : r + C, k * 128 : (k + 1) * 128] = piece.astype(BF)
                out_t[k * 128 : (k + 1) * 128, r : r + C] = piece.T.astype(BF)


def unpack(flat):
    shapes = []
    for shape in ((C, 3 * C), (C, C), (C, F), (F, C)):
        shapes += [shape, shape[::-1]]
    return pl.pallas_call(
        unpack_kernel,
        out_shape=[jax.ShapeDtypeStruct(s, BF) for s in shapes],
        scratch_shapes=[pltpu.VMEM(flat.shape, F32)],
        compiler_params=VMEM,
    )(flat)


def conv_kernel(near_ref, x_ref, w_ref, mask_ref, conv_ref, sums_ref):
    b = pl.program_id(0)

    @pl.when(b == 0)
    def _():
        sums_ref[...] = jnp.zeros_like(sums_ref)

    window = x_ref[pl.ds(pl.multiple_of(b * BLK, BLK), 2 * BLK), :]
    near = near_ref[...]
    place = near + lax.broadcasted_iota(jnp.int32, near.shape, 0)
    place = jnp.where(near < 0, -1, place).astype(F32).astype(BF)
    lane = lax.broadcasted_iota(jnp.int32, (BLK, 2 * BLK), 1).astype(F32).astype(BF)
    one, zero = jnp.ones((), BF), jnp.zeros((), BF)
    total = jnp.zeros((BLK, C), F32)
    for j in range(27):
        pick = jnp.where(place[:, j : j + 1] == lane, one, zero)
        total += nn(pick, window) * w_ref[j : j + 1, :]
    conv_ref[...] = total
    live = jnp.broadcast_to(mask_ref[0].astype(F32), (BLK, BLK)).T
    live = jnp.concatenate([live] * 3, axis=1)
    kept = total * live
    sums_ref[0] += jnp.sum(kept.reshape(BLK // 8, 8, C), axis=0)
    sums_ref[1] += jnp.sum((kept * total).reshape(BLK // 8, 8, C), axis=0)
    sums_ref[2] += jnp.sum(live.reshape(BLK // 8, 8, C), axis=0)


def convolve(near, extended, weight, mask3):
    n = near.shape[0]
    return pl.pallas_call(
        conv_kernel,
        grid=(n // BLK,),
        in_specs=[
            rows_of(27, BLK),
            whole(*extended.shape),
            whole(27, C),
            pl.BlockSpec((1, 1, 128), lambda i: (i, 0, 0)),
        ],
        out_specs=[rows_of(C, BLK), whole(3, 8, C)],
        out_shape=[jax.ShapeDtypeStruct((n, C), F32), jax.ShapeDtypeStruct((3, 8, C), F32)],
        compiler_params=VMEM,
    )(near, extended, weight, mask3)


def conv_back_kernel(near_ref, delta_ref, x_ref, w_ref, first_ref, grad_ref, dw_ref):
    b = pl.program_id(0)

    @pl.when(b == 0)
    def _():
        dw_ref[...] = jnp.zeros_like(dw_ref)

    start = pl.multiple_of(b * BLK, BLK)
    window = delta_ref[pl.ds(start, 2 * BLK), :]
    near = near_ref[pl.ds(start, 2 * BLK), :]
    place = near + lax.broadcasted_iota(jnp.int32, near.shape, 0) - BLK
    place = jnp.where(near < 0, -1, place).astype(F32)
    place = jnp.concatenate([place, jnp.zeros((2 * BLK, 128 - 27), F32)], axis=1).T.astype(BF)
    target = lax.broadcasted_iota(jnp.int32, (BLK, 2 * BLK), 0).astype(F32).astype(BF)
    one, zero = jnp.ones((), BF), jnp.zeros((), BF)
    x = x_ref[...].astype(F32)
    total = first_ref[...]
    for j in range(27):
        pick = jnp.where(place[j : j + 1, :] == target, one, zero)
        come = nn(pick, window)
        total += come * w_ref[j : j + 1, :]
        dw_ref[j] += jnp.sum((come * x).reshape(BLK // 8, 8, C), axis=0)
    grad_ref[...] = total


def convolve_back(near_ext, delta_ext, nodes, weight, delta_first):
    n = nodes.shape[0]
    return pl.pallas_call(
        conv_back_kernel,
        grid=(n // BLK,),
        in_specs=[
            whole(*near_ext.shape),
            whole(*delta_ext.shape),
            rows_of(C, BLK),
            whole(27, C),
            rows_of(C, BLK),
        ],
        out_specs=[rows_of(C, BLK), whole(27, 8, C)],
        out_shape=[jax.ShapeDtypeStruct((n, C), F32), jax.ShapeDtypeStruct((27, 8, C), F32)],
        compiler_params=VMEM,
    )(near_ext, delta_ext, nodes, weight, delta_first)


def mid_kernel(conv_ref,nodes_ref,dy_ref,mask_ref,bn_ref,vb_ref,wj_ref,wjt_ref,wo_ref,wot_ref,wh_ref,wht_ref,wf_ref,wft_ref,
    out_ref,dfirst_ref,flat_ref,bns_ref,
    gj_ref,go_ref,gh_ref,gf_ref,vs_ref,hb_ref,first_s,second_s,qkv_s,kn_s,vn_s,a_s,o_s,ob_s,do_s,dqkv_s,x_s,acc_s,dx_s):
    step=pl.program_id(0)
    rep=T//128
    @pl.when(step==0)
    def _():
        for r in (gj_ref,go_ref,gh_ref,gf_ref,vs_ref,hb_ref,bns_ref): r[...]=jnp.zeros_like(r)
    def col(i,n=C):
        v=vb_ref[pl.ds(i*C,n),:]
        return jnp.concatenate([v]*rep,axis=1) if rep>1 else v
    def fold(x):
        r=x[:,:128]
        for k in range(1,rep): r=r+x[:,128*k:128*(k+1)]
        return r
    scale_a=bn_ref[0:1,:]; shift_b=bn_ref[1:2,:]; r_row=bn_ref[2:3,:]; ar_row=bn_ref[3:4,:]
    first=nodes_ref[...].astype(F32)+(conv_ref[...]*scale_a+shift_b)
    firstT=first.T
    first_s[...]=firstT
    dy=dy_ref[...]
    dyT32=dy.astype(F32).T
    do_s[...]=dyT32
    def ln(x):
        m=jnp.mean(x,axis=0,keepdims=True); c=x-m
        rs=lax.rsqrt(jnp.mean(c*c,axis=0,keepdims=True)+EPS)
        return c*rs, rs
    xh1,rs1=ln(firstT)
    x1=(xh1*col(2)+col(3)).astype(BF)
    x_s[0]=x1
    q=nn(wjt_ref[0:C,:],x1)+col(4)
    qkv_s[0:C,:]=q.astype(BF)
    k=nn(wjt_ref[C:2*C,:],x1)
    qkv_s[C:2*C,:]=k.astype(BF)
    kn_s[...]=k.T.astype(BF)
    v=nn(wjt_ref[2*C:,:],x1)+col(5)
    qkv_s[2*C:,:]=v.astype(BF)
    vn_s[...]=v.T.astype(BF)
    scale=HD**-0.5
    c2=scale*1.4426950408889634
    pi=lax.broadcasted_iota(jnp.int32,(BLK,BLK),0); qi=lax.broadcasted_iota(jnp.int32,(BLK,BLK),1)
    same=(pi&3)==(qi&3)
    for b in range(rep):
        lv=jnp.broadcast_to(mask_ref[b].astype(F32),(BLK,BLK)).T
        live=(lv>0.5)&same
        bias=jnp.where(same,-1e9/scale,-1e30)
        live2=jnp.concatenate([live,live],axis=1); bias2=jnp.concatenate([bias,bias],axis=1)
        cs=slice(b*BLK,(b+1)*BLK)
        z=jnp.zeros((HD,BLK),BF)
        for g in range(3):
            kg=kn_s[cs,g*128:(g+1)*128]
            for hp in range(2):
                h0=hp*2
                def ex(i):
                    qh=qkv_s[g*128+i*32:g*128+(i+1)*32,cs]
                    return jnp.concatenate([qh if t==i else z for t in range(4)],axis=0)
                s=nn(kg,jnp.concatenate([ex(h0),ex(h0+1)],axis=1))
                s=jnp.where(live2,s,bias2)
                m=jnp.max(s,axis=0,keepdims=True)
                e=jnp.exp2((s-m)*c2)
                l=jnp.sum(e,axis=0,keepdims=True)
                a=(e*(1.0/l)).astype(BF)
                for i in range(2):
                    h=g*4+h0+i
                    ah=a[:,i*128:(i+1)*128]
                    a_s[h,:,cs]=ah
                    o_s[h*32:(h+1)*32,cs]=nn(qkv_s[2*C+h*32:2*C+(h+1)*32,cs],ah)
    ob=o_s[...].astype(BF)
    ob_s[...]=ob
    secondT=first_s[...]+(nn(wot_ref[...],ob)+col(6))
    second_s[...]=secondT
    xh2,rs2=ln(secondT)
    x2=(xh2*col(7)+col(8)).astype(BF)
    x_s[1]=x2
    dyTb=do_s[...].astype(BF)
    FC=384
    c0=0.7978845608028654; c1=0.044715
    for f in range(F//FC):
        fs=slice(f*FC,(f+1)*FC)
        hb=vb_ref[9*C+f*FC:9*C+(f+1)*FC,:]
        hb=jnp.concatenate([hb]*rep,axis=1)
        h=nn(wht_ref[fs,:],x2)+hb
        h2=h*h
        t=jnp.tanh(h*(c0+(c0*c1)*h2))
        p=0.5+0.5*t
        act=(h*p).astype(BF)
        dg=p*(1.0+h*(1.0-p)*(2*c0+(6*c0*c1)*h2))
        da=nn(wf_ref[fs,:],dyTb)
        dp32=da*dg
        dpb=dp32.astype(BF)
        hb_ref[fs,:]+=fold(dpb.astype(F32))
        o=nn(wft_ref[:,fs],act)
        d=nn(wh_ref[:,fs],dpb)
        if f==0:
            acc_s[...]=o; dx_s[...]=d
        else:
            acc_s[...]+=o; dx_s[...]+=d
        gf_ref[fs,:]+=nn(act,dy)
        gh_ref[:,fs]+=nt(x2,dpb)
    outT=second_s[...]+(acc_s[...]+col(15-2))
    out_ref[...]=outT.T.astype(BF)
    def ln_back(x,dx,gain,vi):
        xh,rs=ln(x)
        vs_ref[vi]+=fold(dx*xh)
        vs_ref[vi+1]+=fold(dx)
        dh=dx*gain
        m1=jnp.mean(dh,axis=0,keepdims=True)
        m2=jnp.mean(dh*xh,axis=0,keepdims=True)
        return rs*(dh-m1-xh*m2)
    dsec=do_s[...]+ln_back(second_s[...],dx_s[...],col(7),0)
    second_s[...]=dsec
    dbr=dsec.astype(BF)
    vs_ref[2]+=fold(dbr.astype(F32))
    go_ref[...]+=nt(ob_s[...],dbr)
    dat=nn(wo_ref[...],dbr)
    do_s[...]=dat
    dob=dat.astype(BF)
    for b in range(rep):
        cs=slice(b*BLK,(b+1)*BLK)
        z=jnp.zeros((HD,BLK),BF)
        lrow=mask_ref[b].astype(F32)
        for g in range(3):
            vg=vn_s[cs,g*128:(g+1)*128]
            for hp in range(2):
                h0=hp*2
                def ex(i):
                    qh=dob[g*128+i*32:g*128+(i+1)*32,cs]
                    return jnp.concatenate([qh if t==i else z for t in range(4)],axis=0)
                dA=nn(vg,jnp.concatenate([ex(h0),ex(h0+1)],axis=1))
                for i in range(2):
                    h=g*4+h0+i
                    hs=slice(h*32,(h+1)*32)
                    doh=dob[hs,cs]
                    delta=jnp.sum(doh.astype(F32)*o_s[hs,cs],axis=0,keepdims=True)
                    ah=a_s[h,:,cs]
                    ds=(ah.astype(F32)*(dA[:,i*128:(i+1)*128]-delta)).astype(BF)
                    kh=(qkv_s[C+h*32:C+(h+1)*32,cs].astype(F32)*lrow).astype(BF)
                    dqkv_s[h*32:(h+1)*32,cs]=(nn(kh,ds)*scale).astype(BF)
                    dqkv_s[C+h*32:C+(h+1)*32,cs]=(nt(qkv_s[hs,cs],ds)*(lrow*scale)).astype(BF)
                    dqkv_s[2*C+h*32:2*C+(h+1)*32,cs]=nt(doh,ah).astype(BF)
    vs_ref[3]+=fold(dqkv_s[0:C,:].astype(F32))
    vs_ref[4]+=fold(dqkv_s[2*C:,:].astype(F32))
    gj_ref[...]+=nt(x_s[0],dqkv_s[...])
    dx1=nn(wj_ref[...],dqkv_s[...])
    dfT=second_s[...]+ln_back(first_s[...],dx1,col(2),5)
    df=dfT.T
    dfirst_ref[...]=df
    cen=conv_ref[...]*r_row-ar_row
    bns_ref[0]+=jnp.sum((df*cen).reshape(T//8,8,C),axis=0)
    bns_ref[1]+=jnp.sum(df.reshape(T//8,8,C),axis=0)
    bns_ref[2]+=jnp.sum(dy.astype(F32).reshape(T//8,8,C),axis=0)
    @pl.when(step==pl.num_programs(0)-1)
    def _():
        flat_ref[...]=jnp.zeros_like(flat_ref)
        for vi,row in ((0,21),(1,24),(2,18),(3,12),(4,15),(5,6),(6,9)):
            for i in range(3):
                flat_ref[pl.ds(row+i,1),:]=jnp.sum(vs_ref[vi,i*128:(i+1)*128,:].T,axis=0,keepdims=True)
        for i in range(12):
            flat_ref[pl.ds(27+i,1),:]=jnp.sum(hb_ref[i*128:(i+1)*128,:].T,axis=0,keepdims=True)
        for first,mat in ((ROW_JOINT,gj_ref),(ROW_OUT,go_ref),(ROW_HIDDEN,gh_ref),(ROW_FINAL,gf_ref)):
            rows,cols=mat.shape
            per=cols//128
            for k in range(per):
                for r in range(0,rows,C):
                    flat_ref[pl.ds(first+r*per+k,C,stride=per),:]=mat[r:r+C,k*128:(k+1)*128]


def middle(conv,nodes,dy,mask3,bn,vb,ws,flat_rows):
    n=conv.shape[0]
    row=rows_of(C,T)
    in_specs=[row,row,row,pl.BlockSpec((T//128,1,128),lambda i:(i,0,0)),whole(8,C),whole(*vb.shape)]+[whole(*w.shape) for w in ws]
    outs=[((n,C),BF,row),((n,C),F32,row),((flat_rows,128),F32,whole(flat_rows,128)),((3,8,C),F32,whole(3,8,C))]
    scr=[pltpu.VMEM(s,d) for s,d in (((C,3*C),F32),((C,C),F32),((C,F),F32),((F,C),F32),((7,C,128),F32),((F,128),F32),((C,T),F32),((C,T),F32),((3*C,T),BF),((T,C),BF),((T,C),BF),((HEADS,BLK,T),BF),((C,T),F32),((C,T),BF),((C,T),F32),((3*C,T),BF),((2,C,T),BF),((C,T),F32),((C,T),F32))]
    return pl.pallas_call(mid_kernel,grid=(n//T,),in_specs=in_specs,out_specs=[o[2] for o in outs],
      out_shape=[jax.ShapeDtypeStruct(o[0],o[1]) for o in outs],scratch_shapes=scr,
      compiler_params=VMEM)(conv,nodes,dy,mask3,bn,vb,*ws)


def extended_2(block, width):
    count = lax.axis_size(AXES)
    forward = [(i, i + 1) for i in range(count - 1)]
    backward = [(target, source) for source, target in forward]
    low = lax.ppermute(block[block.shape[0] - width :], AXES, forward)
    high = lax.ppermute(block[:width], AXES, backward)
    return jnp.concatenate([low, block, high], axis=0)


def shards(nodes_in, out_grad, neighbours, node_mask, master, first_moment, second_moment):
    n = nodes_in.shape[0]
    shard = master.shape[0] // 128
    flat = lax.all_gather(
        master.reshape(shard, 128).astype(BF), AXES, axis=0, tiled=True
    )
    weights = unpack(flat)
    vectors = flat[:ROW_CONV].astype(F32).reshape(-1)
    spread = jnp.broadcast_to(vectors[:, None], (vectors.shape[0], 128))
    batch_gain, batch_shift = vectors[:C], vectors[C : 2 * C]
    conv_weight = flat[ROW_CONV:ROW_JOINT].astype(F32).reshape(27, C)
    extended = extended_2(nodes_in, HALO)
    near_ext = extended_2(neighbours, HALO)
    mask3 = node_mask.reshape(n // 128, 1, 128)
    convolved, sums = convolve(neighbours, extended, conv_weight, mask3)
    sums = lax.psum(jnp.sum(sums, axis=1), AXES)
    live_total = sums[2]
    average = sums[0] / live_total
    variance = sums[1] / live_total - average * average
    inverse = lax.rsqrt(variance + EPS)
    norm_rows = jnp.stack(
        [inverse * batch_gain, batch_shift - average * inverse * batch_gain, inverse, average * inverse]
        + [jnp.zeros((C,), F32)] * 4
    )
    output, delta_first, flat_grads, norm_sums = middle(
        convolved, nodes_in, out_grad, mask3, norm_rows, spread, weights, shard * lax.axis_size(AXES)
    )
    norm_sums = lax.psum(jnp.sum(norm_sums, axis=1), AXES)
    gain_total, shift_total, bias_total = norm_sums[0], norm_sums[1], norm_sums[2]
    shard_delta = lax.psum_scatter(flat_grads, AXES, scatter_dimension=0, tiled=True)
    sum_spread = batch_gain * gain_total / inverse
    delta_variance = -0.5 * inverse * inverse * inverse * sum_spread
    delta_average = -batch_gain * shift_total * inverse - 2.0 * average * delta_variance
    live_rows = node_mask.astype(F32)[:, None]
    delta_conv = (
        delta_first * (batch_gain * inverse)
        + live_rows * (delta_average + 2.0 * convolved * delta_variance) / live_total
    ).astype(BF)
    node_grad, conv_grad = convolve_back(
        near_ext, extended_2(delta_conv, HALO), nodes_in, conv_weight, delta_first
    )
    conv_grad = lax.psum(jnp.sum(conv_grad, axis=1), AXES)
    early = jnp.concatenate(
        [
            jnp.concatenate([gain_total, shift_total]).reshape(-1, 128),
            jnp.zeros((ROW_CONV - 2 * C // 128 - C // 128, 128), F32),
            bias_total.reshape(-1, 128),
            conv_grad.reshape(-1, 128),
        ]
    )
    me = lax.axis_index(AXES)
    early = jnp.pad(early, ((0, -early.shape[0] % shard + shard), (0, 0)))
    begin = jnp.minimum(me * shard, early.shape[0] - shard)
    shard_delta = shard_delta + lax.dynamic_slice(early, (begin, 0), (shard, 128))
    shard_delta = shard_delta.reshape(-1)
    position = me * master.shape[0] + lax.iota(jnp.int32, master.shape[0])
    step_rate = jnp.where(position < 10 * C + F, 0.2, 0.03)
    new_first = 0.9 * first_moment + 0.1 * shard_delta
    new_second = 0.95 * second_moment + 0.05 * shard_delta * shard_delta
    first_hat = new_first / (1.0 - 0.9**STEP)
    second_hat = new_second / (1.0 - 0.95**STEP)
    new_master = master - step_rate * (first_hat / (jnp.sqrt(second_hat) + 1e-08) + 0.01 * master)
    return (
        output,
        node_grad,
        new_master,
        new_first,
        new_second,
        new_master.astype(BF),
        bias_total,
    )


def solution(mesh):
    rows, flat = P(AXES, None), P(AXES)
    return jax.shard_map(
        shards,
        mesh=mesh,
        in_specs=(rows, rows, rows, flat, flat, flat, flat),
        out_specs=(rows, rows, flat, flat, flat, flat, P()),
        check_vma=False,
    )
```

```python
import functools

import jax
import jax.numpy as jnp
from jax import lax
from jax.experimental import pallas as pl
from jax.experimental.pallas import tpu as pltpu
from jax.sharding import PartitionSpec as P

C = 384
HEADS = 12
HD = 32
F = 1536
HALO = 64
STEP = 5
EPS = 1e-5
AXES = ("rows", "grp")
F32 = jnp.float32
BF = jnp.bfloat16

BLK = 128
T = 256
ROW_CONV = (10 * C + F) // 128
ROW_JOINT = ROW_CONV + 27 * C // 128
ROW_OUT = ROW_JOINT + C * 3 * C // 128
ROW_HIDDEN = ROW_OUT + C * C // 128
ROW_FINAL = ROW_HIDDEN + C * F // 128
ROW_END = ROW_FINAL + C * F // 128
VMEM = pltpu.CompilerParams(vmem_limit_bytes=60 * 1024 * 1024)


def nn(a, b):
    return jnp.dot(a, b, preferred_element_type=F32)


def nt(a, b):
    return lax.dot_general(a, b, (((1,), (1,)), ((), ())), preferred_element_type=F32)


def whole(*shape):
    return pl.BlockSpec(shape, lambda i: (0,) * len(shape), pipeline_mode=pl.Buffered(1))


def rows_of(width, size):
    return pl.BlockSpec((size, width), lambda i: (i, 0))


MESH = pl.DeviceIdType.MESH


def round_up(value, step):
    return -(-value // step) * step


def my_place():
    return lax.axis_index("rows") * lax.axis_size("grp") + lax.axis_index("grp")


def device(place, cores):
    return (place // cores, place % cores)


def stages_of(count):
    out, stride = [], 1
    while stride < count:
        size = min(8, count // stride)
        out.append((stride, size))
        stride *= size
    return out


def others(me, stride, size):
    mine = (me // stride) % size
    return mine, [(k, me + ((mine + k) % size - mine) * stride) for k in range(1, size)]


def greet(partners, cores):
    barrier = pltpu.get_barrier_semaphore()
    for place in partners:
        pl.semaphore_signal(barrier, inc=1, device_id=device(place, cores), device_id_type=MESH)
    pl.semaphore_wait(barrier, len(partners))


def send(source, target, send_sem, recv_sem, place, cores):
    return pltpu.make_async_remote_copy(
        src_ref=source,
        dst_ref=target,
        send_sem=send_sem,
        recv_sem=recv_sem,
        device_id=device(place, cores),
        device_id_type=MESH,
    )


def all_sum(value, me, count, cores, slots, send_sems, recv_sems):
    for s, (stride, size) in enumerate(stages_of(count)):
        mine, partners = others(me, stride, size)
        slots[s, mine] = value
        copies = [
            send(slots.at[s, mine], slots.at[s, mine], send_sems.at[s, k], recv_sems.at[s, k], place, cores)
            for k, place in partners
        ]
        for copy in copies:
            copy.start()
        for copy in copies:
            copy.wait()
        value = slots[s, 0]
        for i in range(1, size):
            value = value + slots[s, i]
    return value


def sum_scratch(count, rows, width):
    n = len(stages_of(count))
    return [
        pltpu.VMEM((n, 8, rows, width), F32),
        pltpu.SemaphoreType.DMA((n, 8)),
        pltpu.SemaphoreType.DMA((n, 8)),
    ]


def conv_kernel(count, cores, owners, near_ref, nodes_ref, mask_ref, master_ref,
                conv_ref, gathered_ref, first_ref, stats_ref,
                ext, early, weight, sums, own_s, local_sem, halo_send, halo_recv, e_send, e_recv, g_send, g_recv,
                slots, s_send, s_recv):
    step = pl.program_id(0)
    steps = pl.num_programs(0)
    block = (step + 1) % steps
    n = nodes_ref.shape[0]
    shard = master_ref.shape[0]
    padded = gathered_ref.shape[-2]
    half = padded // 2
    e_rows = early.shape[1]
    me = my_place()
    low, high = me % 8, me // 8
    y, x, g = low // 4, (low // 2) % 2, low % 2
    highs = stages_of(count // 8)
    left, right = (me + count - 1) % count, (me + 1) % count

    local = pltpu.make_async_copy(nodes_ref, ext.at[pl.ds(HALO, n)], local_sem.at[0])
    keep = pltpu.make_async_copy(own_s, gathered_ref.at[high, y, x, g], local_sem.at[1])
    to_left = send(nodes_ref.at[pl.ds(0, HALO)], ext.at[pl.ds(HALO + n, HALO)], halo_send.at[0], halo_recv.at[0], left, cores)
    to_right = send(nodes_ref.at[pl.ds(n - HALO, HALO)], ext.at[pl.ds(0, HALO)], halo_send.at[1], halo_recv.at[1], right, cores)

    def high_copies(s):
        stride, size = highs[s]
        mine, partners = others(high, stride, size)
        own = gathered_ref.at[pl.ds(high // stride * stride, stride), y, x, g]
        return [
            send(own, own, g_send.at[s, k], g_recv.at[s, k], place * 8 + low, cores)
            for k, place in partners
        ]

    nh = len(highs)
    y_place, x_place, g_place = me + 4 - 8 * y, me + 2 - 4 * x, me + 1 - 2 * g

    def quad_copies(t):
        top, bottom = pl.ds(0, half), pl.ds(half, half)
        if t == 0:
            a = gathered_ref.at[:, y, x, g, top]
            b = gathered_ref.at[:, y, x, g, bottom]
            to_a, to_b = y_place, x_place
        else:
            a = gathered_ref.at[:, :, x, g, top]
            b = gathered_ref.at[:, y, :, g, bottom]
            to_a, to_b = x_place, y_place
        s = nh + t
        return [send(a, a, g_send.at[s, 0], g_recv.at[s, 0], to_a, cores), send(b, b, g_send.at[s, 1], g_recv.at[s, 1], to_b, cores)]

    def core_copies():
        own = gathered_ref.at[:, :, :, g]
        return [send(own, own, g_send.at[nh + 2, 0], g_recv.at[nh + 2, 0], g_place, cores)]

    plan = [functools.partial(high_copies, s) for s in range(nh)]
    plan += [functools.partial(quad_copies, 0), functools.partial(quad_copies, 1), core_copies]
    cuts = [6] * nh + [11, 19, 27]
    for s in range(nh):
        cuts[s] = 3 + 5 * (s + 1) // nh

    @pl.when(step == 0)
    def _():
        local.start()
        sums[...] = jnp.zeros_like(sums)
        own = jnp.concatenate([master_ref[...], jnp.zeros((padded - shard, 128), F32)], axis=0).astype(BF)
        own_s[...] = own
        keep.start()
        wide = [h for h in range(1, count // 8)]
        partners = [left, right]
        partners += [(high + h) % (count // 8) * 8 + low for h in wide]
        partners += [place for _, place in others(me, 1, 8)[1]]
        greet(partners, cores)
        for o in range(owners):
            @pl.when(low == o)
            def _():
                @pl.when(high == 0)
                def _():
                    early[o] = own[:e_rows]
                    out = [
                        send(early.at[o], early.at[o], e_send.at[o, 8 + h], e_recv.at[o, 0], h * 8 + o, cores)
                        for h in wide
                    ]
                    for copy in out:
                        copy.start()
                    for copy in out:
                        copy.wait_send()
                @pl.when(high > 0)
                def _():
                    send(early.at[o], early.at[o], e_send.at[o, 8], e_recv.at[o, 0], left, cores).wait_recv()
                out = [
                    send(early.at[o], early.at[o], e_send.at[o, k], e_recv.at[o, 1], me + k - o, cores)
                    for k in range(8) if k != o
                ]
                for copy in out:
                    copy.start()
                for copy in out:
                    copy.wait_send()
        to_left.start()
        to_right.start()
        keep.wait()
        for copy in plan[0]():
            copy.start()
        for o in range(owners):
            @pl.when(low != o)
            def _():
                send(early.at[o], early.at[o], e_send.at[o, 8], e_recv.at[o, 1], left, cores).wait_recv()
        for o in range(owners):
            rows = min(shard, e_rows)
            first_ref[pl.ds(o * shard, rows), :] = early[o].astype(F32)[:rows]
        for k in range(3):
            weight[:, k * 128 : (k + 1) * 128] = first_ref[pl.ds(ROW_CONV + k, 27, stride=3), :]
        local.wait()

    for s in range(len(plan)):
        @pl.when(step == cuts[s])
        def _(s=s):
            for copy in plan[s]():
                copy.wait()
            if s + 1 < len(plan):
                for copy in plan[s + 1]():
                    copy.start()

    @pl.when(step == steps - 2)
    def _():
        to_left.wait()
        to_right.wait()

    window = ext[pl.ds(pl.multiple_of(block * BLK, BLK), 2 * BLK), :]
    near = near_ref[...]
    place = near + lax.broadcasted_iota(jnp.int32, near.shape, 0)
    place = jnp.where(near < 0, -1, place).astype(F32).astype(BF)
    lane = lax.broadcasted_iota(jnp.int32, (BLK, 2 * BLK), 1).astype(F32).astype(BF)
    one, zero = jnp.ones((), BF), jnp.zeros((), BF)
    total = jnp.zeros((BLK, C), F32)
    for j in range(27):
        pick = jnp.where(place[:, j : j + 1] == lane, one, zero)
        total += nn(pick, window) * weight[j : j + 1, :]
    conv_ref[...] = total
    live = jnp.broadcast_to(mask_ref[0].astype(F32), (BLK, BLK)).T
    live = jnp.concatenate([live] * 3, axis=1)
    kept = total * live
    sums[0] += jnp.sum(kept.reshape(BLK // 8, 8, C), axis=0)
    sums[1] += jnp.sum((kept * total).reshape(BLK // 8, 8, C), axis=0)
    sums[2] += jnp.sum(live.reshape(BLK // 8, 8, C), axis=0)

    @pl.when(step == steps - 1)
    def _():
        rows = [jnp.sum(sums[i], axis=0, keepdims=True) for i in range(3)]
        rows = jnp.concatenate(rows + [jnp.zeros((5, C), F32)], axis=0)
        stats_ref[...] = all_sum(rows, me, count, cores, slots, s_send, s_recv)


def convolve(near, nodes, mask3, master, count, cores):
    n = nodes.shape[0]
    steps = n // BLK
    shard = master.shape[0]
    padded = round_up(shard, 32)
    owners = -(-ROW_JOINT // shard)
    e_rows = min(padded, round_up(ROW_JOINT, 16))
    turned = lambda i: ((i + 1) % steps, 0)
    stages = len(stages_of(count // 8)) + 3
    first_rows = round_up((owners - 1) * shard + e_rows, 8)
    return pl.pallas_call(
        functools.partial(conv_kernel, count, cores, owners),
        grid=(steps,),
        in_specs=[
            pl.BlockSpec((BLK, 27), turned),
            pl.BlockSpec(memory_space=pl.ANY),
            pl.BlockSpec((1, 1, 128), lambda i: ((i + 1) % steps, 0, 0)),
            whole(shard, 128),
        ],
        out_specs=[
            pl.BlockSpec((BLK, C), turned),
            pl.BlockSpec(memory_space=pl.ANY),
            whole(first_rows, 128),
            whole(8, C),
        ],
        out_shape=[
            jax.ShapeDtypeStruct((n, C), F32),
            jax.ShapeDtypeStruct((count // 8, 2, 2, 2, padded, 128), BF),
            jax.ShapeDtypeStruct((first_rows, 128), F32),
            jax.ShapeDtypeStruct((8, C), F32),
        ],
        scratch_shapes=[
            pltpu.VMEM((n + 2 * HALO, C), BF),
            pltpu.VMEM((owners, e_rows, 128), BF),
            pltpu.VMEM((27, C), F32),
            pltpu.VMEM((3, 8, C), F32),
            pltpu.VMEM((padded, 128), BF),
            pltpu.SemaphoreType.DMA((2,)),
            pltpu.SemaphoreType.DMA((2,)),
            pltpu.SemaphoreType.DMA((2,)),
            pltpu.SemaphoreType.DMA((owners, 8 + count // 8)),
            pltpu.SemaphoreType.DMA((owners, 2)),
            pltpu.SemaphoreType.DMA((stages, 8)),
            pltpu.SemaphoreType.DMA((stages, 8)),
        ]
        + sum_scratch(count, 8, C),
        compiler_params=pltpu.CompilerParams(
            vmem_limit_bytes=60 * 1024 * 1024, collective_id=0, has_side_effects=True
        ),
    )(near, nodes, mask3, master)


def conv_back_kernel(count, cores, owners, near_hbm, first_hbm, conv_hbm, x_ref, mask_ref, sums_ref, stats_ref, rows_ref,
                     grads_ref, master_ref, m_ref, v_ref,
                     grad_ref, master_out, m_out, v_out, low_out, bias_out,
                     near, ext, delta, conv, weight, dw, kept, r1, r2, r3, r4, local_sem, halo_send, halo_recv, g_send, g_recv,
                     slots, s_send, s_recv, wslots, w_send, w_recv, total_s, early_s):
    step = pl.program_id(0)
    steps = pl.num_programs(0)
    block = (step + 1) % steps
    n = first_hbm.shape[0]
    shard = master_ref.shape[0]
    padded = grads_ref.shape[-2]
    half = padded // 2
    me = my_place()
    low, high = me % 8, me // 8
    y, x, g = low // 4, (low // 2) % 2, low % 2
    highs = stages_of(count // 8)[::-1]
    nh = len(highs)
    left, right = (me + count - 1) % count, (me + 1) % count
    y_place, x_place, g_place = me + 4 - 8 * y, me + 2 - 4 * x, me + 1 - 2 * g
    top, bottom = pl.ds(0, half), pl.ds(half, half)

    locals_ = [
        pltpu.make_async_copy(first_hbm, delta, local_sem.at[0]),
        pltpu.make_async_copy(conv_hbm, conv, local_sem.at[1]),
        pltpu.make_async_copy(near_hbm, near.at[pl.ds(HALO, n)], local_sem.at[2]),
        pltpu.make_async_copy(grads_ref.at[:, :, :, g], kept, local_sem.at[3]),
    ]
    near_halo = [
        send(near_hbm.at[pl.ds(0, HALO)], near.at[pl.ds(HALO + n, HALO)], halo_send.at[0], halo_recv.at[0], left, cores),
        send(near_hbm.at[pl.ds(n - HALO, HALO)], near.at[pl.ds(0, HALO)], halo_send.at[1], halo_recv.at[1], right, cores),
    ]
    delta_halo = [
        send(ext.at[pl.ds(HALO, HALO)], ext.at[pl.ds(HALO + n, HALO)], halo_send.at[2], halo_recv.at[2], left, cores),
        send(ext.at[pl.ds(n, HALO)], ext.at[pl.ds(0, HALO)], halo_send.at[3], halo_recv.at[3], right, cores),
    ]

    def core_copies():
        return [send(grads_ref.at[:, :, :, 1 - g], r1, g_send.at[0, 0], g_recv.at[0, 0], g_place, cores)]

    def core_add():
        def body(i, _):
            kept[i // 4, (i // 2) % 2, i % 2] = (
                kept[i // 4, (i // 2) % 2, i % 2].astype(F32) + r1[i // 4, (i // 2) % 2, i % 2].astype(F32)
            ).astype(BF)
            return 0
        lax.fori_loop(0, count // 2, body, 0)

    def quad_copies_0():
        return [
            send(kept.at[:, :, 1 - x, top], r2.at[0], g_send.at[1, 0], g_recv.at[1, 0], x_place, cores),
            send(kept.at[:, 1 - y, :, bottom], r2.at[1], g_send.at[1, 1], g_recv.at[1, 1], y_place, cores),
        ]

    def quad_add_0():
        def body(i, _):
            h, w = i // 2, i % 2
            kept[h, w, x, top] = (
                kept[h, w, x, top].astype(F32) + r2[0, h, w].astype(F32)
            ).astype(BF)
            kept[h, y, w, bottom] = (
                kept[h, y, w, bottom].astype(F32) + r2[1, h, w].astype(F32)
            ).astype(BF)
            return 0
        lax.fori_loop(0, count // 4, body, 0)

    def quad_copies_1():
        return [
            send(kept.at[:, 1 - y, x, top], r3.at[0], g_send.at[2, 0], g_recv.at[2, 0], y_place, cores),
            send(kept.at[:, y, 1 - x, bottom], r3.at[1], g_send.at[2, 1], g_recv.at[2, 1], x_place, cores),
        ]

    def quad_add_1():
        def body(h, _):
            kept[h, y, x, top] = (
                kept[h, y, x, top].astype(F32) + r3[0, h].astype(F32)
            ).astype(BF)
            kept[h, y, x, bottom] = (
                kept[h, y, x, bottom].astype(F32) + r3[1, h].astype(F32)
            ).astype(BF)
            return 0
        lax.fori_loop(0, count // 8, body, 0)

    bases = []
    base = 0
    for stride, size in highs:
        bases.append(base)
        base += (size - 1) * stride

    def high_copies(s):
        stride, size = highs[s]
        mine, partners = others(high, stride, size)
        out = []
        for k, place in partners:
            source = kept.at[pl.ds(place // stride * stride, stride), y, x]
            target = r4.at[pl.ds(bases[s] + (k - 1) * stride, stride)]
            out.append(send(source, target, g_send.at[3 + s, k], g_recv.at[3 + s, k], place * 8 + low, cores))
        return out

    def high_add(s):
        stride, size = highs[s]
        start = high // stride * stride
        def body(i, _):
            value = kept[start + i, y, x].astype(F32)
            for k in range(size - 1):
                value = value + r4[bases[s] + k * stride + i].astype(F32)
            if s == nh - 1:
                total_s[...] = value
            else:
                kept[start + i, y, x] = value.astype(BF)
            return 0
        lax.fori_loop(0, stride, body, 0)

    plan = [(core_copies, core_add), (quad_copies_0, quad_add_0), (quad_copies_1, quad_add_1)]
    plan += [(functools.partial(high_copies, s), functools.partial(high_add, s)) for s in range(nh)]
    cuts = [4, 13, 18] + [18 + 10 * (s + 1) // nh for s in range(nh)]

    @pl.when(step == 0)
    def _():
        for copy in locals_:
            copy.start()
        dw[...] = jnp.zeros_like(dw)
        partners = [left, right]
        partners += [(high + h) % (count // 8) * 8 + low for h in range(1, count // 8)]
        partners += [place for _, place in others(me, 1, 8)[1]]
        greet(partners, cores)
        mine = jnp.concatenate([jnp.sum(sums_ref[i], axis=0, keepdims=True) for i in range(3)] + [jnp.zeros((5, C), F32)], axis=0)
        total = all_sum(mine, me, count, cores, slots, s_send, s_recv)
        for copy in plan[0][0]():
            copy.start()
        for copy in near_halo:
            copy.start()
        gain_total, shift_total = total[0:1], total[1:2]
        bias_out[...] = total[2:3]
        early_s[...] = jnp.zeros_like(early_s)
        for i in range(3):
            early_s[i : i + 1, :] = gain_total[:, i * 128 : (i + 1) * 128]
            early_s[3 + i : 4 + i, :] = shift_total[:, i * 128 : (i + 1) * 128]
            early_s[ROW_CONV - 3 + i : ROW_CONV - 2 + i, :] = total[2:3, i * 128 : (i + 1) * 128]
        for k in range(3):
            weight[:, k * 128 : (k + 1) * 128] = rows_ref[pl.ds(ROW_CONV + k, 27, stride=3), :]
        gain = jnp.concatenate([rows_ref[i : i + 1, :] for i in range(3)], axis=1)
        live_total = stats_ref[2:3]
        average = stats_ref[0:1] / live_total
        variance = stats_ref[1:2] / live_total - average * average
        inverse = lax.rsqrt(variance + EPS)
        delta_variance = -0.5 * inverse * inverse * inverse * (gain * gain_total / inverse)
        delta_average = -gain * shift_total * inverse - 2.0 * average * delta_variance
        a = gain * inverse
        b = delta_average / live_total
        c = 2.0 * delta_variance / live_total
        for copy in locals_:
            copy.wait()

        def body(i, _):
            at = pl.ds(pl.multiple_of(i * BLK, BLK), BLK)
            live = jnp.broadcast_to(mask_ref[i].astype(F32), (BLK, BLK)).T
            live = jnp.concatenate([live] * 3, axis=1)
            value = delta[at, :] * a + live * (b + c * conv[at, :])
            ext[pl.ds(pl.multiple_of(i * BLK + HALO, HALO), BLK), :] = value.astype(BF)
            return 0

        lax.fori_loop(0, steps, body, 0)
        for copy in delta_halo:
            copy.start()

    for s in range(len(plan)):
        @pl.when(step == cuts[s])
        def _(s=s):
            for copy in plan[s][0]():
                copy.wait()
            plan[s][1]()
            if s + 1 < len(plan):
                for copy in plan[s + 1][0]():
                    copy.start()

    @pl.when(step == steps - 2)
    def _():
        for copy in near_halo + delta_halo:
            copy.wait()

    start = pl.multiple_of(block * BLK, BLK)
    window = ext[pl.ds(start, 2 * BLK), :]
    near_w = near[pl.ds(start, 2 * BLK), :]
    place = near_w + lax.broadcasted_iota(jnp.int32, near_w.shape, 0) - BLK
    place = jnp.where(near_w < 0, -1, place).astype(F32)
    place = jnp.concatenate([place, jnp.zeros((2 * BLK, 128 - 27), F32)], axis=1).T.astype(BF)
    target = lax.broadcasted_iota(jnp.int32, (BLK, 2 * BLK), 0).astype(F32).astype(BF)
    one, zero = jnp.ones((), BF), jnp.zeros((), BF)
    nodes = x_ref[...].astype(F32)
    total = delta[pl.ds(start, BLK), :]
    for j in range(27):
        pick = jnp.where(place[j : j + 1, :] == target, one, zero)
        come = nn(pick, window)
        total += come * weight[j : j + 1, :]
        dw[j] += jnp.sum((come * nodes).reshape(BLK // 8, 8, C), axis=0)
    grad_ref[...] = total

    @pl.when(step == steps - 1)
    def _():
        mine = jnp.sum(dw[...], axis=1)
        mine = jnp.concatenate([mine, jnp.zeros((5, C), F32)], axis=0)
        dws = all_sum(mine, me, count, cores, wslots, w_send, w_recv)
        for k in range(3):
            early_s[pl.ds(ROW_CONV + k, 27, stride=3), :] = dws[:27, k * 128 : (k + 1) * 128]
        for o in range(owners):
            @pl.when(me == o)
            def _():
                rows = min(shard, early_s.shape[0] - o * shard)
                total_s[0:rows, :] += early_s[o * shard : o * shard + rows, :]
        grad = total_s[0:shard, :]
        row = lax.broadcasted_iota(jnp.int32, (shard, 128), 0) + me * shard
        rate = jnp.where(row < ROW_CONV, 0.2, 0.03)
        old = master_ref[...]
        new_m = 0.9 * m_ref[...] + 0.1 * grad
        new_v = 0.95 * v_ref[...] + 0.05 * grad * grad
        first_hat = new_m / (1.0 - 0.9**STEP)
        second_hat = new_v / (1.0 - 0.95**STEP)
        new = old - rate * (first_hat / (jnp.sqrt(second_hat) + 1e-08) + 0.01 * old)
        master_out[...] = new
        m_out[...] = new_m
        v_out[...] = new_v
        low_out[...] = new.astype(BF)


def convolve_back(near, delta, conv, nodes, mask3, sums, stats, rows, grads, master, m, v, count, cores):
    n = nodes.shape[0]
    steps = n // BLK
    shard = master.shape[0]
    padded = grads.shape[-2]
    highs = count // 8
    owners = -(-ROW_JOINT // shard)
    turned = lambda i: ((i + 1) % steps, 0)
    anywhere = pl.BlockSpec(memory_space=pl.ANY)
    flat = whole(shard, 128)
    r4_rows = sum((size - 1) * stride for stride, size in stages_of(highs))
    return pl.pallas_call(
        functools.partial(conv_back_kernel, count, cores, owners),
        grid=(steps,),
        in_specs=[
            anywhere,
            anywhere,
            anywhere,
            pl.BlockSpec((BLK, C), turned),
            whole(*mask3.shape),
            whole(*sums.shape),
            whole(*stats.shape),
            whole(*rows.shape),
            anywhere,
            flat,
            flat,
            flat,
        ],
        out_specs=[pl.BlockSpec((BLK, C), turned), flat, flat, flat, flat, whole(1, C)],
        out_shape=[jax.ShapeDtypeStruct((n, C), F32)]
        + [jax.ShapeDtypeStruct((shard, 128), d) for d in (F32, F32, F32, BF)]
        + [jax.ShapeDtypeStruct((1, C), F32)],
        scratch_shapes=[
            pltpu.VMEM((n + 2 * HALO, 27), jnp.int32),
            pltpu.VMEM((n + 2 * HALO, C), BF),
            pltpu.VMEM((n, C), F32),
            pltpu.VMEM((n, C), F32),
            pltpu.VMEM((27, C), F32),
            pltpu.VMEM((27, 8, C), F32),
            pltpu.VMEM((highs, 2, 2, padded, 128), BF),
            pltpu.VMEM((highs, 2, 2, padded, 128), BF),
            pltpu.VMEM((2, highs, 2, padded // 2, 128), BF),
            pltpu.VMEM((2, highs, padded // 2, 128), BF),
            pltpu.VMEM((r4_rows, padded, 128), BF),
            pltpu.SemaphoreType.DMA((4,)),
            pltpu.SemaphoreType.DMA((4,)),
            pltpu.SemaphoreType.DMA((4,)),
            pltpu.SemaphoreType.DMA((3 + len(stages_of(highs)), 8)),
            pltpu.SemaphoreType.DMA((3 + len(stages_of(highs)), 8)),
        ]
        + sum_scratch(count, 8, C)
        + sum_scratch(count, 32, C)
        + [pltpu.VMEM((padded, 128), F32), pltpu.VMEM((round_up(ROW_JOINT, 8), 128), F32)],
        compiler_params=pltpu.CompilerParams(
            vmem_limit_bytes=60 * 1024 * 1024, collective_id=1, has_side_effects=True
        ),
    )(near, delta, conv, nodes, mask3, sums, stats, rows, grads, master, m, v)


def prepare(stats, rows, gathered, shard, flat, norm, spread, mats):
    for i in range(gathered.shape[0] * 8):
        flat[i * shard : (i + 1) * shard, :] = gathered[i // 8, (i // 4) % 2, (i // 2) % 2, i % 2].astype(F32)[:shard]
    for first, out, out_t in mats:
        height, width = out.shape
        per = width // 128
        for k in range(per):
            for r in range(0, height, C):
                piece = flat[pl.ds(first + r * per + k, C, stride=per), :]
                out[r : r + C, k * 128 : (k + 1) * 128] = piece.astype(BF)
                out_t[k * 128 : (k + 1) * 128, r : r + C] = piece.T.astype(BF)
    for i in range(ROW_CONV):
        spread[i * 128 : (i + 1) * 128, :] = jnp.broadcast_to(rows[i : i + 1, :], (128, 128)).T
    gain = jnp.concatenate([rows[i : i + 1, :] for i in range(3)], axis=1)
    shift = jnp.concatenate([rows[3 + i : 4 + i, :] for i in range(3)], axis=1)
    live_total = stats[2:3, :]
    average = stats[0:1, :] / live_total
    variance = stats[1:2, :] / live_total - average * average
    inverse = lax.rsqrt(variance + EPS)
    norm[0:1, :] = inverse * gain
    norm[1:2, :] = shift - average * inverse * gain
    norm[2:3, :] = inverse
    norm[3:4, :] = average * inverse


def mid_kernel(shard,conv_ref,nodes_ref,dy_ref,mask_ref,stats_ref,rows_ref,gathered_ref,
    out_ref,dfirst_ref,grads_ref,bns_ref,
    flat_ref,bn_ref,vb_ref,wj_ref,wjt_ref,wo_ref,wot_ref,wh_ref,wht_ref,wf_ref,wft_ref,
    gj_ref,go_ref,gh_ref,gf_ref,vs_ref,hb_ref,first_s,second_s,qkv_s,kn_s,vn_s,a_s,o_s,ob_s,do_s,dqkv_s,x_s,acc_s,dx_s):
    step=pl.program_id(0)
    rep=T//128
    @pl.when(step==0)
    def _():
        for r in (gj_ref,go_ref,gh_ref,gf_ref,vs_ref,hb_ref,bns_ref): r[...]=jnp.zeros_like(r)
        prepare(stats_ref,rows_ref,gathered_ref,shard,flat_ref,bn_ref,vb_ref,
            ((ROW_JOINT,wj_ref,wjt_ref),(ROW_OUT,wo_ref,wot_ref),(ROW_HIDDEN,wh_ref,wht_ref),(ROW_FINAL,wf_ref,wft_ref)))
    def col(i,n=C):
        v=vb_ref[pl.ds(i*C,n),:]
        return jnp.concatenate([v]*rep,axis=1) if rep>1 else v
    def fold(x):
        r=x[:,:128]
        for k in range(1,rep): r=r+x[:,128*k:128*(k+1)]
        return r
    scale_a=bn_ref[0:1,:]; shift_b=bn_ref[1:2,:]; r_row=bn_ref[2:3,:]; ar_row=bn_ref[3:4,:]
    first=nodes_ref[...].astype(F32)+(conv_ref[...]*scale_a+shift_b)
    firstT=first.T
    first_s[...]=firstT
    dy=dy_ref[...]
    dyT32=dy.astype(F32).T
    do_s[...]=dyT32
    def ln(x):
        m=jnp.mean(x,axis=0,keepdims=True); c=x-m
        rs=lax.rsqrt(jnp.mean(c*c,axis=0,keepdims=True)+EPS)
        return c*rs, rs
    xh1,rs1=ln(firstT)
    x1=(xh1*col(2)+col(3)).astype(BF)
    x_s[0]=x1
    q=nn(wjt_ref[0:C,:],x1)+col(4)
    qkv_s[0:C,:]=q.astype(BF)
    k=nn(wjt_ref[C:2*C,:],x1)
    qkv_s[C:2*C,:]=k.astype(BF)
    kn_s[...]=k.T.astype(BF)
    v=nn(wjt_ref[2*C:,:],x1)+col(5)
    qkv_s[2*C:,:]=v.astype(BF)
    vn_s[...]=v.T.astype(BF)
    scale=HD**-0.5
    c2=scale*1.4426950408889634
    pi=lax.broadcasted_iota(jnp.int32,(BLK,BLK),0); qi=lax.broadcasted_iota(jnp.int32,(BLK,BLK),1)
    same=(pi&3)==(qi&3)
    for b in range(rep):
        lv=jnp.broadcast_to(mask_ref[b].astype(F32),(BLK,BLK)).T
        live=(lv>0.5)&same
        bias=jnp.where(same,-1e9/scale,-1e30)
        live2=jnp.concatenate([live,live],axis=1); bias2=jnp.concatenate([bias,bias],axis=1)
        cs=slice(b*BLK,(b+1)*BLK)
        z=jnp.zeros((HD,BLK),BF)
        for g in range(3):
            kg=kn_s[cs,g*128:(g+1)*128]
            for hp in range(2):
                h0=hp*2
                def ex(i):
                    qh=qkv_s[g*128+i*32:g*128+(i+1)*32,cs]
                    return jnp.concatenate([qh if t==i else z for t in range(4)],axis=0)
                s=nn(kg,jnp.concatenate([ex(h0),ex(h0+1)],axis=1))
                s=jnp.where(live2,s,bias2)
                m=jnp.max(s,axis=0,keepdims=True)
                e=jnp.exp2((s-m)*c2)
                l=jnp.sum(e,axis=0,keepdims=True)
                a=(e*(1.0/l)).astype(BF)
                for i in range(2):
                    h=g*4+h0+i
                    ah=a[:,i*128:(i+1)*128]
                    a_s[h,:,cs]=ah
                    o_s[h*32:(h+1)*32,cs]=nn(qkv_s[2*C+h*32:2*C+(h+1)*32,cs],ah)
    ob=o_s[...].astype(BF)
    ob_s[...]=ob
    secondT=first_s[...]+(nn(wot_ref[...],ob)+col(6))
    second_s[...]=secondT
    xh2,rs2=ln(secondT)
    x2=(xh2*col(7)+col(8)).astype(BF)
    x_s[1]=x2
    dyTb=do_s[...].astype(BF)
    FC=384
    c0=0.7978845608028654; c1=0.044715
    for f in range(F//FC):
        fs=slice(f*FC,(f+1)*FC)
        hb=vb_ref[9*C+f*FC:9*C+(f+1)*FC,:]
        hb=jnp.concatenate([hb]*rep,axis=1)
        h=nn(wht_ref[fs,:],x2)+hb
        h2=h*h
        t=jnp.tanh(h*(c0+(c0*c1)*h2))
        p=0.5+0.5*t
        act=(h*p).astype(BF)
        dg=p*(1.0+h*(1.0-p)*(2*c0+(6*c0*c1)*h2))
        da=nn(wf_ref[fs,:],dyTb)
        dp32=da*dg
        dpb=dp32.astype(BF)
        hb_ref[fs,:]+=fold(dpb.astype(F32))
        o=nn(wft_ref[:,fs],act)
        d=nn(wh_ref[:,fs],dpb)
        if f==0:
            acc_s[...]=o; dx_s[...]=d
        else:
            acc_s[...]+=o; dx_s[...]+=d
        gf_ref[fs,:]+=nn(act,dy)
        gh_ref[:,fs]+=nt(x2,dpb)
    outT=second_s[...]+(acc_s[...]+col(15-2))
    out_ref[...]=outT.T.astype(BF)
    def ln_back(x,dx,gain,vi):
        xh,rs=ln(x)
        vs_ref[vi]+=fold(dx*xh)
        vs_ref[vi+1]+=fold(dx)
        dh=dx*gain
        m1=jnp.mean(dh,axis=0,keepdims=True)
        m2=jnp.mean(dh*xh,axis=0,keepdims=True)
        return rs*(dh-m1-xh*m2)
    dsec=do_s[...]+ln_back(second_s[...],dx_s[...],col(7),0)
    second_s[...]=dsec
    dbr=dsec.astype(BF)
    vs_ref[2]+=fold(dbr.astype(F32))
    go_ref[...]+=nt(ob_s[...],dbr)
    dat=nn(wo_ref[...],dbr)
    do_s[...]=dat
    dob=dat.astype(BF)
    for b in range(rep):
        cs=slice(b*BLK,(b+1)*BLK)
        z=jnp.zeros((HD,BLK),BF)
        lrow=mask_ref[b].astype(F32)
        for g in range(3):
            vg=vn_s[cs,g*128:(g+1)*128]
            for hp in range(2):
                h0=hp*2
                def ex(i):
                    qh=dob[g*128+i*32:g*128+(i+1)*32,cs]
                    return jnp.concatenate([qh if t==i else z for t in range(4)],axis=0)
                dA=nn(vg,jnp.concatenate([ex(h0),ex(h0+1)],axis=1))
                for i in range(2):
                    h=g*4+h0+i
                    hs=slice(h*32,(h+1)*32)
                    doh=dob[hs,cs]
                    delta=jnp.sum(doh.astype(F32)*o_s[hs,cs],axis=0,keepdims=True)
                    ah=a_s[h,:,cs]
                    ds=(ah.astype(F32)*(dA[:,i*128:(i+1)*128]-delta)).astype(BF)
                    kh=(qkv_s[C+h*32:C+(h+1)*32,cs].astype(F32)*lrow).astype(BF)
                    dqkv_s[h*32:(h+1)*32,cs]=(nn(kh,ds)*scale).astype(BF)
                    dqkv_s[C+h*32:C+(h+1)*32,cs]=(nt(qkv_s[hs,cs],ds)*(lrow*scale)).astype(BF)
                    dqkv_s[2*C+h*32:2*C+(h+1)*32,cs]=nt(doh,ah).astype(BF)
    vs_ref[3]+=fold(dqkv_s[0:C,:].astype(F32))
    vs_ref[4]+=fold(dqkv_s[2*C:,:].astype(F32))
    gj_ref[...]+=nt(x_s[0],dqkv_s[...])
    dx1=nn(wj_ref[...],dqkv_s[...])
    dfT=second_s[...]+ln_back(first_s[...],dx1,col(2),5)
    df=dfT.T
    dfirst_ref[...]=df
    cen=conv_ref[...]*r_row-ar_row
    bns_ref[0]+=jnp.sum((df*cen).reshape(T//8,8,C),axis=0)
    bns_ref[1]+=jnp.sum(df.reshape(T//8,8,C),axis=0)
    bns_ref[2]+=jnp.sum(dy.astype(F32).reshape(T//8,8,C),axis=0)
    @pl.when(step==pl.num_programs(0)-1)
    def _():
        flat_ref[...]=jnp.zeros_like(flat_ref)
        for vi,row in ((0,21),(1,24),(2,18),(3,12),(4,15),(5,6),(6,9)):
            for i in range(3):
                flat_ref[pl.ds(row+i,1),:]=jnp.sum(vs_ref[vi,i*128:(i+1)*128,:].T,axis=0,keepdims=True)
        for i in range(12):
            flat_ref[pl.ds(27+i,1),:]=jnp.sum(hb_ref[i*128:(i+1)*128,:].T,axis=0,keepdims=True)
        for first,mat in ((ROW_JOINT,gj_ref),(ROW_OUT,go_ref),(ROW_HIDDEN,gh_ref),(ROW_FINAL,gf_ref)):
            rows,cols=mat.shape
            per=cols//128
            for k in range(per):
                for r in range(0,rows,C):
                    flat_ref[pl.ds(first+r*per+k,C,stride=per),:]=mat[r:r+C,k*128:(k+1)*128]
        for i in range(grads_ref.shape[0]*8):
            part=flat_ref[i*shard:(i+1)*shard,:]
            pad=grads_ref.shape[-2]-shard
            grads_ref[i//8,(i//4)%2,(i//2)%2,i%2]=jnp.concatenate([part,jnp.zeros((pad,128),F32)],axis=0).astype(BF)


def middle(conv,nodes,dy,mask3,stats,rows,gathered,shard):
    n=conv.shape[0]
    row=rows_of(C,T)
    flat_rows=gathered.shape[0]*8*shard
    in_specs=[row,row,row,pl.BlockSpec((T//128,1,128),lambda i:(i,0,0)),whole(*stats.shape),whole(*rows.shape),whole(*gathered.shape)]
    outs=[((n,C),BF,row),((n,C),F32,row),(gathered.shape,BF,whole(*gathered.shape)),((3,8,C),F32,whole(3,8,C))]
    mats=[]
    for shape in ((C,3*C),(C,C),(C,F),(F,C)): mats+=[(shape,BF),(shape[::-1],BF)]
    scr=[pltpu.VMEM(s,d) for s,d in [((flat_rows,128),F32),((8,C),F32),((ROW_CONV*128,128),F32)]+mats+[((C,3*C),F32),((C,C),F32),((C,F),F32),((F,C),F32),((7,C,128),F32),((F,128),F32),((C,T),F32),((C,T),F32),((3*C,T),BF),((T,C),BF),((T,C),BF),((HEADS,BLK,T),BF),((C,T),F32),((C,T),BF),((C,T),F32),((3*C,T),BF),((2,C,T),BF),((C,T),F32),((C,T),F32)]]
    return pl.pallas_call(functools.partial(mid_kernel,shard),grid=(n//T,),in_specs=in_specs,out_specs=[o[2] for o in outs],
      out_shape=[jax.ShapeDtypeStruct(o[0],o[1]) for o in outs],scratch_shapes=scr,
      compiler_params=VMEM)(conv,nodes,dy,mask3,stats,rows,gathered)


def shards(nodes_in, out_grad, neighbours, node_mask, master, first_moment, second_moment):
    n = nodes_in.shape[0]
    count, cores = lax.axis_size(AXES), lax.axis_size("grp")
    shard = master.shape[0] // 128
    flat = [a.reshape(shard, 128) for a in (master, first_moment, second_moment)]
    mask3 = node_mask.reshape(n // 128, 1, 128)
    convolved, gathered, first_rows, stats = convolve(neighbours, nodes_in, mask3, flat[0], count, cores)
    output, delta_first, grads, norm_sums = middle(
        convolved, nodes_in, out_grad, mask3, stats, first_rows, gathered, shard
    )
    node_grad, new_master, new_first, new_second, new_low, bias_total = convolve_back(
        neighbours, delta_first, convolved, nodes_in, mask3, norm_sums, stats, first_rows, grads, *flat, count, cores
    )
    return (
        output,
        node_grad,
        new_master.reshape(-1),
        new_first.reshape(-1),
        new_second.reshape(-1),
        new_low.reshape(-1),
        bias_total.reshape(-1),
    )


def solution(mesh):
    rows, flat = P(AXES, None), P(AXES)
    return jax.shard_map(
        shards,
        mesh=mesh,
        in_specs=(rows, rows, rows, flat, flat, flat, flat),
        out_specs=(rows, rows, flat, flat, flat, flat, P()),
        check_vma=False,
    )
```

```python
import functools

import jax
import jax.numpy as jnp
from jax import lax
from jax.experimental import pallas as pl
from jax.experimental.pallas import tpu as pltpu
from jax.sharding import PartitionSpec as P

C = 384
HEADS = 12
HD = 32
F = 1536
HALO = 64
STEP = 5
EPS = 1e-5
AXES = ("rows", "grp")
F32 = jnp.float32
BF = jnp.bfloat16

BLK = 128
T = 512
ROW_CONV = (10 * C + F) // 128
ROW_JOINT = ROW_CONV + 27 * C // 128
ROW_OUT = ROW_JOINT + C * 3 * C // 128
ROW_HIDDEN = ROW_OUT + C * C // 128
ROW_FINAL = ROW_HIDDEN + C * F // 128
ROW_END = ROW_FINAL + C * F // 128
VMEM = pltpu.CompilerParams(vmem_limit_bytes=60 * 1024 * 1024)


def nn(a, b):
    return jnp.dot(a, b, preferred_element_type=F32)


def nt(a, b):
    return lax.dot_general(a, b, (((1,), (1,)), ((), ())), preferred_element_type=F32)


def whole(*shape):
    return pl.BlockSpec(shape, lambda i: (0,) * len(shape), pipeline_mode=pl.Buffered(1))


def rows_of(width, size):
    return pl.BlockSpec((size, width), lambda i: (i, 0))


MESH = pl.DeviceIdType.MESH


def round_up(value, step):
    return -(-value // step) * step


def my_place():
    return lax.axis_index("rows") * lax.axis_size("grp") + lax.axis_index("grp")


def device(place, cores):
    return (place // cores, place % cores)


def stages_of(count):
    out, stride = [], 1
    while stride < count:
        size = min(8, count // stride)
        out.append((stride, size))
        stride *= size
    return out


def others(me, stride, size):
    mine = (me // stride) % size
    return mine, [(k, me + ((mine + k) % size - mine) * stride) for k in range(1, size)]


def greet(partners, cores):
    barrier = pltpu.get_barrier_semaphore()
    for place in partners:
        pl.semaphore_signal(barrier, inc=1, device_id=device(place, cores), device_id_type=MESH)
    pl.semaphore_wait(barrier, len(partners))


def send(source, target, send_sem, recv_sem, place, cores):
    return pltpu.make_async_remote_copy(
        src_ref=source,
        dst_ref=target,
        send_sem=send_sem,
        recv_sem=recv_sem,
        device_id=device(place, cores),
        device_id_type=MESH,
    )


def all_sum(value, me, count, cores, slots, send_sems, recv_sems):
    for s, (stride, size) in enumerate(stages_of(count)):
        mine, partners = others(me, stride, size)
        slots[s, mine] = value
        copies = [
            send(slots.at[s, mine], slots.at[s, mine], send_sems.at[s, k], recv_sems.at[s, k], place, cores)
            for k, place in partners
        ]
        for copy in copies:
            copy.start()
        for copy in copies:
            copy.wait()
        value = slots[s, 0]
        for i in range(1, size):
            value = value + slots[s, i]
    return value


def sum_scratch(count, rows, width):
    n = len(stages_of(count))
    return [
        pltpu.VMEM((n, 8, rows, width), F32),
        pltpu.SemaphoreType.DMA((n, 8)),
        pltpu.SemaphoreType.DMA((n, 8)),
    ]


def conv_kernel(count, cores, owners, near_ref, nodes_ref, mask_ref, master_ref,
                conv_ref, gathered_ref, first_ref, stats_ref,
                ext, early, weight, sums, own_s, local_sem, halo_send, halo_recv, e_send, e_recv, g_send, g_recv,
                slots, s_send, s_recv):
    step = pl.program_id(0)
    steps = pl.num_programs(0)
    block = (step + 1) % steps
    n = nodes_ref.shape[0]
    shard = master_ref.shape[0]
    padded = gathered_ref.shape[-2]
    half = padded // 2
    e_rows = early.shape[1]
    me = my_place()
    low, high = me % 8, me // 8
    y, x, g = low // 4, (low // 2) % 2, low % 2
    highs = stages_of(count // 8)
    left, right = (me + count - 1) % count, (me + 1) % count

    local = pltpu.make_async_copy(nodes_ref, ext.at[pl.ds(HALO, n)], local_sem.at[0])
    keep = pltpu.make_async_copy(own_s, gathered_ref.at[high, y, x, g], local_sem.at[1])
    to_left = send(nodes_ref.at[pl.ds(0, HALO)], ext.at[pl.ds(HALO + n, HALO)], halo_send.at[0], halo_recv.at[0], left, cores)
    to_right = send(nodes_ref.at[pl.ds(n - HALO, HALO)], ext.at[pl.ds(0, HALO)], halo_send.at[1], halo_recv.at[1], right, cores)

    def high_copies(s):
        stride, size = highs[s]
        mine, partners = others(high, stride, size)
        own = gathered_ref.at[pl.ds(high // stride * stride, stride), y, x, g]
        return [
            send(own, own, g_send.at[s, k], g_recv.at[s, k], place * 8 + low, cores)
            for k, place in partners
        ]

    nh = len(highs)
    y_place, x_place, g_place = me + 4 - 8 * y, me + 2 - 4 * x, me + 1 - 2 * g

    def quad_copies(t):
        top, bottom = pl.ds(0, half), pl.ds(half, half)
        if t == 0:
            a = gathered_ref.at[:, y, x, g, top]
            b = gathered_ref.at[:, y, x, g, bottom]
            to_a, to_b = y_place, x_place
        else:
            a = gathered_ref.at[:, :, x, g, top]
            b = gathered_ref.at[:, y, :, g, bottom]
            to_a, to_b = x_place, y_place
        s = nh + t
        return [send(a, a, g_send.at[s, 0], g_recv.at[s, 0], to_a, cores), send(b, b, g_send.at[s, 1], g_recv.at[s, 1], to_b, cores)]

    def core_copies():
        own = gathered_ref.at[:, :, :, g]
        return [send(own, own, g_send.at[nh + 2, 0], g_recv.at[nh + 2, 0], g_place, cores)]

    plan = [functools.partial(high_copies, s) for s in range(nh)]
    plan += [functools.partial(quad_copies, 0), functools.partial(quad_copies, 1), core_copies]
    cuts = [6] * nh + [11, 19, 27]
    for s in range(nh):
        cuts[s] = 3 + 5 * (s + 1) // nh

    @pl.when(step == 0)
    def _():
        local.start()
        sums[...] = jnp.zeros_like(sums)
        own = jnp.concatenate([master_ref[...], jnp.zeros((padded - shard, 128), F32)], axis=0).astype(BF)
        own_s[...] = own
        keep.start()
        wide = [h for h in range(1, count // 8)]
        partners = [left, right]
        partners += [(high + h) % (count // 8) * 8 + low for h in wide]
        partners += [place for _, place in others(me, 1, 8)[1]]
        greet(partners, cores)
        for o in range(owners):
            @pl.when(low == o)
            def _():
                @pl.when(high == 0)
                def _():
                    early[o] = own[:e_rows]
                    out = [
                        send(early.at[o], early.at[o], e_send.at[o, 8 + h], e_recv.at[o, 0], h * 8 + o, cores)
                        for h in wide
                    ]
                    for copy in out:
                        copy.start()
                    for copy in out:
                        copy.wait_send()
                @pl.when(high > 0)
                def _():
                    send(early.at[o], early.at[o], e_send.at[o, 8], e_recv.at[o, 0], left, cores).wait_recv()
                out = [
                    send(early.at[o], early.at[o], e_send.at[o, k], e_recv.at[o, 1], me + k - o, cores)
                    for k in range(8) if k != o
                ]
                for copy in out:
                    copy.start()
                for copy in out:
                    copy.wait_send()
        to_left.start()
        to_right.start()
        keep.wait()
        for copy in plan[0]():
            copy.start()
        for o in range(owners):
            @pl.when(low != o)
            def _():
                send(early.at[o], early.at[o], e_send.at[o, 8], e_recv.at[o, 1], left, cores).wait_recv()
        for o in range(owners):
            rows = min(shard, e_rows)
            first_ref[pl.ds(o * shard, rows), :] = early[o].astype(F32)[:rows]
        for k in range(3):
            weight[:, k * 128 : (k + 1) * 128] = first_ref[pl.ds(ROW_CONV + k, 27, stride=3), :]
        local.wait()

    for s in range(len(plan)):
        @pl.when(step == cuts[s])
        def _(s=s):
            for copy in plan[s]():
                copy.wait()
            if s + 1 < len(plan):
                for copy in plan[s + 1]():
                    copy.start()

    @pl.when(step == steps - 2)
    def _():
        to_left.wait()
        to_right.wait()

    window = ext[pl.ds(pl.multiple_of(block * BLK, BLK), 2 * BLK), :]
    near = near_ref[...]
    place = near + lax.broadcasted_iota(jnp.int32, near.shape, 0)
    place = jnp.where(near < 0, -1, place).astype(F32).astype(BF)
    lane = lax.broadcasted_iota(jnp.int32, (BLK, 2 * BLK), 1).astype(F32).astype(BF)
    one, zero = jnp.ones((), BF), jnp.zeros((), BF)
    total = jnp.zeros((BLK, C), F32)
    for j in range(27):
        pick = jnp.where(place[:, j : j + 1] == lane, one, zero)
        total += nn(pick, window) * weight[j : j + 1, :]
    conv_ref[...] = total
    live = jnp.broadcast_to(mask_ref[0].astype(F32), (BLK, BLK)).T
    live = jnp.concatenate([live] * 3, axis=1)
    kept = total * live
    sums[0] += jnp.sum(kept.reshape(BLK // 8, 8, C), axis=0)
    sums[1] += jnp.sum((kept * total).reshape(BLK // 8, 8, C), axis=0)
    sums[2] += jnp.sum(live.reshape(BLK // 8, 8, C), axis=0)

    @pl.when(step == steps - 1)
    def _():
        rows = [jnp.sum(sums[i], axis=0, keepdims=True) for i in range(3)]
        rows = jnp.concatenate(rows + [jnp.zeros((5, C), F32)], axis=0)
        stats_ref[...] = all_sum(rows, me, count, cores, slots, s_send, s_recv)


def convolve(near, nodes, mask3, master, count, cores):
    n = nodes.shape[0]
    steps = n // BLK
    shard = master.shape[0]
    padded = round_up(shard, 32)
    owners = -(-ROW_JOINT // shard)
    e_rows = min(padded, round_up(ROW_JOINT, 16))
    turned = lambda i: ((i + 1) % steps, 0)
    stages = len(stages_of(count // 8)) + 3
    first_rows = round_up((owners - 1) * shard + e_rows, 8)
    return pl.pallas_call(
        functools.partial(conv_kernel, count, cores, owners),
        grid=(steps,),
        in_specs=[
            pl.BlockSpec((BLK, 27), turned),
            pl.BlockSpec(memory_space=pl.ANY),
            pl.BlockSpec((1, 1, 128), lambda i: ((i + 1) % steps, 0, 0)),
            whole(shard, 128),
        ],
        out_specs=[
            pl.BlockSpec((BLK, C), turned),
            pl.BlockSpec(memory_space=pl.ANY),
            whole(first_rows, 128),
            whole(8, C),
        ],
        out_shape=[
            jax.ShapeDtypeStruct((n, C), F32),
            jax.ShapeDtypeStruct((count // 8, 2, 2, 2, padded, 128), BF),
            jax.ShapeDtypeStruct((first_rows, 128), F32),
            jax.ShapeDtypeStruct((8, C), F32),
        ],
        scratch_shapes=[
            pltpu.VMEM((n + 2 * HALO, C), BF),
            pltpu.VMEM((owners, e_rows, 128), BF),
            pltpu.VMEM((27, C), F32),
            pltpu.VMEM((3, 8, C), F32),
            pltpu.VMEM((padded, 128), BF),
            pltpu.SemaphoreType.DMA((2,)),
            pltpu.SemaphoreType.DMA((2,)),
            pltpu.SemaphoreType.DMA((2,)),
            pltpu.SemaphoreType.DMA((owners, 8 + count // 8)),
            pltpu.SemaphoreType.DMA((owners, 2)),
            pltpu.SemaphoreType.DMA((stages, 8)),
            pltpu.SemaphoreType.DMA((stages, 8)),
        ]
        + sum_scratch(count, 8, C),
        compiler_params=pltpu.CompilerParams(
            vmem_limit_bytes=60 * 1024 * 1024, collective_id=0, has_side_effects=True
        ),
    )(near, nodes, mask3, master)


def conv_back_kernel(count, cores, owners, near_hbm, first_hbm, conv_hbm, x_ref, mask_ref, sums_ref, stats_ref, rows_ref,
                     grads_ref, master_ref, m_ref, v_ref,
                     grad_ref, master_out, m_out, v_out, low_out, bias_out,
                     near, ext, delta, conv, weight, dw, kept, r1, r2, r3, r4, local_sem, halo_send, halo_recv, g_send, g_recv,
                     slots, s_send, s_recv, wslots, w_send, w_recv, total_s, early_s):
    step = pl.program_id(0)
    steps = pl.num_programs(0)
    block = (step + 1) % steps
    n = first_hbm.shape[0]
    shard = master_ref.shape[0]
    padded = grads_ref.shape[-2]
    half = padded // 2
    me = my_place()
    low, high = me % 8, me // 8
    y, x, g = low // 4, (low // 2) % 2, low % 2
    highs = stages_of(count // 8)[::-1]
    nh = len(highs)
    left, right = (me + count - 1) % count, (me + 1) % count
    y_place, x_place, g_place = me + 4 - 8 * y, me + 2 - 4 * x, me + 1 - 2 * g
    top, bottom = pl.ds(0, half), pl.ds(half, half)

    locals_ = [
        pltpu.make_async_copy(first_hbm, delta, local_sem.at[0]),
        pltpu.make_async_copy(conv_hbm, conv, local_sem.at[1]),
        pltpu.make_async_copy(near_hbm, near.at[pl.ds(HALO, n)], local_sem.at[2]),
        pltpu.make_async_copy(grads_ref.at[:, :, :, g], kept, local_sem.at[3]),
    ]
    near_halo = [
        send(near_hbm.at[pl.ds(0, HALO)], near.at[pl.ds(HALO + n, HALO)], halo_send.at[0], halo_recv.at[0], left, cores),
        send(near_hbm.at[pl.ds(n - HALO, HALO)], near.at[pl.ds(0, HALO)], halo_send.at[1], halo_recv.at[1], right, cores),
    ]
    delta_halo = [
        send(ext.at[pl.ds(HALO, HALO)], ext.at[pl.ds(HALO + n, HALO)], halo_send.at[2], halo_recv.at[2], left, cores),
        send(ext.at[pl.ds(n, HALO)], ext.at[pl.ds(0, HALO)], halo_send.at[3], halo_recv.at[3], right, cores),
    ]

    def core_copies():
        return [send(grads_ref.at[:, :, :, 1 - g], r1, g_send.at[0, 0], g_recv.at[0, 0], g_place, cores)]

    def core_add():
        def body(i, _):
            kept[i // 4, (i // 2) % 2, i % 2] = (
                kept[i // 4, (i // 2) % 2, i % 2].astype(F32) + r1[i // 4, (i // 2) % 2, i % 2].astype(F32)
            ).astype(BF)
            return 0
        lax.fori_loop(0, count // 2, body, 0)

    def quad_copies_0():
        return [
            send(kept.at[:, :, 1 - x, top], r2.at[0], g_send.at[1, 0], g_recv.at[1, 0], x_place, cores),
            send(kept.at[:, 1 - y, :, bottom], r2.at[1], g_send.at[1, 1], g_recv.at[1, 1], y_place, cores),
        ]

    def quad_add_0():
        def body(i, _):
            h, w = i // 2, i % 2
            kept[h, w, x, top] = (
                kept[h, w, x, top].astype(F32) + r2[0, h, w].astype(F32)
            ).astype(BF)
            kept[h, y, w, bottom] = (
                kept[h, y, w, bottom].astype(F32) + r2[1, h, w].astype(F32)
            ).astype(BF)
            return 0
        lax.fori_loop(0, count // 4, body, 0)

    def quad_copies_1():
        return [
            send(kept.at[:, 1 - y, x, top], r3.at[0], g_send.at[2, 0], g_recv.at[2, 0], y_place, cores),
            send(kept.at[:, y, 1 - x, bottom], r3.at[1], g_send.at[2, 1], g_recv.at[2, 1], x_place, cores),
        ]

    def quad_add_1():
        def body(h, _):
            kept[h, y, x, top] = (
                kept[h, y, x, top].astype(F32) + r3[0, h].astype(F32)
            ).astype(BF)
            kept[h, y, x, bottom] = (
                kept[h, y, x, bottom].astype(F32) + r3[1, h].astype(F32)
            ).astype(BF)
            return 0
        lax.fori_loop(0, count // 8, body, 0)

    bases = []
    base = 0
    for stride, size in highs:
        bases.append(base)
        base += (size - 1) * stride

    def high_copies(s):
        stride, size = highs[s]
        mine, partners = others(high, stride, size)
        out = []
        for k, place in partners:
            source = kept.at[pl.ds(place // stride * stride, stride), y, x]
            target = r4.at[pl.ds(bases[s] + (k - 1) * stride, stride)]
            out.append(send(source, target, g_send.at[3 + s, k], g_recv.at[3 + s, k], place * 8 + low, cores))
        return out

    def high_add(s):
        stride, size = highs[s]
        start = high // stride * stride
        def body(i, _):
            value = kept[start + i, y, x].astype(F32)
            for k in range(size - 1):
                value = value + r4[bases[s] + k * stride + i].astype(F32)
            if s == nh - 1:
                total_s[...] = value
            else:
                kept[start + i, y, x] = value.astype(BF)
            return 0
        lax.fori_loop(0, stride, body, 0)

    plan = [(core_copies, core_add), (quad_copies_0, quad_add_0), (quad_copies_1, quad_add_1)]
    plan += [(functools.partial(high_copies, s), functools.partial(high_add, s)) for s in range(nh)]
    cuts = [4, 13, 18] + [18 + 10 * (s + 1) // nh for s in range(nh)]

    @pl.when(step == 0)
    def _():
        for copy in locals_:
            copy.start()
        dw[...] = jnp.zeros_like(dw)
        partners = [left, right]
        partners += [(high + h) % (count // 8) * 8 + low for h in range(1, count // 8)]
        partners += [place for _, place in others(me, 1, 8)[1]]
        greet(partners, cores)
        mine = jnp.concatenate([jnp.sum(sums_ref[i], axis=0, keepdims=True) for i in range(3)] + [jnp.zeros((5, C), F32)], axis=0)
        total = all_sum(mine, me, count, cores, slots, s_send, s_recv)
        for copy in plan[0][0]():
            copy.start()
        for copy in near_halo:
            copy.start()
        gain_total, shift_total = total[0:1], total[1:2]
        bias_out[...] = total[2:3]
        early_s[...] = jnp.zeros_like(early_s)
        for i in range(3):
            early_s[i : i + 1, :] = gain_total[:, i * 128 : (i + 1) * 128]
            early_s[3 + i : 4 + i, :] = shift_total[:, i * 128 : (i + 1) * 128]
            early_s[ROW_CONV - 3 + i : ROW_CONV - 2 + i, :] = total[2:3, i * 128 : (i + 1) * 128]
        for k in range(3):
            weight[:, k * 128 : (k + 1) * 128] = rows_ref[pl.ds(ROW_CONV + k, 27, stride=3), :]
        gain = jnp.concatenate([rows_ref[i : i + 1, :] for i in range(3)], axis=1)
        live_total = stats_ref[2:3]
        average = stats_ref[0:1] / live_total
        variance = stats_ref[1:2] / live_total - average * average
        inverse = lax.rsqrt(variance + EPS)
        delta_variance = -0.5 * inverse * inverse * inverse * (gain * gain_total / inverse)
        delta_average = -gain * shift_total * inverse - 2.0 * average * delta_variance
        a = gain * inverse
        b = delta_average / live_total
        c = 2.0 * delta_variance / live_total
        for copy in locals_:
            copy.wait()

        def body(i, _):
            at = pl.ds(pl.multiple_of(i * BLK, BLK), BLK)
            live = jnp.broadcast_to(mask_ref[i].astype(F32), (BLK, BLK)).T
            live = jnp.concatenate([live] * 3, axis=1)
            value = delta[at, :] * a + live * (b + c * conv[at, :])
            ext[pl.ds(pl.multiple_of(i * BLK + HALO, HALO), BLK), :] = value.astype(BF)
            return 0

        lax.fori_loop(0, steps, body, 0)
        for copy in delta_halo:
            copy.start()

    for s in range(len(plan)):
        @pl.when(step == cuts[s])
        def _(s=s):
            for copy in plan[s][0]():
                copy.wait()
            plan[s][1]()
            if s + 1 < len(plan):
                for copy in plan[s + 1][0]():
                    copy.start()

    @pl.when(step == steps - 2)
    def _():
        for copy in near_halo + delta_halo:
            copy.wait()

    start = pl.multiple_of(block * BLK, BLK)
    window = ext[pl.ds(start, 2 * BLK), :]
    near_w = near[pl.ds(start, 2 * BLK), :]
    place = near_w + lax.broadcasted_iota(jnp.int32, near_w.shape, 0) - BLK
    place = jnp.where(near_w < 0, -1, place).astype(F32)
    place = jnp.concatenate([place, jnp.zeros((2 * BLK, 128 - 27), F32)], axis=1).T.astype(BF)
    target = lax.broadcasted_iota(jnp.int32, (BLK, 2 * BLK), 0).astype(F32).astype(BF)
    one, zero = jnp.ones((), BF), jnp.zeros((), BF)
    nodes = x_ref[...].astype(F32)
    total = delta[pl.ds(start, BLK), :]
    for j in range(27):
        pick = jnp.where(place[j : j + 1, :] == target, one, zero)
        come = nn(pick, window)
        total += come * weight[j : j + 1, :]
        dw[j] += jnp.sum((come * nodes).reshape(BLK // 8, 8, C), axis=0)
    grad_ref[...] = total

    @pl.when(step == steps - 1)
    def _():
        mine = jnp.sum(dw[...], axis=1)
        mine = jnp.concatenate([mine, jnp.zeros((5, C), F32)], axis=0)
        dws = all_sum(mine, me, count, cores, wslots, w_send, w_recv)
        for k in range(3):
            early_s[pl.ds(ROW_CONV + k, 27, stride=3), :] = dws[:27, k * 128 : (k + 1) * 128]
        for o in range(owners):
            @pl.when(me == o)
            def _():
                rows = min(shard, early_s.shape[0] - o * shard)
                total_s[0:rows, :] += early_s[o * shard : o * shard + rows, :]
        grad = total_s[0:shard, :]
        row = lax.broadcasted_iota(jnp.int32, (shard, 128), 0) + me * shard
        rate = jnp.where(row < ROW_CONV, 0.2, 0.03)
        old = master_ref[...]
        new_m = 0.9 * m_ref[...] + 0.1 * grad
        new_v = 0.95 * v_ref[...] + 0.05 * grad * grad
        first_hat = new_m / (1.0 - 0.9**STEP)
        second_hat = new_v / (1.0 - 0.95**STEP)
        new = old - rate * (first_hat / (jnp.sqrt(second_hat) + 1e-08) + 0.01 * old)
        master_out[...] = new
        m_out[...] = new_m
        v_out[...] = new_v
        low_out[...] = new.astype(BF)


def convolve_back(near, delta, conv, nodes, mask3, sums, stats, rows, grads, master, m, v, count, cores):
    n = nodes.shape[0]
    steps = n // BLK
    shard = master.shape[0]
    padded = grads.shape[-2]
    highs = count // 8
    owners = -(-ROW_JOINT // shard)
    turned = lambda i: ((i + 1) % steps, 0)
    anywhere = pl.BlockSpec(memory_space=pl.ANY)
    flat = whole(shard, 128)
    r4_rows = sum((size - 1) * stride for stride, size in stages_of(highs))
    return pl.pallas_call(
        functools.partial(conv_back_kernel, count, cores, owners),
        grid=(steps,),
        in_specs=[
            anywhere,
            anywhere,
            anywhere,
            pl.BlockSpec((BLK, C), turned),
            whole(*mask3.shape),
            whole(*sums.shape),
            whole(*stats.shape),
            whole(*rows.shape),
            anywhere,
            flat,
            flat,
            flat,
        ],
        out_specs=[pl.BlockSpec((BLK, C), turned), flat, flat, flat, flat, whole(1, C)],
        out_shape=[jax.ShapeDtypeStruct((n, C), F32)]
        + [jax.ShapeDtypeStruct((shard, 128), d) for d in (F32, F32, F32, BF)]
        + [jax.ShapeDtypeStruct((1, C), F32)],
        scratch_shapes=[
            pltpu.VMEM((n + 2 * HALO, 27), jnp.int32),
            pltpu.VMEM((n + 2 * HALO, C), BF),
            pltpu.VMEM((n, C), F32),
            pltpu.VMEM((n, C), F32),
            pltpu.VMEM((27, C), F32),
            pltpu.VMEM((27, 8, C), F32),
            pltpu.VMEM((highs, 2, 2, padded, 128), BF),
            pltpu.VMEM((highs, 2, 2, padded, 128), BF),
            pltpu.VMEM((2, highs, 2, padded // 2, 128), BF),
            pltpu.VMEM((2, highs, padded // 2, 128), BF),
            pltpu.VMEM((r4_rows, padded, 128), BF),
            pltpu.SemaphoreType.DMA((4,)),
            pltpu.SemaphoreType.DMA((4,)),
            pltpu.SemaphoreType.DMA((4,)),
            pltpu.SemaphoreType.DMA((3 + len(stages_of(highs)), 8)),
            pltpu.SemaphoreType.DMA((3 + len(stages_of(highs)), 8)),
        ]
        + sum_scratch(count, 8, C)
        + sum_scratch(count, 32, C)
        + [pltpu.VMEM((padded, 128), F32), pltpu.VMEM((round_up(ROW_JOINT, 8), 128), F32)],
        compiler_params=pltpu.CompilerParams(
            vmem_limit_bytes=60 * 1024 * 1024, collective_id=1, has_side_effects=True
        ),
    )(near, delta, conv, nodes, mask3, sums, stats, rows, grads, master, m, v)


def prepare(stats, rows, gathered, shard, flat, norm, spread, mats):
    for i in range(gathered.shape[0] * 8):
        flat[i * shard : (i + 1) * shard, :] = gathered[i // 8, (i // 4) % 2, (i // 2) % 2, i % 2].astype(F32)[:shard]
    for first, out, out_t in mats:
        height, width = out.shape
        per = width // 128
        for k in range(per):
            for r in range(0, height, C):
                piece = flat[pl.ds(first + r * per + k, C, stride=per), :]
                out[r : r + C, k * 128 : (k + 1) * 128] = piece.astype(BF)
                out_t[k * 128 : (k + 1) * 128, r : r + C] = piece.T.astype(BF)
    for i in range(ROW_CONV):
        spread[i * 128 : (i + 1) * 128, :] = jnp.broadcast_to(rows[i : i + 1, :], (128, 128)).T
    gain = jnp.concatenate([rows[i : i + 1, :] for i in range(3)], axis=1)
    shift = jnp.concatenate([rows[3 + i : 4 + i, :] for i in range(3)], axis=1)
    live_total = stats[2:3, :]
    average = stats[0:1, :] / live_total
    variance = stats[1:2, :] / live_total - average * average
    inverse = lax.rsqrt(variance + EPS)
    norm[0:1, :] = inverse * gain
    norm[1:2, :] = shift - average * inverse * gain
    norm[2:3, :] = inverse
    norm[3:4, :] = average * inverse


def mid_kernel(shard,conv_ref,nodes_ref,dy_ref,mask_ref,stats_ref,rows_ref,gathered_ref,
    out_ref,dfirst_ref,grads_ref,bns_ref,
    flat_ref,bn_ref,vb_ref,wj_ref,wjt_ref,wo_ref,wot_ref,wh_ref,wht_ref,wf_ref,wft_ref,
    gj_ref,go_ref,gh_ref,gf_ref,vs_ref,hb_ref,first_s,second_s,qkv_s,kn_s,vn_s,a_s,o_s,ob_s,do_s,dqkv_s,x_s,acc_s,dx_s):
    step=pl.program_id(0)
    rep=T//128
    @pl.when(step==0)
    def _():
        for r in (gj_ref,go_ref,gh_ref,gf_ref,vs_ref,hb_ref,bns_ref): r[...]=jnp.zeros_like(r)
        prepare(stats_ref,rows_ref,gathered_ref,shard,flat_ref,bn_ref,vb_ref,
            ((ROW_JOINT,wj_ref,wjt_ref),(ROW_OUT,wo_ref,wot_ref),(ROW_HIDDEN,wh_ref,wht_ref),(ROW_FINAL,wf_ref,wft_ref)))
    def col(i,n=C):
        v=vb_ref[pl.ds(i*C,n),:]
        return jnp.concatenate([v]*rep,axis=1) if rep>1 else v
    def fold(x):
        r=x[:,:128]
        for k in range(1,rep): r=r+x[:,128*k:128*(k+1)]
        return r
    scale_a=bn_ref[0:1,:]; shift_b=bn_ref[1:2,:]; r_row=bn_ref[2:3,:]; ar_row=bn_ref[3:4,:]
    first=nodes_ref[...].astype(F32)+(conv_ref[...]*scale_a+shift_b)
    firstT=first.T
    first_s[...]=firstT
    dy=dy_ref[...]
    dyT32=dy.astype(F32).T
    do_s[...]=dyT32
    def ln(x):
        m=jnp.mean(x,axis=0,keepdims=True); c=x-m
        rs=lax.rsqrt(jnp.mean(c*c,axis=0,keepdims=True)+EPS)
        return c*rs, rs
    xh1,rs1=ln(firstT)
    x1=(xh1*col(2)+col(3)).astype(BF)
    x_s[0]=x1
    q=nn(wjt_ref[0:C,:],x1)+col(4)
    qkv_s[0:C,:]=q.astype(BF)
    k=nn(wjt_ref[C:2*C,:],x1)
    qkv_s[C:2*C,:]=k.astype(BF)
    kn_s[...]=k.T.astype(BF)
    v=nn(wjt_ref[2*C:,:],x1)+col(5)
    qkv_s[2*C:,:]=v.astype(BF)
    vn_s[...]=v.T.astype(BF)
    scale=HD**-0.5
    c2=scale*1.4426950408889634
    pi=lax.broadcasted_iota(jnp.int32,(BLK,BLK),0); qi=lax.broadcasted_iota(jnp.int32,(BLK,BLK),1)
    same=(pi&3)==(qi&3)
    lives=[]
    def bd(ref,row,blk):
        parts=[]
        z=jnp.zeros((HD,BLK),BF)
        for i in range(2):
            pass
        return parts
    z=jnp.zeros((HD,BLK),BF)
    masks=[]
    for b in range(rep):
        lv=jnp.broadcast_to(mask_ref[b].astype(F32),(BLK,BLK)).T
        live=(lv>0.5)&same
        bias=jnp.where(same,-1e9/scale,-1e30)
        masks.append((jnp.concatenate([live,live],axis=1),jnp.concatenate([bias,bias],axis=1)))
    def ex(ref,g,i,cs):
        qh=ref[g*128+i*32:g*128+(i+1)*32,cs]
        return jnp.concatenate([qh if t==i else z for t in range(4)],axis=0)
    tasks=[(b,g,hp*2) for b in range(rep) for g in range(3) for hp in range(2)]
    S={};A={}
    def f_s(t):
        b,g,h0=t; cs=slice(b*BLK,(b+1)*BLK)
        S[t]=nn(kn_s[cs,g*128:(g+1)*128],jnp.concatenate([ex(qkv_s,g,h0,cs),ex(qkv_s,g,h0+1,cs)],axis=1))
    def f_a(t):
        b,g,h0=t; cs=slice(b*BLK,(b+1)*BLK)
        s=jnp.where(masks[b][0],S.pop(t),masks[b][1])
        m=jnp.max(s,axis=0,keepdims=True)
        e=jnp.exp2((s-m)*c2)
        l=jnp.sum(e,axis=0,keepdims=True)
        a=(e*(1.0/l)).astype(BF)
        for i in range(2): a_s[g*4+h0+i,:,cs]=a[:,i*128:(i+1)*128]
        A[t]=a
    def f_o(t):
        b,g,h0=t; cs=slice(b*BLK,(b+1)*BLK)
        a=A.pop(t)
        for i in range(2):
            h=g*4+h0+i
            o_s[h*32:(h+1)*32,cs]=nn(qkv_s[2*C+h*32:2*C+(h+1)*32,cs],a[:,i*128:(i+1)*128])
    def skew(stages,tasks):
        for i in range(len(tasks)+len(stages)-1):
            for k,st in enumerate(stages):
                if 0<=i-k<len(tasks): st(tasks[i-k])
    skew([f_s,f_a,f_o],tasks)
    ob=o_s[...].astype(BF)
    ob_s[...]=ob
    secondT=first_s[...]+(nn(wot_ref[...],ob)+col(6))
    second_s[...]=secondT
    xh2,rs2=ln(secondT)
    x2=(xh2*col(7)+col(8)).astype(BF)
    x_s[1]=x2
    dyTb=do_s[...].astype(BF)
    FC=512
    c0=0.7978845608028654; c1=0.044715
    HH={};PP={}
    def g_h(f):
        fs=slice(f*FC,(f+1)*FC)
        HH[f]=(nn(wht_ref[fs,:],x2),nn(wf_ref[fs,:],dyTb))
    def g_g(f):
        fs=slice(f*FC,(f+1)*FC)
        hb=vb_ref[9*C+f*FC:9*C+(f+1)*FC,:]
        hb=jnp.concatenate([hb]*rep,axis=1)
        h,da=HH.pop(f)
        h=h+hb
        h2=h*h
        t=jnp.tanh(h*(c0+(c0*c1)*h2))
        p=0.5+0.5*t
        act=(h*p).astype(BF)
        dg=p*(1.0+h*(1.0-p)*(2*c0+(6*c0*c1)*h2))
        dpb=(da*dg).astype(BF)
        hb_ref[fs,:]+=fold(dpb.astype(F32))
        PP[f]=(act,dpb)
    def g_o(f):
        fs=slice(f*FC,(f+1)*FC)
        act,dpb=PP.pop(f)
        o=nn(wft_ref[:,fs],act)
        d=nn(wh_ref[:,fs],dpb)
        if f==0:
            acc_s[...]=o; dx_s[...]=d
        else:
            acc_s[...]+=o; dx_s[...]+=d
        gf_ref[fs,:]+=nn(act,dy)
        gh_ref[:,fs]+=nt(x2,dpb)
    skew([g_h,g_g,g_o],list(range(F//FC)))
    outT=second_s[...]+(acc_s[...]+col(15-2))
    out_ref[...]=outT.T.astype(BF)
    def ln_back(x,dx,gain,vi):
        xh,rs=ln(x)
        vs_ref[vi]+=fold(dx*xh)
        vs_ref[vi+1]+=fold(dx)
        dh=dx*gain
        m1=jnp.mean(dh,axis=0,keepdims=True)
        m2=jnp.mean(dh*xh,axis=0,keepdims=True)
        return rs*(dh-m1-xh*m2)
    dsec=do_s[...]+ln_back(second_s[...],dx_s[...],col(7),0)
    second_s[...]=dsec
    dbr=dsec.astype(BF)
    vs_ref[2]+=fold(dbr.astype(F32))
    go_ref[...]+=nt(ob_s[...],dbr)
    dat=nn(wo_ref[...],dbr)
    do_s[...]=dat
    dob=dat.astype(BF)
    D={};G={}
    def b_d(t):
        b,g,h0=t; cs=slice(b*BLK,(b+1)*BLK)
        D[t]=nn(vn_s[cs,g*128:(g+1)*128],jnp.concatenate([ex(dob,g,h0,cs),ex(dob,g,h0+1,cs)],axis=1))
    def b_s(t):
        b,g,h0=t; cs=slice(b*BLK,(b+1)*BLK)
        dA=D.pop(t)
        out=[]
        for i in range(2):
            h=g*4+h0+i; hs=slice(h*32,(h+1)*32)
            delta=jnp.sum(dob[hs,cs].astype(F32)*o_s[hs,cs],axis=0,keepdims=True)
            out.append((a_s[h,:,cs].astype(F32)*(dA[:,i*128:(i+1)*128]-delta)).astype(BF))
        G[t]=out
    def b_q(t):
        b,g,h0=t; cs=slice(b*BLK,(b+1)*BLK)
        lrow=mask_ref[b].astype(F32)
        out=G.pop(t)
        for i in range(2):
            h=g*4+h0+i; hs=slice(h*32,(h+1)*32); ds=out[i]
            kh=(qkv_s[C+h*32:C+(h+1)*32,cs].astype(F32)*lrow).astype(BF)
            dqkv_s[h*32:(h+1)*32,cs]=(nn(kh,ds)*scale).astype(BF)
            dqkv_s[C+h*32:C+(h+1)*32,cs]=(nt(qkv_s[hs,cs],ds)*(lrow*scale)).astype(BF)
            dqkv_s[2*C+h*32:2*C+(h+1)*32,cs]=nt(dob[hs,cs],a_s[h,:,cs]).astype(BF)
    skew([b_d,b_s,b_q],tasks)
    vs_ref[3]+=fold(dqkv_s[0:C,:].astype(F32))
    vs_ref[4]+=fold(dqkv_s[2*C:,:].astype(F32))
    gj_ref[...]+=nt(x_s[0],dqkv_s[...])
    dx1=nn(wj_ref[...],dqkv_s[...])
    dfT=second_s[...]+ln_back(first_s[...],dx1,col(2),5)
    df=dfT.T
    dfirst_ref[...]=df
    cen=conv_ref[...]*r_row-ar_row
    bns_ref[0]+=jnp.sum((df*cen).reshape(T//8,8,C),axis=0)
    bns_ref[1]+=jnp.sum(df.reshape(T//8,8,C),axis=0)
    bns_ref[2]+=jnp.sum(dy.astype(F32).reshape(T//8,8,C),axis=0)
    @pl.when(step==pl.num_programs(0)-1)
    def _():
        flat_ref[...]=jnp.zeros_like(flat_ref)
        for vi,row in ((0,21),(1,24),(2,18),(3,12),(4,15),(5,6),(6,9)):
            for i in range(3):
                flat_ref[pl.ds(row+i,1),:]=jnp.sum(vs_ref[vi,i*128:(i+1)*128,:].T,axis=0,keepdims=True)
        for i in range(12):
            flat_ref[pl.ds(27+i,1),:]=jnp.sum(hb_ref[i*128:(i+1)*128,:].T,axis=0,keepdims=True)
        for first,mat in ((ROW_JOINT,gj_ref),(ROW_OUT,go_ref),(ROW_HIDDEN,gh_ref),(ROW_FINAL,gf_ref)):
            rows,cols=mat.shape
            per=cols//128
            for k in range(per):
                for r in range(0,rows,C):
                    flat_ref[pl.ds(first+r*per+k,C,stride=per),:]=mat[r:r+C,k*128:(k+1)*128]
        for i in range(grads_ref.shape[0]*8):
            part=flat_ref[i*shard:(i+1)*shard,:]
            pad=grads_ref.shape[-2]-shard
            grads_ref[i//8,(i//4)%2,(i//2)%2,i%2]=jnp.concatenate([part,jnp.zeros((pad,128),F32)],axis=0).astype(BF)


def middle(conv,nodes,dy,mask3,stats,rows,gathered,shard):
    n=conv.shape[0]
    row=rows_of(C,T)
    flat_rows=gathered.shape[0]*8*shard
    in_specs=[row,row,row,pl.BlockSpec((T//128,1,128),lambda i:(i,0,0)),whole(*stats.shape),whole(*rows.shape),whole(*gathered.shape)]
    outs=[((n,C),BF,row),((n,C),F32,row),(gathered.shape,BF,whole(*gathered.shape)),((3,8,C),F32,whole(3,8,C))]
    mats=[]
    for shape in ((C,3*C),(C,C),(C,F),(F,C)): mats+=[(shape,BF),(shape[::-1],BF)]
    scr=[pltpu.VMEM(s,d) for s,d in [((flat_rows,128),F32),((8,C),F32),((ROW_CONV*128,128),F32)]+mats+[((C,3*C),F32),((C,C),F32),((C,F),F32),((F,C),F32),((7,C,128),F32),((F,128),F32),((C,T),F32),((C,T),F32),((3*C,T),BF),((T,C),BF),((T,C),BF),((HEADS,BLK,T),BF),((C,T),F32),((C,T),BF),((C,T),F32),((3*C,T),BF),((2,C,T),BF),((C,T),F32),((C,T),F32)]]
    return pl.pallas_call(functools.partial(mid_kernel,shard),grid=(n//T,),in_specs=in_specs,out_specs=[o[2] for o in outs],
      out_shape=[jax.ShapeDtypeStruct(o[0],o[1]) for o in outs],scratch_shapes=scr,
      compiler_params=VMEM)(conv,nodes,dy,mask3,stats,rows,gathered)


def shards(nodes_in, out_grad, neighbours, node_mask, master, first_moment, second_moment):
    n = nodes_in.shape[0]
    count, cores = lax.axis_size(AXES), lax.axis_size("grp")
    shard = master.shape[0] // 128
    flat = [a.reshape(shard, 128) for a in (master, first_moment, second_moment)]
    mask3 = node_mask.reshape(n // 128, 1, 128)
    convolved, gathered, first_rows, stats = convolve(neighbours, nodes_in, mask3, flat[0], count, cores)
    output, delta_first, grads, norm_sums = middle(
        convolved, nodes_in, out_grad, mask3, stats, first_rows, gathered, shard
    )
    node_grad, new_master, new_first, new_second, new_low, bias_total = convolve_back(
        neighbours, delta_first, convolved, nodes_in, mask3, norm_sums, stats, first_rows, grads, *flat, count, cores
    )
    return (
        output,
        node_grad,
        new_master.reshape(-1),
        new_first.reshape(-1),
        new_second.reshape(-1),
        new_low.reshape(-1),
        bias_total.reshape(-1),
    )


def solution(mesh):
    rows, flat = P(AXES, None), P(AXES)
    return jax.shard_map(
        shards,
        mesh=mesh,
        in_specs=(rows, rows, rows, flat, flat, flat, flat),
        out_specs=(rows, rows, flat, flat, flat, flat, P()),
        check_vma=False,
    )
```

```python
import functools

import jax
import jax.numpy as jnp
from jax import lax
from jax.experimental import pallas as pl
from jax.experimental.pallas import tpu as pltpu
from jax.sharding import PartitionSpec as P

C = 384
HEADS = 12
HD = 32
F = 1536
HALO = 64
STEP = 5
EPS = 1e-5
AXES = ("rows", "grp")
F32 = jnp.float32
BF = jnp.bfloat16

BLK = 128
T = 512
TB = 512
ROW_CONV = (10 * C + F) // 128
ROW_JOINT = ROW_CONV + 27 * C // 128
ROW_OUT = ROW_JOINT + C * 3 * C // 128
ROW_HIDDEN = ROW_OUT + C * C // 128
ROW_FINAL = ROW_HIDDEN + C * F // 128
ROW_END = ROW_FINAL + C * F // 128
VMEM = pltpu.CompilerParams(vmem_limit_bytes=60 * 1024 * 1024)


def nn(a, b):
    return jnp.dot(a, b, preferred_element_type=F32)


def nt(a, b):
    return lax.dot_general(a, b, (((1,), (1,)), ((), ())), preferred_element_type=F32)


def whole(*shape):
    return pl.BlockSpec(shape, lambda i: (0,) * len(shape), pipeline_mode=pl.Buffered(1))


def skew(stages, tasks):
    for i in range(len(tasks) + len(stages) - 1):
        for k, stage in enumerate(stages):
            if 0 <= i - k < len(tasks):
                stage(tasks[i - k])


def along_sublanes(row):
    parts = [row[:, i : i + 128] for i in range(0, row.shape[1], 128)]
    return jnp.concatenate([jnp.broadcast_to(p, (128, 128)).T for p in parts], axis=0)


def lane_sums(value):
    parts = [value[i : i + 128, :].T for i in range(0, value.shape[0], 128)]
    return jnp.concatenate([jnp.sum(p, axis=0, keepdims=True) for p in parts], axis=1)


def rows_of(width, size):
    return pl.BlockSpec((size, width), lambda i: (i, 0))


MESH = pl.DeviceIdType.MESH


def CUTS_GATHER(nh):
    return [1 + (s + 1) // nh for s in range(nh)] + [4, 7]


def round_up(value, step):
    return -(-value // step) * step


def my_place():
    return lax.axis_index("rows") * lax.axis_size("grp") + lax.axis_index("grp")


def device(place, cores):
    return (place // cores, place % cores)


def stages_of(count):
    out, stride = [], 1
    while stride < count:
        size = min(8, count // stride)
        out.append((stride, size))
        stride *= size
    return out


def others(me, stride, size):
    mine = (me // stride) % size
    return mine, [(k, me + ((mine + k) % size - mine) * stride) for k in range(1, size)]


def greet(partners, cores):
    barrier = pltpu.get_barrier_semaphore()
    for place in partners:
        pl.semaphore_signal(barrier, inc=1, device_id=device(place, cores), device_id_type=MESH)
    pl.semaphore_wait(barrier, len(partners))


def send(source, target, send_sem, recv_sem, place, cores):
    return pltpu.make_async_remote_copy(
        src_ref=source,
        dst_ref=target,
        send_sem=send_sem,
        recv_sem=recv_sem,
        device_id=device(place, cores),
        device_id_type=MESH,
    )


def all_sum(value, me, count, cores, slots, send_sems, recv_sems, beside=None):
    for s, (stride, size) in enumerate(stages_of(count)):
        mine, partners = others(me, stride, size)
        slots[s, mine] = value
        copies = [
            send(slots.at[s, mine], slots.at[s, mine], send_sems.at[s, k], recv_sems.at[s, k], place, cores)
            for k, place in partners
        ]
        for copy in copies:
            copy.start()
        if beside is not None:
            beside(s)
        for copy in copies:
            copy.wait()
        value = slots[s, 0]
        for i in range(1, size):
            value = value + slots[s, i]
    return value


def sum_scratch(count, rows, width):
    n = len(stages_of(count))
    return [
        pltpu.VMEM((n, 8, rows, width), F32),
        pltpu.SemaphoreType.DMA((n, 8)),
        pltpu.SemaphoreType.DMA((n, 8)),
    ]


def conv_kernel(count, cores, owners, near_ref, nodes_ref, dy_ref, mask_ref, master_ref,
                convt_ref, conv_ref, nodest_ref, dyt_ref, gathered_ref, first_ref, stats_ref,
                ext, extt, dy_s, early, weight, sums, own_s, local_sem, halo_send, halo_recv, e_send, e_recv, g_send,
                g_recv, slots, s_send, s_recv):
    step = pl.program_id(0)
    steps = pl.num_programs(0)
    block = (step + 1) % steps
    n = nodes_ref.shape[0]
    shard = master_ref.shape[0]
    padded = gathered_ref.shape[-2]
    half = padded // 2
    e_rows = early.shape[1]
    me = my_place()
    low, high = me % 8, me // 8
    y, x, g = low // 4, (low // 2) % 2, low % 2
    highs = stages_of(count // 8)
    left, right = (me + count - 1) % count, (me + 1) % count

    local = pltpu.make_async_copy(nodes_ref, ext.at[pl.ds(HALO, n)], local_sem.at[0])
    keep = pltpu.make_async_copy(own_s, gathered_ref.at[high, y, x, g], local_sem.at[1])
    local_dy = pltpu.make_async_copy(dy_ref, dy_s, local_sem.at[2])

    def turn(k):
        at = pl.ds(pl.multiple_of(k * BLK, BLK), BLK)
        extt[:, at] = ext[at, :].T
        return 0
    to_left = send(nodes_ref.at[pl.ds(0, HALO)], ext.at[pl.ds(HALO + n, HALO)], halo_send.at[0], halo_recv.at[0], left, cores)
    to_right = send(nodes_ref.at[pl.ds(n - HALO, HALO)], ext.at[pl.ds(0, HALO)], halo_send.at[1], halo_recv.at[1], right, cores)

    def high_copies(s):
        stride, size = highs[s]
        mine, partners = others(high, stride, size)
        own = gathered_ref.at[pl.ds(high // stride * stride, stride), y, x, g]
        return [
            send(own, own, g_send.at[s, k], g_recv.at[s, k], place * 8 + low, cores)
            for k, place in partners
        ]

    nh = len(highs)
    y_place, x_place, g_place = me + 4 - 8 * y, me + 2 - 4 * x, me + 1 - 2 * g

    def quad_copies(t):
        top, bottom = pl.ds(0, half), pl.ds(half, half)
        if t == 0:
            a = gathered_ref.at[:, y, x, g, top]
            b = gathered_ref.at[:, y, x, g, bottom]
            to_a, to_b = y_place, x_place
        else:
            a = gathered_ref.at[:, :, x, g, top]
            b = gathered_ref.at[:, y, :, g, bottom]
            to_a, to_b = x_place, y_place
        s = nh + t
        return [send(a, a, g_send.at[s, 0], g_recv.at[s, 0], to_a, cores), send(b, b, g_send.at[s, 1], g_recv.at[s, 1], to_b, cores)]

    def core_copies():
        own = gathered_ref.at[:, :, :, g]
        return [send(own, own, g_send.at[nh + 2, 0], g_recv.at[nh + 2, 0], g_place, cores)]

    plan = [functools.partial(high_copies, s) for s in range(nh)]
    plan += [functools.partial(quad_copies, 0), functools.partial(quad_copies, 1), core_copies]
    cuts = CUTS_GATHER(nh)

    @pl.when(step == 0)
    def _():
        local.start()
        local_dy.start()
        sums[...] = jnp.zeros_like(sums)
        own = jnp.concatenate([master_ref[...], jnp.zeros((padded - shard, 128), F32)], axis=0).astype(BF)
        own_s[...] = own
        keep.start()
        wide = [h for h in range(1, count // 8)]
        partners = [left, right]
        partners += [(high + h) % (count // 8) * 8 + low for h in wide]
        partners += [place for _, place in others(me, 1, 8)[1]]
        greet(partners, cores)
        for o in range(owners):
            @pl.when(low == o)
            def _():
                @pl.when(high == 0)
                def _():
                    early[o] = own[:e_rows]
                    out = [
                        send(early.at[o], early.at[o], e_send.at[o, 8 + h], e_recv.at[o, 0], h * 8 + o, cores)
                        for h in wide
                    ]
                    for copy in out:
                        copy.start()
                    for copy in out:
                        copy.wait_send()
                @pl.when(high > 0)
                def _():
                    send(early.at[o], early.at[o], e_send.at[o, 8], e_recv.at[o, 0], left, cores).wait_recv()
                out = [
                    send(early.at[o], early.at[o], e_send.at[o, k], e_recv.at[o, 1], me + k - o, cores)
                    for k in range(8) if k != o
                ]
                for copy in out:
                    copy.start()
                for copy in out:
                    copy.wait_send()
        to_left.start()
        to_right.start()
        keep.wait()
        for copy in plan[0]():
            copy.start()
        local.wait()
        lax.fori_loop(1, n // BLK, lambda k, _: turn(k), 0)
        for o in range(owners):
            @pl.when(low != o)
            def _():
                send(early.at[o], early.at[o], e_send.at[o, 8], e_recv.at[o, 1], left, cores).wait_recv()
        for o in range(owners):
            rows = min(shard, e_rows)
            first_ref[pl.ds(o * shard, rows), :] = early[o].astype(F32)[:rows]
        for j in range(27):
            row = jnp.concatenate([first_ref[ROW_CONV + 3 * j + i : ROW_CONV + 3 * j + i + 1, :] for i in range(3)], axis=1)
            weight[j] = along_sublanes(row)

    for s in range(len(plan) - 1):
        @pl.when(step == cuts[s])
        def _(s=s):
            for copy in plan[s]():
                copy.wait()
            for copy in plan[s + 1]():
                copy.start()

    @pl.when(step == steps - 2)
    def _():
        to_left.wait()
        to_right.wait()
        turn(0)
        turn(n // BLK)

    sub = lax.broadcasted_iota(jnp.int32, (2 * BLK, BLK), 0).astype(F32).astype(BF)
    one, zero = jnp.ones((), BF), jnp.zeros((), BF)
    pairs = [(j, j + 1) for j in range(0, 12, 2)] + [(12, 14)] + [(j, j + 1) for j in range(15, 27, 2)]
    at = pl.multiple_of(block * T, T)
    lane = lax.broadcasted_iota(jnp.int32, (27, BLK), 1)
    places, totals, picks, comes = {}, {}, {}, {}
    for b in range(T // BLK):
        near = near_ref[:, b * BLK : (b + 1) * BLK]
        places[b] = jnp.where(near < 0, -1, near + lane).astype(F32).astype(BF)

    def pick(task):
        b, q = task
        if q == 0:
            center = ext[pl.ds(at + b * BLK + HALO, BLK), :].astype(F32).T
            nodest_ref[:, b * BLK : (b + 1) * BLK] = center.astype(BF)
            totals[b] = center * weight[13]
        picks[task] = jnp.concatenate(
            [jnp.where(places[b][j : j + 1, :] == sub, one, zero) for j in pairs[q]], axis=1
        )

    def multiply(task):
        b, q = task
        comes[task] = nn(extt[:, pl.ds(at + b * BLK, 2 * BLK)], picks.pop(task))

    def add(task):
        b, q = task
        come = comes.pop(task)
        totals[b] = totals[b] + (come[:, :BLK] * weight[pairs[q][0]] + come[:, BLK:] * weight[pairs[q][1]])
        if q == len(pairs) - 1:
            total = totals.pop(b)
            convt_ref[:, b * BLK : (b + 1) * BLK] = total
            conv_ref[b * BLK : (b + 1) * BLK, :] = total.T.astype(BF)
            live = mask_ref[b].astype(F32)
            kept = total * live
            sums[0] += kept
            sums[1] += kept * total
            sums[2, 0:1] += live

    skew([pick, multiply, add], [(b, q) for b in range(T // BLK) for q in range(len(pairs))])

    @pl.when(step == steps - 1)
    def _():
        rows = [lane_sums(sums[i]) for i in range(2)]
        rows += [jnp.broadcast_to(jnp.sum(sums[2, 0:1], axis=1, keepdims=True), (1, C))]
        rows = jnp.concatenate(rows + [jnp.zeros((5, C), F32)], axis=0)
        local_dy.wait()
        cut = len(stages_of(count))

        def beside(s):
            def body(k, _):
                at = pl.ds(pl.multiple_of(k * BLK, BLK), BLK)
                dyt_ref[:, at] = dy_s[at, :].T
                return 0
            lax.fori_loop(n // BLK * s // cut, n // BLK * (s + 1) // cut, body, 0)

        stats_ref[...] = all_sum(rows, me, count, cores, slots, s_send, s_recv, beside)
        for copy in plan[-1]():
            copy.wait()


def convolve(near, nodes, dy, mask3, master, count, cores):
    n = nodes.shape[0]
    steps = n // T
    shard = master.shape[0]
    padded = round_up(shard, 32)
    owners = -(-ROW_JOINT // shard)
    e_rows = min(padded, round_up(ROW_JOINT, 16))
    down = pl.BlockSpec((T, C), lambda i: ((i + 1) % steps, 0))
    across = pl.BlockSpec((C, T), lambda i: (0, (i + 1) % steps))
    anywhere = pl.BlockSpec(memory_space=pl.ANY)
    stages = len(stages_of(count // 8)) + 3
    first_rows = round_up((owners - 1) * shard + e_rows, 8)
    return pl.pallas_call(
        functools.partial(conv_kernel, count, cores, owners),
        grid=(steps,),
        in_specs=[
            pl.BlockSpec((27, T), lambda i: (0, (i + 1) % steps)),
            anywhere,
            anywhere,
            pl.BlockSpec((T // BLK, 1, 128), lambda i: ((i + 1) % steps, 0, 0)),
            whole(shard, 128),
        ],
        out_specs=[across, down, across, whole(C, n), anywhere, whole(first_rows, 128), whole(8, C)],
        out_shape=[
            jax.ShapeDtypeStruct((C, n), F32),
            jax.ShapeDtypeStruct((n, C), BF),
            jax.ShapeDtypeStruct((C, n), BF),
            jax.ShapeDtypeStruct((C, n), BF),
            jax.ShapeDtypeStruct((count // 8, 2, 2, 2, padded, 128), BF),
            jax.ShapeDtypeStruct((first_rows, 128), F32),
            jax.ShapeDtypeStruct((8, C), F32),
        ],
        scratch_shapes=[
            pltpu.VMEM((n + 2 * HALO, C), BF),
            pltpu.VMEM((C, n + 2 * HALO), BF),
            pltpu.VMEM((n, C), BF),
            pltpu.VMEM((owners, e_rows, 128), BF),
            pltpu.VMEM((27, C, 128), F32),
            pltpu.VMEM((3, C, 128), F32),
            pltpu.VMEM((padded, 128), BF),
            pltpu.SemaphoreType.DMA((3,)),
            pltpu.SemaphoreType.DMA((2,)),
            pltpu.SemaphoreType.DMA((2,)),
            pltpu.SemaphoreType.DMA((owners, 8 + count // 8)),
            pltpu.SemaphoreType.DMA((owners, 2)),
            pltpu.SemaphoreType.DMA((stages, 8)),
            pltpu.SemaphoreType.DMA((stages, 8)),
        ]
        + sum_scratch(count, 8, C),
        compiler_params=pltpu.CompilerParams(
            vmem_limit_bytes=60 * 1024 * 1024, collective_id=0, has_side_effects=True
        ),
    )(near, nodes, dy, mask3, master)


def conv_back_kernel(count, cores, owners, near_hbm, first_hbm, conv_hbm, x_ref, mask_ref, sums_ref, stats_ref,
                     rows_ref, grads_ref,
                     grad_ref, total_s, bias_out,
                     near, ext, delta, conv, weight, dw, kept, r1, r2, r3, r4, local_sem, halo_send, halo_recv, g_send,
                     g_recv, slots, s_send, s_recv, w_own, w_slots, w_high, w_sem, w_recv, w_recv_high, early_s):
    step = pl.program_id(0)
    steps = pl.num_programs(0)
    block = (step + 1) % steps
    n = first_hbm.shape[0]
    shard = total_s.shape[0]
    padded = grads_ref.shape[-2]
    half = padded // 2
    me = my_place()
    low, high = me % 8, me // 8
    y, x, g = low // 4, (low // 2) % 2, low % 2
    highs = stages_of(count // 8)[::-1]
    nh = len(highs)
    left, right = (me + count - 1) % count, (me + 1) % count
    y_place, x_place, g_place = me + 4 - 8 * y, me + 2 - 4 * x, me + 1 - 2 * g
    top, bottom = pl.ds(0, half), pl.ds(half, half)

    locals_ = [
        pltpu.make_async_copy(first_hbm, delta, local_sem.at[0]),
        pltpu.make_async_copy(conv_hbm, conv, local_sem.at[1]),
        pltpu.make_async_copy(near_hbm, near.at[:, pl.ds(BLK, n)], local_sem.at[2]),
        pltpu.make_async_copy(grads_ref.at[:, :, :, g], kept, local_sem.at[3]),
    ]
    near_halo = [
        send(near_hbm.at[:, pl.ds(0, BLK)], near.at[:, pl.ds(BLK + n, BLK)], halo_send.at[0], halo_recv.at[0], left, cores),
        send(near_hbm.at[:, pl.ds(n - BLK, BLK)], near.at[:, pl.ds(0, BLK)], halo_send.at[1], halo_recv.at[1], right, cores),
    ]
    delta_halo = [
        send(ext.at[pl.ds(HALO, HALO)], ext.at[pl.ds(HALO + n, HALO)], halo_send.at[2], halo_recv.at[2], left, cores),
        send(ext.at[pl.ds(n, HALO)], ext.at[pl.ds(0, HALO)], halo_send.at[3], halo_recv.at[3], right, cores),
    ]

    def core_copies():
        return [send(grads_ref.at[:, :, :, 1 - g], r1, g_send.at[0, 0], g_recv.at[0, 0], g_place, cores)]

    def core_add():
        def body(i, _):
            kept[i // 4, (i // 2) % 2, i % 2] = (
                kept[i // 4, (i // 2) % 2, i % 2].astype(F32) + r1[i // 4, (i // 2) % 2, i % 2].astype(F32)
            ).astype(BF)
            return 0
        lax.fori_loop(0, count // 2, body, 0)

    def quad_copies_0():
        return [
            send(kept.at[:, :, 1 - x, top], r2.at[0], g_send.at[1, 0], g_recv.at[1, 0], x_place, cores),
            send(kept.at[:, 1 - y, :, bottom], r2.at[1], g_send.at[1, 1], g_recv.at[1, 1], y_place, cores),
        ]

    def quad_add_0():
        def body(i, _):
            h, w = i // 2, i % 2
            kept[h, w, x, top] = (
                kept[h, w, x, top].astype(F32) + r2[0, h, w].astype(F32)
            ).astype(BF)
            kept[h, y, w, bottom] = (
                kept[h, y, w, bottom].astype(F32) + r2[1, h, w].astype(F32)
            ).astype(BF)
            return 0
        lax.fori_loop(0, count // 4, body, 0)

    def quad_copies_1():
        return [
            send(kept.at[:, 1 - y, x, top], r3.at[0], g_send.at[2, 0], g_recv.at[2, 0], y_place, cores),
            send(kept.at[:, y, 1 - x, bottom], r3.at[1], g_send.at[2, 1], g_recv.at[2, 1], x_place, cores),
        ]

    def quad_add_1():
        def body(h, _):
            kept[h, y, x, top] = (
                kept[h, y, x, top].astype(F32) + r3[0, h].astype(F32)
            ).astype(BF)
            kept[h, y, x, bottom] = (
                kept[h, y, x, bottom].astype(F32) + r3[1, h].astype(F32)
            ).astype(BF)
            return 0
        lax.fori_loop(0, count // 8, body, 0)

    bases = []
    base = 0
    for stride, size in highs:
        bases.append(base)
        base += (size - 1) * stride

    def high_copies(s):
        stride, size = highs[s]
        mine, partners = others(high, stride, size)
        out = []
        for k, place in partners:
            source = kept.at[pl.ds(place // stride * stride, stride), y, x]
            target = r4.at[pl.ds(bases[s] + (k - 1) * stride, stride)]
            out.append(send(source, target, g_send.at[3 + s, k], g_recv.at[3 + s, k], place * 8 + low, cores))
        return out

    def high_add(s):
        stride, size = highs[s]
        start = high // stride * stride
        def body(i, _):
            value = kept[start + i, y, x].astype(F32)
            for k in range(size - 1):
                value = value + r4[bases[s] + k * stride + i].astype(F32)
            if s == nh - 1:
                total_s[...] = value[:shard]
            else:
                kept[start + i, y, x] = value.astype(BF)
            return 0
        lax.fori_loop(0, stride, body, 0)

    plan = [(core_copies, core_add), (quad_copies_0, quad_add_0), (quad_copies_1, quad_add_1)]
    plan += [(functools.partial(high_copies, s), functools.partial(high_add, s)) for s in range(nh)]
    cuts = CUTS_SCATTER(nh)

    @pl.when(step == 0)
    def _():
        for copy in locals_:
            copy.start()
        dw[...] = jnp.zeros_like(dw)
        partners = [left, right]
        partners += [(high + h) % (count // 8) * 8 + low for h in range(1, count // 8)]
        partners += [place for _, place in others(me, 1, 8)[1]]
        greet(partners, cores)
        def beside(s):
            if s == 0:
                for copy in plan[0][0]() + near_halo:
                    copy.start()
        total = all_sum(sums_ref[...], me, count, cores, slots, s_send, s_recv, beside)
        gain_total, shift_total = total[0:1], total[1:2]
        bias_out[...] = jnp.concatenate([total[2:3, i * 128 : (i + 1) * 128] for i in range(3)], axis=0)
        early_s[...] = jnp.zeros_like(early_s)
        for i in range(3):
            early_s[i : i + 1, :] = gain_total[:, i * 128 : (i + 1) * 128]
            early_s[3 + i : 4 + i, :] = shift_total[:, i * 128 : (i + 1) * 128]
            early_s[ROW_CONV - 3 + i : ROW_CONV - 2 + i, :] = total[2:3, i * 128 : (i + 1) * 128]
        for k in range(3):
            weight[:, k * 128 : (k + 1) * 128] = rows_ref[pl.ds(ROW_CONV + k, 27, stride=3), :]
        gain = jnp.concatenate([rows_ref[i : i + 1, :] for i in range(3)], axis=1)
        live_total = stats_ref[2:3]
        average = stats_ref[0:1] / live_total
        variance = stats_ref[1:2] / live_total - average * average
        inverse = lax.rsqrt(variance + EPS)
        delta_variance = -0.5 * inverse * inverse * inverse * (gain * gain_total / inverse)
        delta_average = -gain * shift_total * inverse - 2.0 * average * delta_variance
        a = gain * inverse
        b = delta_average / live_total
        c = 2.0 * delta_variance / live_total
        for copy in locals_:
            copy.wait()

        def body(i, _):
            at = pl.ds(pl.multiple_of(i * BLK, BLK), BLK)
            live = jnp.broadcast_to(mask_ref[i].astype(F32), (BLK, BLK)).T
            live = jnp.concatenate([live] * 3, axis=1)
            value = delta[at, :] * a + live * (b + c * conv[at, :].astype(F32))
            ext[pl.ds(pl.multiple_of(i * BLK + HALO, HALO), BLK), :] = value.astype(BF)
            return 0

        lax.fori_loop(0, n // BLK, body, 0)
        for copy in delta_halo:
            copy.start()

    for s in range(len(plan)):
        @pl.when(step == cuts[s])
        def _(s=s):
            for copy in plan[s][0]():
                copy.wait()
            plan[s][1]()
            if s + 1 < len(plan):
                for copy in plan[s + 1][0]():
                    copy.start()

    @pl.when(step == steps - 2)
    def _():
        for copy in near_halo + delta_halo:
            copy.wait()

    start = pl.multiple_of(block * TB, TB)
    target = lax.broadcasted_iota(jnp.int32, (BLK, 2 * BLK), 0).astype(F32).astype(BF)
    one, zero = jnp.ones((), BF), jnp.zeros((), BF)
    lane = lax.broadcasted_iota(jnp.int32, (27, 2 * BLK), 1) - BLK
    places, totals, picks, comes, xs = {}, {}, {}, {}, {}
    for b in range(TB // BLK):
        near_w = near[:, pl.ds(start + b * BLK, 3 * BLK)][:, HALO : HALO + 2 * BLK]
        places[b] = jnp.where(near_w < 0, -1, near_w + lane).astype(F32).astype(BF)

    def pick(task):
        b, q = task
        picks[task] = jnp.concatenate(
            [jnp.where(places[b][j : j + 1, :] == target, one, zero) for j in range(3 * q, 3 * q + 3)], axis=0
        )

    def multiply(task):
        b, q = task
        comes[task] = nn(picks.pop(task), ext[pl.ds(start + b * BLK, 2 * BLK), :])

    def add(task):
        b, q = task
        come = comes.pop(task)
        if q == 0:
            xs[b] = x_ref[b * BLK : (b + 1) * BLK, :].astype(F32)
            totals[b] = delta[pl.ds(start + b * BLK, BLK), :]
        for i in range(3):
            j, part = 3 * q + i, come[i * BLK : (i + 1) * BLK]
            totals[b] = totals[b] + part * weight[j : j + 1, :]
            dw[j] += jnp.sum((part * xs[b]).reshape(BLK // 8, 8, C), axis=0)
        if q == 8:
            grad_ref[b * BLK : (b + 1) * BLK, :] = totals.pop(b)

    skew([pick, multiply, add], [(b, q) for b in range(TB // BLK) for q in range(9)])

    @pl.when(step == steps - 1)
    def _():
        w_own[0:27] = jnp.sum(dw[...], axis=1)
        w_own[27:32] = jnp.zeros((5, C), F32)
        to_first = send(w_own, w_slots.at[low], w_sem.at[0], w_recv.at[low], me - low, cores)

        @pl.when(low != 0)
        def _():
            to_first.start()
            to_first.wait_send()

        @pl.when(low == 0)
        def _():
            for k in range(1, 8):
                send(w_own, w_slots.at[k], w_sem.at[0], w_recv.at[k], me + k, cores).wait_recv()
            w_own[...] = w_own[...] + sum(w_slots[k] for k in range(1, 8))

            @pl.when(high != 0)
            def _():
                up = send(w_own, w_high.at[high], w_sem.at[0], w_recv_high.at[high], 0, cores)
                up.start()
                up.wait_send()

            @pl.when(high == 0)
            def _():
                for h in range(1, count // 8):
                    send(w_own, w_high.at[h], w_sem.at[0], w_recv_high.at[h], h * 8, cores).wait_recv()
                w_own[...] = w_own[...] + sum(w_high[h] for h in range(1, count // 8))
                out = [send(w_own, w_high.at[0], w_sem.at[o], w_recv_high.at[0], o, cores) for o in range(1, owners)]
                for copy in out:
                    copy.start()
                for copy in out:
                    copy.wait_send()

        for o in range(owners):
            @pl.when(me == o)
            def _(o=o):
                if o == 0:
                    sums = w_own[...]
                else:
                    send(w_own, w_high.at[0], w_sem.at[0], w_recv_high.at[0], 0, cores).wait_recv()
                    sums = w_high[0]
                for k in range(3):
                    early_s[pl.ds(ROW_CONV + k, 27, stride=3), :] = sums[:27, k * 128 : (k + 1) * 128]
                rows = min(shard, early_s.shape[0] - o * shard)
                total_s[0:rows, :] += early_s[o * shard : o * shard + rows, :]


def CUTS_SCATTER(nh):
    return [1, 3, 4] + [4 + 3 * (s + 1) // nh for s in range(nh)]


def convolve_back(near, delta, conv, nodes, mask3, sums, stats, rows, grads, shard, count, cores):
    n = nodes.shape[0]
    steps = n // TB
    padded = grads.shape[-2]
    highs = count // 8
    owners = -(-ROW_JOINT // shard)
    turned = pl.BlockSpec((TB, C), lambda i: ((i + 1) % steps, 0))
    anywhere = pl.BlockSpec(memory_space=pl.ANY)
    r4_rows = sum((size - 1) * stride for stride, size in stages_of(highs))
    return pl.pallas_call(
        functools.partial(conv_back_kernel, count, cores, owners),
        grid=(steps,),
        in_specs=[
            anywhere,
            anywhere,
            anywhere,
            turned,
            whole(*mask3.shape),
            whole(*sums.shape),
            whole(*stats.shape),
            whole(*rows.shape),
            anywhere,
        ],
        out_specs=[turned, whole(shard, 128), whole(3, 128)],
        out_shape=[
            jax.ShapeDtypeStruct((n, C), F32),
            jax.ShapeDtypeStruct((shard, 128), F32),
            jax.ShapeDtypeStruct((3, 128), F32),
        ],
        scratch_shapes=[
            pltpu.VMEM((27, n + 2 * BLK), jnp.int32),
            pltpu.VMEM((n + 2 * HALO, C), BF),
            pltpu.VMEM((n, C), F32),
            pltpu.VMEM((n, C), BF),
            pltpu.VMEM((27, C), F32),
            pltpu.VMEM((27, 8, C), F32),
            pltpu.VMEM((highs, 2, 2, padded, 128), BF),
            pltpu.VMEM((highs, 2, 2, padded, 128), BF),
            pltpu.VMEM((2, highs, 2, padded // 2, 128), BF),
            pltpu.VMEM((2, highs, padded // 2, 128), BF),
            pltpu.VMEM((r4_rows, padded, 128), BF),
            pltpu.SemaphoreType.DMA((4,)),
            pltpu.SemaphoreType.DMA((4,)),
            pltpu.SemaphoreType.DMA((4,)),
            pltpu.SemaphoreType.DMA((3 + len(stages_of(highs)), 8)),
            pltpu.SemaphoreType.DMA((3 + len(stages_of(highs)), 8)),
        ]
        + sum_scratch(count, 8, C)
        + [
            pltpu.VMEM((32, C), F32),
            pltpu.VMEM((8, 32, C), F32),
            pltpu.VMEM((highs, 32, C), F32),
            pltpu.SemaphoreType.DMA((max(owners, 1),)),
            pltpu.SemaphoreType.DMA((8,)),
            pltpu.SemaphoreType.DMA((highs,)),
            pltpu.VMEM((round_up(ROW_JOINT, 8), 128), F32),
        ],
        compiler_params=pltpu.CompilerParams(
            vmem_limit_bytes=60 * 1024 * 1024, collective_id=1, has_side_effects=True
        ),
    )(near, delta, conv, nodes, mask3, sums, stats, rows, grads)


def prepare(stats, rows, gathered, shard, flat, norm, spread, mats):
    for i in range(gathered.shape[0] * 8):
        flat[i * shard : (i + 1) * shard, :] = gathered[i // 8, (i // 4) % 2, (i // 2) % 2, i % 2].astype(F32)[:shard]
    for first, out, out_t in mats:
        height, width = out.shape
        per = width // 128
        for k in range(per):
            for r in range(0, height, C):
                piece = flat[pl.ds(first + r * per + k, C, stride=per), :]
                out[r : r + C, k * 128 : (k + 1) * 128] = piece.astype(BF)
                out_t[k * 128 : (k + 1) * 128, r : r + C] = piece.T.astype(BF)
    for i in range(ROW_CONV):
        spread[i * 128 : (i + 1) * 128, :] = jnp.broadcast_to(rows[i : i + 1, :], (128, 128)).T
    gain = jnp.concatenate([rows[i : i + 1, :] for i in range(3)], axis=1)
    shift = jnp.concatenate([rows[3 + i : 4 + i, :] for i in range(3)], axis=1)
    live_total = stats[2:3, :]
    average = stats[0:1, :] / live_total
    variance = stats[1:2, :] / live_total - average * average
    inverse = lax.rsqrt(variance + EPS)
    norm[0] = along_sublanes(inverse * gain)
    norm[1] = along_sublanes(shift - average * inverse * gain)
    norm[2] = along_sublanes(inverse)
    norm[3] = along_sublanes(average * inverse)


def mid_kernel(shard,conv_ref,nodes_ref,dyt_ref,mask_ref,stats_ref,rows_ref,gathered_ref,
    out_ref,dfirst_ref,grads_ref,bns_ref,
    flat_ref,bn_ref,vb_ref,wj_ref,wjt_ref,wo_ref,wot_ref,wh_ref,wht_ref,wf_ref,wft_ref,
    gj_ref,go_ref,gh_ref,gf_ref,vs_ref,hb_ref,first_s,second_s,qkv_s,kn_s,vn_s,a_s,o_s,ob_s,inv_s,dob_s,dqkv_s,x_s,acc_s,dx_s):
    step=pl.program_id(0)
    rep=T//128
    @pl.when(step==0)
    def _():
        for r in (gj_ref,go_ref,gh_ref,gf_ref,vs_ref,hb_ref): r[...]=jnp.zeros_like(r)
        prepare(stats_ref,rows_ref,gathered_ref,shard,flat_ref,bn_ref,vb_ref,
            ((ROW_JOINT,wj_ref,wjt_ref),(ROW_OUT,wo_ref,wot_ref),(ROW_HIDDEN,wh_ref,wht_ref),(ROW_FINAL,wf_ref,wft_ref)))
    def col(i,n=C):
        v=vb_ref[pl.ds(i*C,n),:]
        return jnp.concatenate([v]*rep,axis=1) if rep>1 else v
    def fold(x):
        r=x[:,:128]
        for k in range(1,rep): r=r+x[:,128*k:128*(k+1)]
        return r
    def wide(v): return jnp.concatenate([v]*rep,axis=1)
    firstT=nodes_ref[...].astype(F32)+(conv_ref[...]*wide(bn_ref[0])+wide(bn_ref[1]))
    first_s[...]=firstT
    def ln(x):
        m=jnp.mean(x,axis=0,keepdims=True); c=x-m
        rs=lax.rsqrt(jnp.mean(c*c,axis=0,keepdims=True)+EPS)
        return c*rs, rs
    xh1,rs1=ln(firstT)
    x1=(xh1*col(2)+col(3)).astype(BF)
    x_s[0]=x1
    scale=HD**-0.5
    c2=scale*1.4426950408889634
    live_row=jnp.concatenate([mask_ref[b].astype(F32) for b in range(rep)],axis=1)
    q=(nn(wjt_ref[0:C,:],x1)+col(4))*c2
    qkv_s[0:C,:]=q.astype(BF)
    k=nn(wjt_ref[C:2*C,:],x1)*live_row
    qkv_s[C:2*C,:]=k.astype(BF)
    kn_s[...]=k.T.astype(BF)
    v=nn(wjt_ref[2*C:,:],x1)+col(5)
    qkv_s[2*C:,:]=v.astype(BF)
    vn_s[...]=v.T.astype(BF)
    pi=lax.broadcasted_iota(jnp.int32,(BLK,BLK),0); qi=lax.broadcasted_iota(jnp.int32,(BLK,BLK),1)
    wq=jnp.where(pi<4,jnp.where((qi&3)==pi,0.0,-1e30),jnp.where(pi==4,-1e9*1.4426950408889634,0.0)).astype(BF)
    wq=jnp.concatenate([wq,wq],axis=1)
    wps=[]
    for b in range(rep):
        lv=jnp.broadcast_to(mask_ref[b].astype(F32),(BLK,BLK)).T
        wps.append(jnp.where(qi<4,jnp.where((pi&3)==qi,1.0,0.0),jnp.where(qi==4,1.0-lv,0.0)).astype(BF))
    z=jnp.zeros((HD,BLK),BF)
    def ex(part,i):
        return jnp.concatenate([part if t==i else z for t in range(4)],axis=0)
    tasks=[(b,g,hp*2) for b in range(rep) for g in range(3) for hp in range(2)]
    S={};A={}
    def f_s(t):
        b,g,h0=t; cs=slice(b*BLK,(b+1)*BLK)
        qs=[ex(qkv_s[g*128+i*32:g*128+(i+1)*32,cs],i) for i in (h0,h0+1)]
        S[t]=nn(jnp.concatenate([kn_s[cs,g*128:(g+1)*128],wps[b]],axis=1),jnp.concatenate([jnp.concatenate(qs,axis=1),wq],axis=0))
    def f_a(t):
        b,g,h0=t; cs=slice(b*BLK,(b+1)*BLK)
        s=S.pop(t)
        m=jnp.max(s,axis=0,keepdims=True)
        e=jnp.exp2(s-m)
        inv=1.0/jnp.sum(e,axis=0,keepdims=True)
        a=e.astype(BF)
        for i in range(2):
            a_s[g*4+h0+i,:,cs]=a[:,i*128:(i+1)*128]
            inv_s[g*4+h0+i:g*4+h0+i+1,cs]=inv[:,i*128:(i+1)*128]
        A[t]=(a,inv)
    def f_o(t):
        b,g,h0=t; cs=slice(b*BLK,(b+1)*BLK)
        a,inv=A.pop(t)
        for i in range(2):
            h=g*4+h0+i
            o_s[h*32:(h+1)*32,cs]=nn(qkv_s[2*C+h*32:2*C+(h+1)*32,cs],a[:,i*128:(i+1)*128])*inv[:,i*128:(i+1)*128]
    skew([f_s,f_a,f_o],tasks)
    ob=o_s[...].astype(BF)
    ob_s[...]=ob
    secondT=first_s[...]+(nn(wot_ref[...],ob)+col(6))
    second_s[...]=secondT
    xh2,rs2=ln(secondT)
    x2=(xh2*col(7)+col(8)).astype(BF)
    x_s[1]=x2
    dyTb=dyt_ref[...]
    FC=512
    c0=0.7978845608028654; c1=0.044715
    HH={};PP={}
    def g_h(f):
        fs=slice(f*FC,(f+1)*FC)
        HH[f]=(nn(wht_ref[fs,:],x2),nn(wf_ref[fs,:],dyTb))
    def g_g(f):
        fs=slice(f*FC,(f+1)*FC)
        hb=vb_ref[9*C+f*FC:9*C+(f+1)*FC,:]
        hb=jnp.concatenate([hb]*rep,axis=1)
        h,da=HH.pop(f)
        h=h+hb
        h2=h*h
        t=jnp.tanh(h*(c0+(c0*c1)*h2))
        p=0.5+0.5*t
        act=(h*p).astype(BF)
        dg=p*(1.0+h*(1.0-p)*(2*c0+(6*c0*c1)*h2))
        dpb=(da*dg).astype(BF)
        hb_ref[fs,:]+=fold(dpb.astype(F32))
        PP[f]=(act,dpb)
    def g_o(f):
        fs=slice(f*FC,(f+1)*FC)
        act,dpb=PP.pop(f)
        o=nn(wft_ref[:,fs],act)
        d=nn(wh_ref[:,fs],dpb)
        if f==0:
            acc_s[...]=o; dx_s[...]=d
        else:
            acc_s[...]+=o; dx_s[...]+=d
        gf_ref[fs,:]+=nt(act,dyTb)
        gh_ref[:,fs]+=nt(x2,dpb)
    skew([g_h,g_g,g_o],list(range(F//FC)))
    outT=second_s[...]+(acc_s[...]+col(15-2))
    out_ref[...]=outT.T.astype(BF)
    def ln_back(x,dx,gain,vi):
        xh,rs=ln(x)
        vs_ref[vi]+=fold(dx*xh)
        vs_ref[vi+1]+=fold(dx)
        dh=dx*gain
        m1=jnp.mean(dh,axis=0,keepdims=True)
        m2=jnp.mean(dh*xh,axis=0,keepdims=True)
        return rs*(dh-m1-xh*m2)
    dsec=dyt_ref[...].astype(F32)+ln_back(second_s[...],dx_s[...],col(7),0)
    second_s[...]=dsec
    dbr=dsec.astype(BF)
    vs_ref[2]+=fold(dbr.astype(F32))
    go_ref[...]+=nt(ob_s[...],dbr)
    dat=nn(wo_ref[...],dbr)
    for h in range(HEADS):
        hs=slice(h*32,(h+1)*32)
        dob_s[hs,:]=(dat[hs,:]*inv_s[h:h+1,:]).astype(BF)
    D={};G={}
    def b_d(t):
        b,g,h0=t; cs=slice(b*BLK,(b+1)*BLK)
        ds=[ex(dob_s[g*128+i*32:g*128+(i+1)*32,cs],i) for i in (h0,h0+1)]
        D[t]=nn(vn_s[cs,g*128:(g+1)*128],jnp.concatenate(ds,axis=1))
    def b_s(t):
        b,g,h0=t; cs=slice(b*BLK,(b+1)*BLK)
        dA=D.pop(t)
        out=[]
        for i in range(2):
            h=g*4+h0+i; hs=slice(h*32,(h+1)*32)
            delta=jnp.sum(dob_s[hs,cs].astype(F32)*o_s[hs,cs],axis=0,keepdims=True)
            out.append(a_s[h,:,cs]*(dA[:,i*128:(i+1)*128]-delta).astype(BF))
        G[t]=out
    def b_q(t):
        b,g,h0=t; cs=slice(b*BLK,(b+1)*BLK)
        lrow=live_row[:,cs]
        out=G.pop(t)
        for i in range(2):
            h=g*4+h0+i; hs=slice(h*32,(h+1)*32); ds=out[i]
            dqkv_s[h*32:(h+1)*32,cs]=(nn(qkv_s[C+h*32:C+(h+1)*32,cs],ds)*scale).astype(BF)
            dqkv_s[C+h*32:C+(h+1)*32,cs]=(nt(qkv_s[hs,cs],ds)*(lrow*(scale/c2))).astype(BF)
            dqkv_s[2*C+h*32:2*C+(h+1)*32,cs]=nt(dob_s[hs,cs],a_s[h,:,cs]).astype(BF)
    skew([b_d,b_s,b_q],tasks)
    vs_ref[3]+=fold(dqkv_s[0:C,:].astype(F32))
    vs_ref[4]+=fold(dqkv_s[2*C:,:].astype(F32))
    gj_ref[...]+=nt(x_s[0],dqkv_s[...])
    dx1=nn(wj_ref[...],dqkv_s[...])
    dfT=second_s[...]+ln_back(first_s[...],dx1,col(2),5)
    dfirst_ref[...]=dfT.T
    vs_ref[7]+=fold(dfT*(conv_ref[...]*wide(bn_ref[2])-wide(bn_ref[3])))
    vs_ref[8]+=fold(dfT)
    vs_ref[9]+=fold(dyt_ref[...].astype(F32))
    @pl.when(step==pl.num_programs(0)-1)
    def _():
        flat_ref[...]=jnp.zeros_like(flat_ref)
        bns_ref[...]=jnp.concatenate([lane_sums(vs_ref[i]) for i in (7,8,9)]+[jnp.zeros((5,C),F32)],axis=0)
        for vi,row in ((0,21),(1,24),(2,18),(3,12),(4,15),(5,6),(6,9)):
            for i in range(3):
                flat_ref[pl.ds(row+i,1),:]=jnp.sum(vs_ref[vi,i*128:(i+1)*128,:].T,axis=0,keepdims=True)
        for i in range(12):
            flat_ref[pl.ds(27+i,1),:]=jnp.sum(hb_ref[i*128:(i+1)*128,:].T,axis=0,keepdims=True)
        for first,mat in ((ROW_JOINT,gj_ref),(ROW_OUT,go_ref),(ROW_HIDDEN,gh_ref),(ROW_FINAL,gf_ref)):
            rows,cols=mat.shape
            per=cols//128
            for k in range(per):
                for r in range(0,rows,C):
                    flat_ref[pl.ds(first+r*per+k,C,stride=per),:]=mat[r:r+C,k*128:(k+1)*128]
        for i in range(grads_ref.shape[0]*8):
            part=flat_ref[i*shard:(i+1)*shard,:]
            pad=grads_ref.shape[-2]-shard
            grads_ref[i//8,(i//4)%2,(i//2)%2,i%2]=jnp.concatenate([part,jnp.zeros((pad,128),F32)],axis=0).astype(BF)


def middle(conv,nodes,dy,mask3,stats,rows,gathered,shard):
    n=conv.shape[1]
    across=pl.BlockSpec((C,T),lambda i:(0,i))
    down=rows_of(C,T)
    flat_rows=gathered.shape[0]*8*shard
    in_specs=[across,across,across,pl.BlockSpec((T//128,1,128),lambda i:(i,0,0)),whole(*stats.shape),whole(*rows.shape),whole(*gathered.shape)]
    outs=[((n,C),BF,down),((n,C),F32,down),(gathered.shape,BF,whole(*gathered.shape)),((8,C),F32,whole(8,C))]
    mats=[]
    for shape in ((C,3*C),(C,C),(C,F),(F,C)): mats+=[(shape,BF),(shape[::-1],BF)]
    scr=[pltpu.VMEM(s,d) for s,d in [((flat_rows,128),F32),((4,C,128),F32),((ROW_CONV*128,128),F32)]+mats+[((C,3*C),F32),((C,C),F32),((C,F),F32),((F,C),F32),((10,C,128),F32),((F,128),F32),((C,T),F32),((C,T),F32),((3*C,T),BF),((T,C),BF),((T,C),BF),((HEADS,BLK,T),BF),((C,T),F32),((C,T),BF),((16,T),F32),((C,T),BF),((3*C,T),BF),((2,C,T),BF),((C,T),F32),((C,T),F32)]]
    return pl.pallas_call(functools.partial(mid_kernel,shard),grid=(n//T,),in_specs=in_specs,out_specs=[o[2] for o in outs],
      out_shape=[jax.ShapeDtypeStruct(o[0],o[1]) for o in outs],scratch_shapes=scr,
      compiler_params=VMEM)(conv,nodes,dy,mask3,stats,rows,gathered)


def shards(nodes_in, out_grad, neighbours, node_mask, master, first_moment, second_moment):
    n = nodes_in.shape[0]
    count, cores = lax.axis_size(AXES), lax.axis_size("grp")
    shard = master.shape[0] // 128
    mask3 = node_mask.reshape(n // 128, 1, 128)
    near = neighbours.T
    conv_t, conv, nodes_t, dy_t, gathered, first_rows, stats = convolve(
        near, nodes_in, out_grad, mask3, master.reshape(shard, 128), count, cores
    )
    output, delta_first, grads, norm_sums = middle(conv_t, nodes_t, dy_t, mask3, stats, first_rows, gathered, shard)
    node_grad, shard_delta, bias_total = convolve_back(
        near, delta_first, conv, nodes_in, mask3, norm_sums, stats, first_rows, grads, shard, count, cores
    )
    shard_delta = shard_delta.reshape(-1)
    position = lax.axis_index(AXES) * master.shape[0] + lax.iota(jnp.int32, master.shape[0])
    step_rate = jnp.where(position < 10 * C + F, 0.2, 0.03)
    new_first = 0.9 * first_moment + 0.1 * shard_delta
    new_second = 0.95 * second_moment + 0.05 * shard_delta * shard_delta
    first_hat = new_first / (1.0 - 0.9**STEP)
    second_hat = new_second / (1.0 - 0.95**STEP)
    new_master = master - step_rate * (first_hat / (jnp.sqrt(second_hat) + 1e-08) + 0.01 * master)
    return (
        output,
        node_grad,
        new_master,
        new_first,
        new_second,
        new_master.astype(BF),
        bias_total.reshape(-1),
    )


def solution(mesh):
    rows, flat = P(AXES, None), P(AXES)
    return jax.shard_map(
        shards,
        mesh=mesh,
        in_specs=(rows, rows, rows, flat, flat, flat, flat),
        out_specs=(rows, rows, flat, flat, flat, flat, P()),
        check_vma=False,
    )
```

```python
import functools

import jax
import jax.numpy as jnp
from jax import lax
from jax.experimental import pallas as pl
from jax.experimental.pallas import tpu as pltpu
from jax.sharding import PartitionSpec as P

C = 384
HEADS = 12
HD = 32
F = 1536
HALO = 64
STEP = 5
EPS = 1e-5
AXES = ("rows", "grp")
F32 = jnp.float32
BF = jnp.bfloat16

BLK = 128
T = 512
TB = 512
ROW_CONV = (10 * C + F) // 128
ROW_JOINT = ROW_CONV + 27 * C // 128
ROW_OUT = ROW_JOINT + C * 3 * C // 128
ROW_HIDDEN = ROW_OUT + C * C // 128
ROW_FINAL = ROW_HIDDEN + C * F // 128
ROW_END = ROW_FINAL + C * F // 128
VMEM = pltpu.CompilerParams(vmem_limit_bytes=60 * 1024 * 1024)


def nn(a, b):
    return jnp.dot(a, b, preferred_element_type=F32)


def nt(a, b):
    return lax.dot_general(a, b, (((1,), (1,)), ((), ())), preferred_element_type=F32)


def whole(*shape):
    return pl.BlockSpec(shape, lambda i: (0,) * len(shape), pipeline_mode=pl.Buffered(1))


def skew(stages, tasks):
    for i in range(len(tasks) + len(stages) - 1):
        for k, stage in enumerate(stages):
            if 0 <= i - k < len(tasks):
                stage(tasks[i - k])


def along_sublanes(row):
    parts = [row[:, i : i + 128] for i in range(0, row.shape[1], 128)]
    return jnp.concatenate([jnp.broadcast_to(p, (128, 128)).T for p in parts], axis=0)


def lane_sums(value):
    parts = [value[i : i + 128, :].T for i in range(0, value.shape[0], 128)]
    return jnp.concatenate([jnp.sum(p, axis=0, keepdims=True) for p in parts], axis=1)


def rows_of(width, size):
    return pl.BlockSpec((size, width), lambda i: (i, 0))


MESH = pl.DeviceIdType.MESH


def CUTS_GATHER(nh):
    return [1] * nh + [3, 7]


def round_up(value, step):
    return -(-value // step) * step


def my_place():
    return lax.axis_index("rows") * lax.axis_size("grp") + lax.axis_index("grp")


def device(place, cores):
    return (place // cores, place % cores)


def stages_of(count):
    out, stride = [], 1
    while stride < count:
        size = min(8, count // stride)
        out.append((stride, size))
        stride *= size
    return out


def others(me, stride, size):
    mine = (me // stride) % size
    return mine, [(k, me + ((mine + k) % size - mine) * stride) for k in range(1, size)]


def greet(partners, cores):
    barrier = pltpu.get_barrier_semaphore()
    for place in partners:
        pl.semaphore_signal(barrier, inc=1, device_id=device(place, cores), device_id_type=MESH)
    pl.semaphore_wait(barrier, len(partners))


def send(source, target, send_sem, recv_sem, place, cores):
    return pltpu.make_async_remote_copy(
        src_ref=source,
        dst_ref=target,
        send_sem=send_sem,
        recv_sem=recv_sem,
        device_id=device(place, cores),
        device_id_type=MESH,
    )


def all_sum(value, me, count, cores, slots, send_sems, recv_sems, beside=None):
    for s, (stride, size) in enumerate(stages_of(count)):
        mine, partners = others(me, stride, size)
        slots[s, mine] = value
        copies = [
            send(slots.at[s, mine], slots.at[s, mine], send_sems.at[s, k], recv_sems.at[s, k], place, cores)
            for k, place in partners
        ]
        for copy in copies:
            copy.start()
        if beside is not None:
            beside(s)
        for copy in copies:
            copy.wait()
        value = slots[s, 0]
        for i in range(1, size):
            value = value + slots[s, i]
    return value


def sum_scratch(count, rows, width):
    n = len(stages_of(count))
    return [
        pltpu.VMEM((n, 8, rows, width), F32),
        pltpu.SemaphoreType.DMA((n, 8)),
        pltpu.SemaphoreType.DMA((n, 8)),
    ]


def conv_kernel(count, cores, owners, near_ref, nodes_ref, dy_ref, mask_ref, master_ref,
                convt_ref, conv_ref, nodest_ref, dyt_ref, gathered_ref, first_ref, stats_ref,
                ext, extt, dy_s, early, weight, sums, own_s, local_sem, halo_send, halo_recv, e_send, e_recv, g_send,
                g_recv, slots, s_send, s_recv):
    step = pl.program_id(0)
    steps = pl.num_programs(0)
    block = (step + 1) % steps
    n = nodes_ref.shape[0]
    shard = master_ref.shape[0]
    padded = gathered_ref.shape[-2]
    half = padded // 2
    e_rows = early.shape[1]
    me = my_place()
    low, high = me % 8, me // 8
    y, x, g = low // 4, (low // 2) % 2, low % 2
    highs = stages_of(count // 8)
    left, right = (me + count - 1) % count, (me + 1) % count

    local = pltpu.make_async_copy(nodes_ref, ext.at[pl.ds(HALO, n)], local_sem.at[0])
    keep = pltpu.make_async_copy(own_s, gathered_ref.at[high, y, x, g], local_sem.at[1])
    local_dy = pltpu.make_async_copy(dy_ref, dy_s, local_sem.at[2])

    def turn_dy(k):
        at = pl.ds(pl.multiple_of(k * BLK, BLK), BLK)
        dyt_ref[:, at] = dy_s[at, :].T
        return 0

    def turn(k):
        at = pl.ds(pl.multiple_of(k * BLK, BLK), BLK)
        extt[:, at] = ext[at, :].T
        return 0
    to_left = send(nodes_ref.at[pl.ds(0, HALO)], ext.at[pl.ds(HALO + n, HALO)], halo_send.at[0], halo_recv.at[0], left, cores)
    to_right = send(nodes_ref.at[pl.ds(n - HALO, HALO)], ext.at[pl.ds(0, HALO)], halo_send.at[1], halo_recv.at[1], right, cores)

    def high_copies(s):
        stride, size = highs[s]
        mine, partners = others(high, stride, size)
        own = gathered_ref.at[pl.ds(high // stride * stride, stride), y, x, g]
        return [
            send(own, own, g_send.at[s, k], g_recv.at[s, k], place * 8 + low, cores)
            for k, place in partners
        ]

    nh = len(highs)
    y_place, x_place, g_place = me + 4 - 8 * y, me + 2 - 4 * x, me + 1 - 2 * g

    def quad_copies(t):
        top, bottom = pl.ds(0, half), pl.ds(half, half)
        if t == 0:
            a = gathered_ref.at[:, y, x, g, top]
            b = gathered_ref.at[:, y, x, g, bottom]
            to_a, to_b = y_place, x_place
        else:
            a = gathered_ref.at[:, :, x, g, top]
            b = gathered_ref.at[:, y, :, g, bottom]
            to_a, to_b = x_place, y_place
        s = nh + t
        return [send(a, a, g_send.at[s, 0], g_recv.at[s, 0], to_a, cores), send(b, b, g_send.at[s, 1], g_recv.at[s, 1], to_b, cores)]

    def core_copies():
        own = gathered_ref.at[:, :, :, g]
        return [send(own, own, g_send.at[nh + 2, 0], g_recv.at[nh + 2, 0], g_place, cores)]

    plan = [functools.partial(high_copies, s) for s in range(nh)]
    plan += [functools.partial(quad_copies, 0), functools.partial(quad_copies, 1), core_copies]
    cuts = CUTS_GATHER(nh)

    @pl.when(step == 0)
    def _():
        local.start()
        local_dy.start()
        sums[...] = jnp.zeros_like(sums)
        own = jnp.concatenate([master_ref[...], jnp.zeros((padded - shard, 128), F32)], axis=0).astype(BF)
        own_s[...] = own
        keep.start()
        wide = [h for h in range(1, count // 8)]
        partners = [left, right]
        partners += [(high + h) % (count // 8) * 8 + low for h in wide]
        partners += [place for _, place in others(me, 1, 8)[1]]
        greet(partners, cores)
        early_copies = []
        for o in range(owners):
            up = [send(early.at[o], early.at[o], e_send.at[o, 8 + h], e_recv.at[o, 0], h * 8 + o, cores) for h in wide]
            out = [
                send(early.at[o], early.at[o], e_send.at[o, k], e_recv.at[o, 1], me + k - o, cores)
                for k in range(8) if k != o
            ]
            early_copies.append((up, out))

            @pl.when(low == o)
            def _(o=o, up=up, out=out):
                @pl.when(high == 0)
                def _():
                    early[o] = own[:e_rows]
                    for copy in up:
                        copy.start()
                @pl.when(high > 0)
                def _():
                    send(early.at[o], early.at[o], e_send.at[o, 8], e_recv.at[o, 0], left, cores).wait_recv()
                for copy in out:
                    copy.start()
        to_left.start()
        to_right.start()
        keep.wait()
        for copy in plan[0]():
            copy.start()
        local.wait()
        lax.fori_loop(1, n // BLK, lambda k, _: turn(k), 0)
        for o in range(owners):
            @pl.when(low != o)
            def _():
                send(early.at[o], early.at[o], e_send.at[o, 8], e_recv.at[o, 1], left, cores).wait_recv()
        for o in range(owners):
            rows = min(shard, e_rows)
            first_ref[pl.ds(o * shard, rows), :] = early[o].astype(F32)[:rows]
        for j in range(27):
            row = jnp.concatenate([first_ref[ROW_CONV + 3 * j + i : ROW_CONV + 3 * j + i + 1, :] for i in range(3)], axis=1)
            weight[j] = along_sublanes(row)
        for o, (up, out) in enumerate(early_copies):
            @pl.when(low == o)
            def _(up=up, out=out):
                @pl.when(high == 0)
                def _():
                    for copy in up:
                        copy.wait_send()
                for copy in out:
                    copy.wait_send()

    for s in range(len(plan) - 1):
        @pl.when(step == cuts[s])
        def _(s=s):
            for copy in plan[s]():
                copy.wait()
            for copy in plan[s + 1]():
                copy.start()

    @pl.when(step == steps - 2)
    def _():
        to_left.wait()
        to_right.wait()
        turn(0)
        turn(n // BLK)

    sub = lax.broadcasted_iota(jnp.int32, (2 * BLK, BLK), 0).astype(F32).astype(BF)
    one, zero = jnp.ones((), BF), jnp.zeros((), BF)
    pairs = [(j, j + 1) for j in range(0, 12, 2)] + [(12, 14)] + [(j, j + 1) for j in range(15, 27, 2)]
    at = pl.multiple_of(block * T, T)
    lane = lax.broadcasted_iota(jnp.int32, (27, BLK), 1)
    places, totals, picks, comes = {}, {}, {}, {}
    for b in range(T // BLK):
        near = near_ref[:, b * BLK : (b + 1) * BLK]
        places[b] = jnp.where(near < 0, -1, near + lane).astype(F32).astype(BF)

    def pick(task):
        b, q = task
        if q == 0:
            center = ext[pl.ds(at + b * BLK + HALO, BLK), :].astype(F32).T
            nodest_ref[:, b * BLK : (b + 1) * BLK] = center.astype(BF)
            totals[b] = center * weight[13]
        picks[task] = jnp.concatenate(
            [jnp.where(places[b][j : j + 1, :] == sub, one, zero) for j in pairs[q]], axis=1
        )

    def multiply(task):
        b, q = task
        comes[task] = nn(extt[:, pl.ds(at + b * BLK, 2 * BLK)], picks.pop(task))

    def add(task):
        b, q = task
        come = comes.pop(task)
        totals[b] = totals[b] + (come[:, :BLK] * weight[pairs[q][0]] + come[:, BLK:] * weight[pairs[q][1]])
        if q == len(pairs) - 1:
            total = totals.pop(b)
            convt_ref[:, b * BLK : (b + 1) * BLK] = total
            conv_ref[b * BLK : (b + 1) * BLK, :] = total.T.astype(BF)
            live = mask_ref[b].astype(F32)
            kept = total * live
            sums[0] += kept
            sums[1] += kept * total
            sums[2, 0:1] += live

    skew([pick, multiply, add], [(b, q) for b in range(T // BLK) for q in range(len(pairs))])

    @pl.when(step == steps - 1)
    def _():
        rows = [lane_sums(sums[i]) for i in range(2)]
        rows += [jnp.broadcast_to(jnp.sum(sums[2, 0:1], axis=1, keepdims=True), (1, C))]
        rows = jnp.concatenate(rows + [jnp.zeros((5, C), F32)], axis=0)
        local_dy.wait()
        cut = len(stages_of(count))

        def beside(s):
            lax.fori_loop(n // BLK * s // cut, n // BLK * (s + 1) // cut, lambda k, _: turn_dy(k), 0)

        stats_ref[...] = all_sum(rows, me, count, cores, slots, s_send, s_recv, beside)
        for copy in plan[-1]():
            copy.wait()


def convolve(near, nodes, dy, mask3, master, count, cores):
    n = nodes.shape[0]
    steps = n // T
    shard = master.shape[0]
    padded = round_up(shard, 32)
    owners = -(-ROW_JOINT // shard)
    e_rows = min(padded, round_up(ROW_JOINT, 16))
    down = pl.BlockSpec((T, C), lambda i: ((i + 1) % steps, 0))
    across = pl.BlockSpec((C, T), lambda i: (0, (i + 1) % steps))
    anywhere = pl.BlockSpec(memory_space=pl.ANY)
    stages = len(stages_of(count // 8)) + 3
    first_rows = round_up((owners - 1) * shard + e_rows, 8)
    return pl.pallas_call(
        functools.partial(conv_kernel, count, cores, owners),
        grid=(steps,),
        in_specs=[
            pl.BlockSpec((27, T), lambda i: (0, (i + 1) % steps)),
            anywhere,
            anywhere,
            pl.BlockSpec((T // BLK, 1, 128), lambda i: ((i + 1) % steps, 0, 0)),
            whole(shard, 128),
        ],
        out_specs=[across, down, across, whole(C, n), anywhere, whole(first_rows, 128), whole(8, C)],
        out_shape=[
            jax.ShapeDtypeStruct((C, n), F32),
            jax.ShapeDtypeStruct((n, C), BF),
            jax.ShapeDtypeStruct((C, n), BF),
            jax.ShapeDtypeStruct((C, n), BF),
            jax.ShapeDtypeStruct((count // 8, 2, 2, 2, padded, 128), BF),
            jax.ShapeDtypeStruct((first_rows, 128), F32),
            jax.ShapeDtypeStruct((8, C), F32),
        ],
        scratch_shapes=[
            pltpu.VMEM((n + 2 * HALO, C), BF),
            pltpu.VMEM((C, n + 2 * HALO), BF),
            pltpu.VMEM((n, C), BF),
            pltpu.VMEM((owners, e_rows, 128), BF),
            pltpu.VMEM((27, C, 128), F32),
            pltpu.VMEM((3, C, 128), F32),
            pltpu.VMEM((padded, 128), BF),
            pltpu.SemaphoreType.DMA((3,)),
            pltpu.SemaphoreType.DMA((2,)),
            pltpu.SemaphoreType.DMA((2,)),
            pltpu.SemaphoreType.DMA((owners, 8 + count // 8)),
            pltpu.SemaphoreType.DMA((owners, 2)),
            pltpu.SemaphoreType.DMA((stages, 8)),
            pltpu.SemaphoreType.DMA((stages, 8)),
        ]
        + sum_scratch(count, 8, C),
        compiler_params=pltpu.CompilerParams(
            vmem_limit_bytes=60 * 1024 * 1024, collective_id=0, has_side_effects=True
        ),
    )(near, nodes, dy, mask3, master)


def conv_back_kernel(count, cores, owners, near_hbm, first_hbm, conv_hbm, x_ref, mask_ref, sums_ref, stats_ref,
                     rows_ref, grads_ref,
                     grad_ref, total_s, bias_out,
                     near, ext, delta, conv, weight, dw, kept, r1, r2, r3, r4, local_sem, halo_send, halo_recv, g_send,
                     g_recv, slots, s_send, s_recv, w_own, w_slots, w_high, w_sem, w_recv, w_recv_high, early_s, factors, w_sum):
    step = pl.program_id(0)
    steps = pl.num_programs(0)
    block = (step + 1) % steps
    n = first_hbm.shape[0]
    shard = total_s.shape[0]
    padded = grads_ref.shape[-2]
    half = padded // 2
    me = my_place()
    low, high = me % 8, me // 8
    y, x, g = low // 4, (low // 2) % 2, low % 2
    highs = stages_of(count // 8)[::-1]
    nh = len(highs)
    left, right = (me + count - 1) % count, (me + 1) % count
    y_place, x_place, g_place = me + 4 - 8 * y, me + 2 - 4 * x, me + 1 - 2 * g
    top, bottom = pl.ds(0, half), pl.ds(half, half)

    locals_ = [
        pltpu.make_async_copy(first_hbm, delta, local_sem.at[0]),
        pltpu.make_async_copy(conv_hbm, conv, local_sem.at[1]),
        pltpu.make_async_copy(near_hbm, near.at[:, pl.ds(BLK, n)], local_sem.at[2]),
        pltpu.make_async_copy(grads_ref.at[:, :, :, g], kept, local_sem.at[3]),
    ]
    near_halo = [
        send(near_hbm.at[:, pl.ds(0, BLK)], near.at[:, pl.ds(BLK + n, BLK)], halo_send.at[0], halo_recv.at[0], left, cores),
        send(near_hbm.at[:, pl.ds(n - BLK, BLK)], near.at[:, pl.ds(0, BLK)], halo_send.at[1], halo_recv.at[1], right, cores),
    ]
    delta_halo = [
        send(ext.at[pl.ds(HALO, HALO)], ext.at[pl.ds(HALO + n, HALO)], halo_send.at[2], halo_recv.at[2], left, cores),
        send(ext.at[pl.ds(n, HALO)], ext.at[pl.ds(0, HALO)], halo_send.at[3], halo_recv.at[3], right, cores),
    ]

    blocks, per = n // BLK, TB // BLK

    def make_rows(i):
        at = pl.ds(pl.multiple_of(i * BLK, BLK), BLK)
        live = jnp.broadcast_to(mask_ref[i].astype(F32), (BLK, BLK)).T
        live = jnp.concatenate([live] * 3, axis=1)
        value = delta[at, :] * factors[0:1, :] + live * (factors[1:2, :] + factors[2:3, :] * conv[at, :].astype(F32))
        ext[pl.ds(pl.multiple_of(i * BLK + HALO, HALO), BLK), :] = value.astype(BF)
        return 0

    def core_copies():
        return [send(grads_ref.at[:, :, :, 1 - g], r1, g_send.at[0, 0], g_recv.at[0, 0], g_place, cores)]

    def core_add():
        def body(i, _):
            kept[i // 4, (i // 2) % 2, i % 2] = (
                kept[i // 4, (i // 2) % 2, i % 2].astype(F32) + r1[i // 4, (i // 2) % 2, i % 2].astype(F32)
            ).astype(BF)
            return 0
        lax.fori_loop(0, count // 2, body, 0)

    def quad_copies_0():
        return [
            send(kept.at[:, :, 1 - x, top], r2.at[0], g_send.at[1, 0], g_recv.at[1, 0], x_place, cores),
            send(kept.at[:, 1 - y, :, bottom], r2.at[1], g_send.at[1, 1], g_recv.at[1, 1], y_place, cores),
        ]

    def quad_add_0():
        def body(i, _):
            h, w = i // 2, i % 2
            kept[h, w, x, top] = (
                kept[h, w, x, top].astype(F32) + r2[0, h, w].astype(F32)
            ).astype(BF)
            kept[h, y, w, bottom] = (
                kept[h, y, w, bottom].astype(F32) + r2[1, h, w].astype(F32)
            ).astype(BF)
            return 0
        lax.fori_loop(0, count // 4, body, 0)

    def quad_copies_1():
        return [
            send(kept.at[:, 1 - y, x, top], r3.at[0], g_send.at[2, 0], g_recv.at[2, 0], y_place, cores),
            send(kept.at[:, y, 1 - x, bottom], r3.at[1], g_send.at[2, 1], g_recv.at[2, 1], x_place, cores),
        ]

    def quad_add_1():
        def body(h, _):
            kept[h, y, x, top] = (
                kept[h, y, x, top].astype(F32) + r3[0, h].astype(F32)
            ).astype(BF)
            kept[h, y, x, bottom] = (
                kept[h, y, x, bottom].astype(F32) + r3[1, h].astype(F32)
            ).astype(BF)
            return 0
        lax.fori_loop(0, count // 8, body, 0)

    bases = []
    base = 0
    for stride, size in highs:
        bases.append(base)
        base += (size - 1) * stride

    def high_copies(s):
        stride, size = highs[s]
        mine, partners = others(high, stride, size)
        out = []
        for k, place in partners:
            source = kept.at[pl.ds(place // stride * stride, stride), y, x]
            target = r4.at[pl.ds(bases[s] + (k - 1) * stride, stride)]
            out.append(send(source, target, g_send.at[3 + s, k], g_recv.at[3 + s, k], place * 8 + low, cores))
        return out

    def high_add(s):
        stride, size = highs[s]
        start = high // stride * stride
        def body(i, _):
            value = kept[start + i, y, x].astype(F32)
            for k in range(size - 1):
                value = value + r4[bases[s] + k * stride + i].astype(F32)
            if s == nh - 1:
                total_s[...] = value[:shard]
            else:
                kept[start + i, y, x] = value.astype(BF)
            return 0
        lax.fori_loop(0, stride, body, 0)

    plan = [(core_copies, core_add), (quad_copies_0, quad_add_0), (quad_copies_1, quad_add_1)]
    plan += [(functools.partial(high_copies, s), functools.partial(high_add, s)) for s in range(nh)]
    cuts = CUTS_SCATTER(nh)

    @pl.when(step == 0)
    def _():
        for copy in locals_:
            copy.start()
        dw[...] = jnp.zeros_like(dw)
        partners = [left, right]
        partners += [(high + h) % (count // 8) * 8 + low for h in range(1, count // 8)]
        partners += [place for _, place in others(me, 1, 8)[1]]
        greet(partners, cores)
        def beside(s):
            if s == 0:
                for copy in plan[0][0]() + near_halo:
                    copy.start()
        total = all_sum(sums_ref[...], me, count, cores, slots, s_send, s_recv, beside)
        gain_total, shift_total = total[0:1], total[1:2]
        bias_out[...] = jnp.concatenate([total[2:3, i * 128 : (i + 1) * 128] for i in range(3)], axis=0)
        early_s[...] = jnp.zeros_like(early_s)
        for i in range(3):
            early_s[i : i + 1, :] = gain_total[:, i * 128 : (i + 1) * 128]
            early_s[3 + i : 4 + i, :] = shift_total[:, i * 128 : (i + 1) * 128]
            early_s[ROW_CONV - 3 + i : ROW_CONV - 2 + i, :] = total[2:3, i * 128 : (i + 1) * 128]
        for k in range(3):
            weight[:, k * 128 : (k + 1) * 128] = rows_ref[pl.ds(ROW_CONV + k, 27, stride=3), :]
        gain = jnp.concatenate([rows_ref[i : i + 1, :] for i in range(3)], axis=1)
        live_total = stats_ref[2:3]
        average = stats_ref[0:1] / live_total
        variance = stats_ref[1:2] / live_total - average * average
        inverse = lax.rsqrt(variance + EPS)
        delta_variance = -0.5 * inverse * inverse * inverse * (gain * gain_total / inverse)
        delta_average = -gain * shift_total * inverse - 2.0 * average * delta_variance
        a = gain * inverse
        b = delta_average / live_total
        c = 2.0 * delta_variance / live_total
        for copy in locals_:
            copy.wait()

        factors[0:1, :] = a
        factors[1:2, :] = b
        factors[2:3, :] = c
        make_rows(0)
        make_rows(blocks - 1)
        lax.fori_loop(per - 1, 2 * per + 1, lambda k, _: make_rows(k), 0)
        for copy in delta_halo:
            copy.start()

    for s in range(len(plan)):
        @pl.when(step == cuts[s])
        def _(s=s):
            for copy in plan[s][0]():
                copy.wait()
            plan[s][1]()
            if s + 1 < len(plan):
                for copy in plan[s + 1][0]():
                    copy.start()

    @pl.when(step == steps - 2)
    def _():
        for copy in near_halo + delta_halo:
            copy.wait()

    start = pl.multiple_of(block * TB, TB)
    target = lax.broadcasted_iota(jnp.int32, (BLK, 2 * BLK), 0).astype(F32).astype(BF)
    one, zero = jnp.ones((), BF), jnp.zeros((), BF)
    lane = lax.broadcasted_iota(jnp.int32, (27, 2 * BLK), 1) - BLK
    places, totals, picks, comes, xs = {}, {}, {}, {}, {}
    for b in range(TB // BLK):
        near_w = near[:, pl.ds(start + b * BLK, 3 * BLK)][:, HALO : HALO + 2 * BLK]
        places[b] = jnp.where(near_w < 0, -1, near_w + lane).astype(F32).astype(BF)

    def pick(task):
        b, q = task
        picks[task] = jnp.concatenate(
            [jnp.where(places[b][j : j + 1, :] == target, one, zero) for j in range(3 * q, 3 * q + 3)], axis=0
        )

    def multiply(task):
        b, q = task
        comes[task] = nn(picks.pop(task), ext[pl.ds(start + b * BLK, 2 * BLK), :])

    def add(task):
        b, q = task
        come = comes.pop(task)
        if q == 0:
            xs[b] = x_ref[b * BLK : (b + 1) * BLK, :].astype(F32)
            totals[b] = delta[pl.ds(start + b * BLK, BLK), :]
        for i in range(3):
            j, part = 3 * q + i, come[i * BLK : (i + 1) * BLK]
            totals[b] = totals[b] + part * weight[j : j + 1, :]
            dw[j] += jnp.sum((part * xs[b]).reshape(BLK // 8, 8, C), axis=0)
        if q == 8:
            grad_ref[b * BLK : (b + 1) * BLK, :] = totals.pop(b)

    skew([pick, multiply, add], [(b, q) for b in range(TB // BLK) for q in range(9)])

    for k in range(per):
        i = ((block + 1) * per + 1 + k) % blocks
        make_rows(jnp.where((i == 0) | (i == blocks - 1), blocks - 2, i))

    @pl.when(step == steps - 1)
    def _():
        mine = jnp.concatenate([jnp.sum(dw[...], axis=1), jnp.zeros((5, C), F32)], axis=0)
        w_own[...] = mine.astype(BF)
        to_first = send(w_own, w_slots.at[low], w_sem.at[0], w_recv.at[low], me - low, cores)

        @pl.when(low != 0)
        def _():
            to_first.start()
            to_first.wait_send()

        @pl.when(low == 0)
        def _():
            for k in range(1, 8):
                send(w_own, w_slots.at[k], w_sem.at[0], w_recv.at[k], me + k, cores).wait_recv()
            mine_8 = mine + sum(w_slots[k].astype(F32) for k in range(1, 8))
            w_own[...] = mine_8.astype(BF)

            @pl.when(high != 0)
            def _():
                up = send(w_own, w_high.at[high], w_sem.at[0], w_recv_high.at[high], 0, cores)
                up.start()
                up.wait_send()

            @pl.when(high == 0)
            def _():
                for h in range(1, count // 8):
                    send(w_own, w_high.at[h], w_sem.at[0], w_recv_high.at[h], h * 8, cores).wait_recv()
                mine_all = mine_8 + sum(w_high[h].astype(F32) for h in range(1, count // 8))
                w_own[...] = mine_all.astype(BF)
                w_sum[...] = mine_all
                out = [send(w_own, w_high.at[0], w_sem.at[o], w_recv_high.at[0], o, cores) for o in range(1, owners)]
                for copy in out:
                    copy.start()
                for copy in out:
                    copy.wait_send()

        for o in range(owners):
            @pl.when(me == o)
            def _(o=o):
                if o == 0:
                    sums = w_sum[...]
                else:
                    send(w_own, w_high.at[0], w_sem.at[0], w_recv_high.at[0], 0, cores).wait_recv()
                    sums = w_high[0].astype(F32)
                for k in range(3):
                    early_s[pl.ds(ROW_CONV + k, 27, stride=3), :] = sums[:27, k * 128 : (k + 1) * 128]
                rows = min(shard, early_s.shape[0] - o * shard)
                total_s[0:rows, :] += early_s[o * shard : o * shard + rows, :]


def CUTS_SCATTER(nh):
    return [1, 3, 4] + [4 + 3 * (s + 1) // nh for s in range(nh)]


def convolve_back(near, delta, conv, nodes, mask3, sums, stats, rows, grads, shard, count, cores):
    n = nodes.shape[0]
    steps = n // TB
    padded = grads.shape[-2]
    highs = count // 8
    owners = -(-ROW_JOINT // shard)
    turned = pl.BlockSpec((TB, C), lambda i: ((i + 1) % steps, 0))
    anywhere = pl.BlockSpec(memory_space=pl.ANY)
    r4_rows = sum((size - 1) * stride for stride, size in stages_of(highs))
    return pl.pallas_call(
        functools.partial(conv_back_kernel, count, cores, owners),
        grid=(steps,),
        in_specs=[
            anywhere,
            anywhere,
            anywhere,
            turned,
            whole(*mask3.shape),
            whole(*sums.shape),
            whole(*stats.shape),
            whole(*rows.shape),
            anywhere,
        ],
        out_specs=[turned, whole(shard, 128), whole(3, 128)],
        out_shape=[
            jax.ShapeDtypeStruct((n, C), F32),
            jax.ShapeDtypeStruct((shard, 128), F32),
            jax.ShapeDtypeStruct((3, 128), F32),
        ],
        scratch_shapes=[
            pltpu.VMEM((27, n + 2 * BLK), jnp.int32),
            pltpu.VMEM((n + 2 * HALO, C), BF),
            pltpu.VMEM((n, C), F32),
            pltpu.VMEM((n, C), BF),
            pltpu.VMEM((27, C), F32),
            pltpu.VMEM((27, 8, C), F32),
            pltpu.VMEM((highs, 2, 2, padded, 128), BF),
            pltpu.VMEM((highs, 2, 2, padded, 128), BF),
            pltpu.VMEM((2, highs, 2, padded // 2, 128), BF),
            pltpu.VMEM((2, highs, padded // 2, 128), BF),
            pltpu.VMEM((r4_rows, padded, 128), BF),
            pltpu.SemaphoreType.DMA((4,)),
            pltpu.SemaphoreType.DMA((4,)),
            pltpu.SemaphoreType.DMA((4,)),
            pltpu.SemaphoreType.DMA((3 + len(stages_of(highs)), 8)),
            pltpu.SemaphoreType.DMA((3 + len(stages_of(highs)), 8)),
        ]
        + sum_scratch(count, 8, C)
        + [
            pltpu.VMEM((32, C), BF),
            pltpu.VMEM((8, 32, C), BF),
            pltpu.VMEM((highs, 32, C), BF),
            pltpu.SemaphoreType.DMA((max(owners, 1),)),
            pltpu.SemaphoreType.DMA((8,)),
            pltpu.SemaphoreType.DMA((highs,)),
            pltpu.VMEM((round_up(ROW_JOINT, 8), 128), F32),
            pltpu.VMEM((8, C), F32),
            pltpu.VMEM((32, C), F32),
        ],
        compiler_params=pltpu.CompilerParams(
            vmem_limit_bytes=60 * 1024 * 1024, collective_id=1, has_side_effects=True
        ),
    )(near, delta, conv, nodes, mask3, sums, stats, rows, grads)


def prepare(stats, rows, gathered, shard, flat, norm, spread, mats):
    for i in range(gathered.shape[0] * 8):
        flat[i * shard : (i + 1) * shard, :] = gathered[i // 8, (i // 4) % 2, (i // 2) % 2, i % 2].astype(F32)[:shard]
    for first, out, out_t in mats:
        height, width = out.shape
        per = width // 128
        for k in range(per):
            for r in range(0, height, C):
                piece = flat[pl.ds(first + r * per + k, C, stride=per), :]
                out[r : r + C, k * 128 : (k + 1) * 128] = piece.astype(BF)
                out_t[k * 128 : (k + 1) * 128, r : r + C] = piece.T.astype(BF)
    for i in range(ROW_CONV):
        spread[i * 128 : (i + 1) * 128, :] = jnp.broadcast_to(rows[i : i + 1, :], (128, 128)).T
    gain = jnp.concatenate([rows[i : i + 1, :] for i in range(3)], axis=1)
    shift = jnp.concatenate([rows[3 + i : 4 + i, :] for i in range(3)], axis=1)
    live_total = stats[2:3, :]
    average = stats[0:1, :] / live_total
    variance = stats[1:2, :] / live_total - average * average
    inverse = lax.rsqrt(variance + EPS)
    norm[0] = along_sublanes(inverse * gain)
    norm[1] = along_sublanes(shift - average * inverse * gain)
    norm[2] = along_sublanes(inverse)
    norm[3] = along_sublanes(average * inverse)


def mid_kernel(shard,conv_ref,nodes_ref,dyt_ref,mask_ref,stats_ref,rows_ref,gathered_ref,
    out_ref,dfirst_ref,grads_ref,bns_ref,
    flat_ref,bn_ref,vb_ref,wj_ref,wjt_ref,wo_ref,wot_ref,wh_ref,wht_ref,wf_ref,wft_ref,
    gj_ref,go_ref,gh_ref,gf_ref,vs_ref,hb_ref,first_s,second_s,qkv_s,kn_s,vn_s,a_s,o_s,ob_s,inv_s,dob_s,dqkv_s,x_s,acc_s,dx_s):
    step=pl.program_id(0)
    rep=T//128
    @pl.when(step==0)
    def _():
        for r in (gj_ref,go_ref,gh_ref,gf_ref,vs_ref,hb_ref): r[...]=jnp.zeros_like(r)
        prepare(stats_ref,rows_ref,gathered_ref,shard,flat_ref,bn_ref,vb_ref,
            ((ROW_JOINT,wj_ref,wjt_ref),(ROW_OUT,wo_ref,wot_ref),(ROW_HIDDEN,wh_ref,wht_ref),(ROW_FINAL,wf_ref,wft_ref)))
    def col(i,n=C):
        v=vb_ref[pl.ds(i*C,n),:]
        return jnp.concatenate([v]*rep,axis=1) if rep>1 else v
    def fold(x):
        r=x[:,:128]
        for k in range(1,rep): r=r+x[:,128*k:128*(k+1)]
        return r
    def wide(v): return jnp.concatenate([v]*rep,axis=1)
    firstT=nodes_ref[...].astype(F32)+(conv_ref[...]*wide(bn_ref[0])+wide(bn_ref[1]))
    first_s[...]=firstT
    def ln(x):
        m=jnp.mean(x,axis=0,keepdims=True); c=x-m
        rs=lax.rsqrt(jnp.mean(c*c,axis=0,keepdims=True)+EPS)
        return c*rs, rs
    xh1,rs1=ln(firstT)
    x1=(xh1*col(2)+col(3)).astype(BF)
    x_s[0]=x1
    scale=HD**-0.5
    c2=scale*1.4426950408889634
    live_row=jnp.concatenate([mask_ref[b].astype(F32) for b in range(rep)],axis=1)
    q=(nn(wjt_ref[0:C,:],x1)+col(4))*c2
    qkv_s[0:C,:]=q.astype(BF)
    k=nn(wjt_ref[C:2*C,:],x1)*live_row
    qkv_s[C:2*C,:]=k.astype(BF)
    kn_s[...]=k.T.astype(BF)
    v=nn(wjt_ref[2*C:,:],x1)+col(5)
    qkv_s[2*C:,:]=v.astype(BF)
    vn_s[...]=v.T.astype(BF)
    pi=lax.broadcasted_iota(jnp.int32,(BLK,BLK),0); qi=lax.broadcasted_iota(jnp.int32,(BLK,BLK),1)
    wq=jnp.where(pi<4,jnp.where((qi&3)==pi,0.0,-1e30),jnp.where(pi==4,-1e9*1.4426950408889634,0.0)).astype(BF)
    wq=jnp.concatenate([wq,wq],axis=1)
    wps=[]
    for b in range(rep):
        lv=jnp.broadcast_to(mask_ref[b].astype(F32),(BLK,BLK)).T
        wps.append(jnp.where(qi<4,jnp.where((pi&3)==qi,1.0,0.0),jnp.where(qi==4,1.0-lv,0.0)).astype(BF))
    z=jnp.zeros((HD,BLK),BF)
    def ex(part,i):
        return jnp.concatenate([part if t==i else z for t in range(4)],axis=0)
    tasks=[(b,g,hp*2) for b in range(rep) for g in range(3) for hp in range(2)]
    S={};A={}
    def f_s(t):
        b,g,h0=t; cs=slice(b*BLK,(b+1)*BLK)
        qs=[ex(qkv_s[g*128+i*32:g*128+(i+1)*32,cs],i) for i in (h0,h0+1)]
        S[t]=nn(jnp.concatenate([kn_s[cs,g*128:(g+1)*128],wps[b]],axis=1),jnp.concatenate([jnp.concatenate(qs,axis=1),wq],axis=0))
    def f_a(t):
        b,g,h0=t; cs=slice(b*BLK,(b+1)*BLK)
        s=S.pop(t)
        m=jnp.max(s,axis=0,keepdims=True)
        e=jnp.exp2(s-m)
        inv=1.0/jnp.sum(e,axis=0,keepdims=True)
        a=e.astype(BF)
        for i in range(2):
            a_s[g*4+h0+i,:,cs]=a[:,i*128:(i+1)*128]
            inv_s[g*4+h0+i:g*4+h0+i+1,cs]=inv[:,i*128:(i+1)*128]
        A[t]=(a,inv)
    def f_o(t):
        b,g,h0=t; cs=slice(b*BLK,(b+1)*BLK)
        a,inv=A.pop(t)
        for i in range(2):
            h=g*4+h0+i
            o_s[h*32:(h+1)*32,cs]=nn(qkv_s[2*C+h*32:2*C+(h+1)*32,cs],a[:,i*128:(i+1)*128])*inv[:,i*128:(i+1)*128]
    skew([f_s,f_a,f_o],tasks)
    ob=o_s[...].astype(BF)
    ob_s[...]=ob
    secondT=first_s[...]+(nn(wot_ref[...],ob)+col(6))
    second_s[...]=secondT
    xh2,rs2=ln(secondT)
    x2=(xh2*col(7)+col(8)).astype(BF)
    x_s[1]=x2
    dyTb=dyt_ref[...]
    FC=512
    c0=0.7978845608028654; c1=0.044715
    HH={};PP={}
    def g_h(f):
        fs=slice(f*FC,(f+1)*FC)
        HH[f]=(nn(wht_ref[fs,:],x2),nn(wf_ref[fs,:],dyTb))
    def g_g(f):
        fs=slice(f*FC,(f+1)*FC)
        hb=vb_ref[9*C+f*FC:9*C+(f+1)*FC,:]
        hb=jnp.concatenate([hb]*rep,axis=1)
        h,da=HH.pop(f)
        h=h+hb
        h2=h*h
        t=jnp.tanh(h*(c0+(c0*c1)*h2))
        p=0.5+0.5*t
        act=(h*p).astype(BF)
        dg=p*(1.0+h*(1.0-p)*(2*c0+(6*c0*c1)*h2))
        dpb=(da*dg).astype(BF)
        hb_ref[fs,:]+=fold(dpb.astype(F32))
        PP[f]=(act,dpb)
    def g_o(f):
        fs=slice(f*FC,(f+1)*FC)
        act,dpb=PP.pop(f)
        o=nn(wft_ref[:,fs],act)
        d=nn(wh_ref[:,fs],dpb)
        if f==0:
            acc_s[...]=o; dx_s[...]=d
        else:
            acc_s[...]+=o; dx_s[...]+=d
        gf_ref[:,fs]+=nt(dyTb,act)
        gh_ref[:,fs]+=nt(x2,dpb)
    skew([g_h,g_g,g_o],list(range(F//FC)))
    outT=second_s[...]+(acc_s[...]+col(15-2))
    out_ref[...]=outT.T.astype(BF)
    def ln_back(x,dx,gain,vi):
        xh,rs=ln(x)
        vs_ref[vi]+=fold(dx*xh)
        vs_ref[vi+1]+=fold(dx)
        dh=dx*gain
        m1=jnp.mean(dh,axis=0,keepdims=True)
        m2=jnp.mean(dh*xh,axis=0,keepdims=True)
        return rs*(dh-m1-xh*m2)
    dsec=dyt_ref[...].astype(F32)+ln_back(second_s[...],dx_s[...],col(7),0)
    second_s[...]=dsec
    dbr=dsec.astype(BF)
    vs_ref[2]+=fold(dbr.astype(F32))
    go_ref[...]+=nt(ob_s[...],dbr)
    dat=nn(wo_ref[...],dbr)
    for h in range(HEADS):
        hs=slice(h*32,(h+1)*32)
        dob_s[hs,:]=(dat[hs,:]*inv_s[h:h+1,:]).astype(BF)
    D={};G={}
    def b_d(t):
        b,g,h0=t; cs=slice(b*BLK,(b+1)*BLK)
        ds=[ex(dob_s[g*128+i*32:g*128+(i+1)*32,cs],i) for i in (h0,h0+1)]
        D[t]=nn(vn_s[cs,g*128:(g+1)*128],jnp.concatenate(ds,axis=1))
    def b_s(t):
        b,g,h0=t; cs=slice(b*BLK,(b+1)*BLK)
        dA=D.pop(t)
        out=[]
        for i in range(2):
            h=g*4+h0+i; hs=slice(h*32,(h+1)*32)
            delta=jnp.sum(dob_s[hs,cs].astype(F32)*o_s[hs,cs],axis=0,keepdims=True)
            out.append(a_s[h,:,cs]*(dA[:,i*128:(i+1)*128]-delta).astype(BF))
        G[t]=out
    def b_q(t):
        b,g,h0=t; cs=slice(b*BLK,(b+1)*BLK)
        lrow=live_row[:,cs]
        out=G.pop(t)
        for i in range(2):
            h=g*4+h0+i; hs=slice(h*32,(h+1)*32); ds=out[i]
            dqkv_s[h*32:(h+1)*32,cs]=(nn(qkv_s[C+h*32:C+(h+1)*32,cs],ds)*scale).astype(BF)
            dqkv_s[C+h*32:C+(h+1)*32,cs]=(nt(qkv_s[hs,cs],ds)*(lrow*(scale/c2))).astype(BF)
            dqkv_s[2*C+h*32:2*C+(h+1)*32,cs]=nt(dob_s[hs,cs],a_s[h,:,cs]).astype(BF)
    skew([b_d,b_s,b_q],tasks)
    vs_ref[3]+=fold(dqkv_s[0:C,:].astype(F32))
    vs_ref[4]+=fold(dqkv_s[2*C:,:].astype(F32))
    gj_ref[...]+=nt(x_s[0],dqkv_s[...])
    dx1=nn(wj_ref[...],dqkv_s[...])
    dfT=second_s[...]+ln_back(first_s[...],dx1,col(2),5)
    dfirst_ref[...]=dfT.T
    vs_ref[7]+=fold(dfT*(conv_ref[...]*wide(bn_ref[2])-wide(bn_ref[3])))
    vs_ref[8]+=fold(dfT)
    vs_ref[9]+=fold(dyt_ref[...].astype(F32))
    @pl.when(step==pl.num_programs(0)-1)
    def _():
        flat_ref[...]=jnp.zeros_like(flat_ref)
        bns_ref[...]=jnp.concatenate([lane_sums(vs_ref[i]) for i in (7,8,9)]+[jnp.zeros((5,C),F32)],axis=0)
        for vi,row in ((0,21),(1,24),(2,18),(3,12),(4,15),(5,6),(6,9)):
            for i in range(3):
                flat_ref[pl.ds(row+i,1),:]=jnp.sum(vs_ref[vi,i*128:(i+1)*128,:].T,axis=0,keepdims=True)
        for i in range(12):
            flat_ref[pl.ds(27+i,1),:]=jnp.sum(hb_ref[i*128:(i+1)*128,:].T,axis=0,keepdims=True)
        for first,mat in ((ROW_JOINT,gj_ref),(ROW_OUT,go_ref),(ROW_HIDDEN,gh_ref)):
            rows,cols=mat.shape
            per=cols//128
            for k in range(per):
                for r in range(0,rows,C):
                    flat_ref[pl.ds(first+r*per+k,C,stride=per),:]=mat[r:r+C,k*128:(k+1)*128]
        for k in range(3):
            flat_ref[pl.ds(ROW_FINAL+k,F,stride=3),:]=gf_ref[k*128:(k+1)*128,:].T
        for i in range(grads_ref.shape[0]*8):
            part=flat_ref[i*shard:(i+1)*shard,:]
            pad=grads_ref.shape[-2]-shard
            grads_ref[i//8,(i//4)%2,(i//2)%2,i%2]=jnp.concatenate([part,jnp.zeros((pad,128),F32)],axis=0).astype(BF)


def middle(conv,nodes,dy,mask3,stats,rows,gathered,shard):
    n=conv.shape[1]
    across=pl.BlockSpec((C,T),lambda i:(0,i))
    down=rows_of(C,T)
    flat_rows=gathered.shape[0]*8*shard
    in_specs=[across,across,across,pl.BlockSpec((T//128,1,128),lambda i:(i,0,0)),whole(*stats.shape),whole(*rows.shape),whole(*gathered.shape)]
    outs=[((n,C),BF,down),((n,C),F32,down),(gathered.shape,BF,whole(*gathered.shape)),((8,C),F32,whole(8,C))]
    mats=[]
    for shape in ((C,3*C),(C,C),(C,F),(F,C)): mats+=[(shape,BF),(shape[::-1],BF)]
    scr=[pltpu.VMEM(s,d) for s,d in [((flat_rows,128),F32),((4,C,128),F32),((ROW_CONV*128,128),F32)]+mats+[((C,3*C),F32),((C,C),F32),((C,F),F32),((C,F),F32),((10,C,128),F32),((F,128),F32),((C,T),F32),((C,T),F32),((3*C,T),BF),((T,C),BF),((T,C),BF),((HEADS,BLK,T),BF),((C,T),F32),((C,T),BF),((16,T),F32),((C,T),BF),((3*C,T),BF),((2,C,T),BF),((C,T),F32),((C,T),F32)]]
    return pl.pallas_call(functools.partial(mid_kernel,shard),grid=(n//T,),in_specs=in_specs,out_specs=[o[2] for o in outs],
      out_shape=[jax.ShapeDtypeStruct(o[0],o[1]) for o in outs],scratch_shapes=scr,
      compiler_params=VMEM)(conv,nodes,dy,mask3,stats,rows,gathered)


def shards(nodes_in, out_grad, neighbours, node_mask, master, first_moment, second_moment):
    n = nodes_in.shape[0]
    count, cores = lax.axis_size(AXES), lax.axis_size("grp")
    shard = master.shape[0] // 128
    mask3 = node_mask.reshape(n // 128, 1, 128)
    near = neighbours.T
    conv_t, conv, nodes_t, dy_t, gathered, first_rows, stats = convolve(
        near, nodes_in, out_grad, mask3, master.reshape(shard, 128), count, cores
    )
    output, delta_first, grads, norm_sums = middle(conv_t, nodes_t, dy_t, mask3, stats, first_rows, gathered, shard)
    node_grad, shard_delta, bias_total = convolve_back(
        near, delta_first, conv, nodes_in, mask3, norm_sums, stats, first_rows, grads, shard, count, cores
    )
    shard_delta = shard_delta.reshape(-1)
    position = lax.axis_index(AXES) * master.shape[0] + lax.iota(jnp.int32, master.shape[0])
    step_rate = jnp.where(position < 10 * C + F, 0.2, 0.03)
    new_first = 0.9 * first_moment + 0.1 * shard_delta
    new_second = 0.95 * second_moment + 0.05 * shard_delta * shard_delta
    first_hat = new_first / (1.0 - 0.9**STEP)
    second_hat = new_second / (1.0 - 0.95**STEP)
    new_master = master - step_rate * (first_hat / (jnp.sqrt(second_hat) + 1e-08) + 0.01 * master)
    return (
        output,
        node_grad,
        new_master,
        new_first,
        new_second,
        new_master.astype(BF),
        bias_total.reshape(-1),
    )


def solution(mesh):
    rows, flat = P(AXES, None), P(AXES)
    return jax.shard_map(
        shards,
        mesh=mesh,
        in_specs=(rows, rows, rows, flat, flat, flat, flat),
        out_specs=(rows, rows, flat, flat, flat, flat, P()),
        check_vma=False,
    )
```

```python
import functools

import jax
import jax.numpy as jnp
from jax import lax
from jax.experimental import pallas as pl
from jax.experimental.pallas import tpu as pltpu
from jax.sharding import PartitionSpec as P

C = 384
HEADS = 12
HD = 32
F = 1536
HALO = 64
STEP = 5
EPS = 1e-5
AXES = ("rows", "grp")
F32 = jnp.float32
BF = jnp.bfloat16

BLK = 128
T = 512
TB = 512
ROW_CONV = (10 * C + F) // 128
ROW_JOINT = ROW_CONV + 27 * C // 128
ROW_OUT = ROW_JOINT + C * 3 * C // 128
ROW_HIDDEN = ROW_OUT + C * C // 128
ROW_FINAL = ROW_HIDDEN + C * F // 128
ROW_END = ROW_FINAL + C * F // 128
VMEM = pltpu.CompilerParams(vmem_limit_bytes=60 * 1024 * 1024)


def nn(a, b):
    return jnp.dot(a, b, preferred_element_type=F32)


def nt(a, b):
    return lax.dot_general(a, b, (((1,), (1,)), ((), ())), preferred_element_type=F32)


def whole(*shape):
    return pl.BlockSpec(shape, lambda i: (0,) * len(shape), pipeline_mode=pl.Buffered(1))


def skew(stages, tasks):
    for i in range(len(tasks) + len(stages) - 1):
        for k, stage in enumerate(stages):
            if 0 <= i - k < len(tasks):
                stage(tasks[i - k])


def along_sublanes(row):
    parts = [row[:, i : i + 128] for i in range(0, row.shape[1], 128)]
    return jnp.concatenate([jnp.broadcast_to(p, (128, 128)).T for p in parts], axis=0)


def lane_sums(value):
    parts = [value[i : i + 128, :].T for i in range(0, value.shape[0], 128)]
    return jnp.concatenate([jnp.sum(p, axis=0, keepdims=True) for p in parts], axis=1)


def rows_of(width, size):
    return pl.BlockSpec((size, width), lambda i: (i, 0))


MESH = pl.DeviceIdType.MESH


def CUTS_GATHER(nh):
    return [1] * nh + [3, 7]


def round_up(value, step):
    return -(-value // step) * step


def my_place():
    return lax.axis_index("rows") * lax.axis_size("grp") + lax.axis_index("grp")


def device(place, cores):
    return (place // cores, place % cores)


def stages_of(count):
    out, stride = [], 1
    while stride < count:
        size = min(8, count // stride)
        out.append((stride, size))
        stride *= size
    return out


def others(me, stride, size):
    mine = (me // stride) % size
    return mine, [(k, me + ((mine + k) % size - mine) * stride) for k in range(1, size)]


def greet(partners, cores):
    barrier = pltpu.get_barrier_semaphore()
    for place in partners:
        pl.semaphore_signal(barrier, inc=1, device_id=device(place, cores), device_id_type=MESH)
    pl.semaphore_wait(barrier, len(partners))


def send(source, target, send_sem, recv_sem, place, cores):
    return pltpu.make_async_remote_copy(
        src_ref=source,
        dst_ref=target,
        send_sem=send_sem,
        recv_sem=recv_sem,
        device_id=device(place, cores),
        device_id_type=MESH,
    )


def all_sum(value, me, count, cores, slots, send_sems, recv_sems, beside=None):
    for s, (stride, size) in enumerate(stages_of(count)):
        mine, partners = others(me, stride, size)
        slots[s, mine] = value
        copies = [
            send(slots.at[s, mine], slots.at[s, mine], send_sems.at[s, k], recv_sems.at[s, k], place, cores)
            for k, place in partners
        ]
        for copy in copies:
            copy.start()
        if beside is not None:
            beside(s)
        for copy in copies:
            copy.wait()
        value = slots[s, 0]
        for i in range(1, size):
            value = value + slots[s, i]
    return value


def sum_scratch(count, rows, width):
    n = len(stages_of(count))
    return [
        pltpu.VMEM((n, 8, rows, width), F32),
        pltpu.SemaphoreType.DMA((n, 8)),
        pltpu.SemaphoreType.DMA((n, 8)),
    ]


def conv_kernel(count, cores, owners, near_ref, nodes_ref, dy_ref, mask_ref, master_ref,
                convt_ref, conv_ref, nodest_ref, dyt_ref, gathered_ref, first_ref, stats_ref,
                ext, extt, dy_s, early, weight, sums, own_s, local_sem, halo_send, halo_recv, e_send, e_recv, g_send,
                g_recv, slots, s_send, s_recv):
    step = pl.program_id(0)
    steps = pl.num_programs(0)
    block = (step + 1) % steps
    n = nodes_ref.shape[0]
    shard = master_ref.shape[0]
    padded = gathered_ref.shape[-2]
    half = padded // 2
    e_rows = early.shape[1]
    me = my_place()
    low, high = me % 8, me // 8
    y, x, g = low // 4, (low // 2) % 2, low % 2
    highs = stages_of(count // 8)
    left, right = (me + count - 1) % count, (me + 1) % count

    local = pltpu.make_async_copy(nodes_ref, ext.at[pl.ds(HALO, n)], local_sem.at[0])
    keep = pltpu.make_async_copy(own_s, gathered_ref.at[high, y, x, g], local_sem.at[1])
    local_dy = pltpu.make_async_copy(dy_ref, dy_s, local_sem.at[2])

    def turn_dy(k):
        at = pl.ds(pl.multiple_of(k * BLK, BLK), BLK)
        dyt_ref[:, at] = dy_s[at, :].T
        return 0

    def turn(k):
        at = pl.ds(pl.multiple_of(k * BLK, BLK), BLK)
        extt[:, at] = ext[at, :].T
        return 0
    to_left = send(nodes_ref.at[pl.ds(0, HALO)], ext.at[pl.ds(HALO + n, HALO)], halo_send.at[0], halo_recv.at[0], left, cores)
    to_right = send(nodes_ref.at[pl.ds(n - HALO, HALO)], ext.at[pl.ds(0, HALO)], halo_send.at[1], halo_recv.at[1], right, cores)

    def high_copies(s):
        stride, size = highs[s]
        mine, partners = others(high, stride, size)
        own = gathered_ref.at[pl.ds(high // stride * stride, stride), y, x, g]
        return [
            send(own, own, g_send.at[s, k], g_recv.at[s, k], place * 8 + low, cores)
            for k, place in partners
        ]

    nh = len(highs)
    y_place, x_place, g_place = me + 4 - 8 * y, me + 2 - 4 * x, me + 1 - 2 * g

    def quad_copies(t):
        top, bottom = pl.ds(0, half), pl.ds(half, half)
        if t == 0:
            a = gathered_ref.at[:, y, x, g, top]
            b = gathered_ref.at[:, y, x, g, bottom]
            to_a, to_b = y_place, x_place
        else:
            a = gathered_ref.at[:, :, x, g, top]
            b = gathered_ref.at[:, y, :, g, bottom]
            to_a, to_b = x_place, y_place
        s = nh + t
        return [send(a, a, g_send.at[s, 0], g_recv.at[s, 0], to_a, cores), send(b, b, g_send.at[s, 1], g_recv.at[s, 1], to_b, cores)]

    def core_copies():
        own = gathered_ref.at[:, :, :, g]
        return [send(own, own, g_send.at[nh + 2, 0], g_recv.at[nh + 2, 0], g_place, cores)]

    plan = [functools.partial(high_copies, s) for s in range(nh)]
    plan += [functools.partial(quad_copies, 0), functools.partial(quad_copies, 1), core_copies]
    cuts = CUTS_GATHER(nh)

    @pl.when(step == 0)
    def _():
        local.start()
        local_dy.start()
        sums[...] = jnp.zeros_like(sums)
        own = jnp.concatenate([master_ref[...], jnp.zeros((padded - shard, 128), F32)], axis=0).astype(BF)
        own_s[...] = own
        keep.start()
        wide = [h for h in range(1, count // 8)]
        partners = [left, right]
        partners += [(high + h) % (count // 8) * 8 + low for h in wide]
        partners += [place for _, place in others(me, 1, 8)[1]]
        greet(partners, cores)
        early_copies = []
        for o in range(owners):
            up = [send(early.at[o], early.at[o], e_send.at[o, 8 + h], e_recv.at[o, 0], h * 8 + o, cores) for h in wide]
            out = [
                send(early.at[o], early.at[o], e_send.at[o, k], e_recv.at[o, 1], me + k - o, cores)
                for k in range(8) if k != o
            ]
            early_copies.append((up, out))

            @pl.when(low == o)
            def _(o=o, up=up, out=out):
                @pl.when(high == 0)
                def _():
                    early[o] = own[:e_rows]
                    for copy in up:
                        copy.start()
                @pl.when(high > 0)
                def _():
                    send(early.at[o], early.at[o], e_send.at[o, 8], e_recv.at[o, 0], left, cores).wait_recv()
                for copy in out:
                    copy.start()
        to_left.start()
        to_right.start()
        keep.wait()
        for copy in plan[0]():
            copy.start()
        local.wait()
        lax.fori_loop(1, n // BLK, lambda k, _: turn(k), 0)
        for o in range(owners):
            @pl.when(low != o)
            def _():
                send(early.at[o], early.at[o], e_send.at[o, 8], e_recv.at[o, 1], left, cores).wait_recv()
        for o in range(owners):
            rows = min(shard, e_rows)
            first_ref[pl.ds(o * shard, rows), :] = early[o].astype(F32)[:rows]
        for j in range(27):
            row = jnp.concatenate([first_ref[ROW_CONV + 3 * j + i : ROW_CONV + 3 * j + i + 1, :] for i in range(3)], axis=1)
            weight[j] = along_sublanes(row)
        for o, (up, out) in enumerate(early_copies):
            @pl.when(low == o)
            def _(up=up, out=out):
                @pl.when(high == 0)
                def _():
                    for copy in up:
                        copy.wait_send()
                for copy in out:
                    copy.wait_send()

    for s in range(len(plan) - 1):
        @pl.when(step == cuts[s])
        def _(s=s):
            for copy in plan[s]():
                copy.wait()
            for copy in plan[s + 1]():
                copy.start()

    @pl.when(step == steps - 2)
    def _():
        to_left.wait()
        to_right.wait()
        turn(0)
        turn(n // BLK)

    sub = lax.broadcasted_iota(jnp.int32, (2 * BLK, BLK), 0).astype(F32).astype(BF)
    one, zero = jnp.ones((), BF), jnp.zeros((), BF)
    pairs = [(j, j + 1) for j in range(0, 12, 2)] + [(12, 14)] + [(j, j + 1) for j in range(15, 27, 2)]
    at = pl.multiple_of(block * T, T)
    lane = lax.broadcasted_iota(jnp.int32, (27, BLK), 1)
    places, totals, picks, comes = {}, {}, {}, {}
    for b in range(T // BLK):
        near = near_ref[:, b * BLK : (b + 1) * BLK]
        places[b] = jnp.where(near < 0, -1, near + lane).astype(F32).astype(BF)

    def pick(task):
        b, q = task
        if q == 0:
            center = ext[pl.ds(at + b * BLK + HALO, BLK), :].astype(F32).T
            nodest_ref[:, b * BLK : (b + 1) * BLK] = center.astype(BF)
            totals[b] = center * weight[13]
        picks[task] = jnp.concatenate(
            [jnp.where(places[b][j : j + 1, :] == sub, one, zero) for j in pairs[q]], axis=1
        )

    def multiply(task):
        b, q = task
        comes[task] = nn(extt[:, pl.ds(at + b * BLK, 2 * BLK)], picks.pop(task))

    def add(task):
        b, q = task
        come = comes.pop(task)
        totals[b] = totals[b] + (come[:, :BLK] * weight[pairs[q][0]] + come[:, BLK:] * weight[pairs[q][1]])
        if q == len(pairs) - 1:
            total = totals.pop(b)
            convt_ref[:, b * BLK : (b + 1) * BLK] = total
            conv_ref[b * BLK : (b + 1) * BLK, :] = total.T.astype(BF)
            live = mask_ref[b].astype(F32)
            kept = total * live
            sums[0] += kept
            sums[1] += kept * total
            sums[2, 0:1] += live

    skew([pick, multiply, add], [(b, q) for b in range(T // BLK) for q in range(len(pairs))])

    @pl.when(step == steps - 1)
    def _():
        rows = [lane_sums(sums[i]) for i in range(2)]
        rows += [jnp.broadcast_to(jnp.sum(sums[2, 0:1], axis=1, keepdims=True), (1, C))]
        rows = jnp.concatenate(rows + [jnp.zeros((5, C), F32)], axis=0)
        local_dy.wait()
        cut = len(stages_of(count))

        def beside(s):
            lax.fori_loop(n // BLK * s // cut, n // BLK * (s + 1) // cut, lambda k, _: turn_dy(k), 0)

        stats_ref[...] = all_sum(rows, me, count, cores, slots, s_send, s_recv, beside)
        for copy in plan[-1]():
            copy.wait()


def convolve(near, nodes, dy, mask3, master, count, cores):
    n = nodes.shape[0]
    steps = n // T
    shard = master.shape[0]
    padded = round_up(shard, 32)
    owners = -(-ROW_JOINT // shard)
    e_rows = min(padded, round_up(ROW_JOINT, 16))
    down = pl.BlockSpec((T, C), lambda i: ((i + 1) % steps, 0))
    across = pl.BlockSpec((C, T), lambda i: (0, (i + 1) % steps))
    anywhere = pl.BlockSpec(memory_space=pl.ANY)
    stages = len(stages_of(count // 8)) + 3
    first_rows = round_up((owners - 1) * shard + e_rows, 8)
    return pl.pallas_call(
        functools.partial(conv_kernel, count, cores, owners),
        grid=(steps,),
        in_specs=[
            pl.BlockSpec((27, T), lambda i: (0, (i + 1) % steps)),
            anywhere,
            anywhere,
            pl.BlockSpec((T // BLK, 1, 128), lambda i: ((i + 1) % steps, 0, 0)),
            whole(shard, 128),
        ],
        out_specs=[across, down, across, whole(C, n), anywhere, whole(first_rows, 128), whole(8, C)],
        out_shape=[
            jax.ShapeDtypeStruct((C, n), F32),
            jax.ShapeDtypeStruct((n, C), BF),
            jax.ShapeDtypeStruct((C, n), BF),
            jax.ShapeDtypeStruct((C, n), BF),
            jax.ShapeDtypeStruct((count // 8, 2, 2, 2, padded, 128), BF),
            jax.ShapeDtypeStruct((first_rows, 128), F32),
            jax.ShapeDtypeStruct((8, C), F32),
        ],
        scratch_shapes=[
            pltpu.VMEM((n + 2 * HALO, C), BF),
            pltpu.VMEM((C, n + 2 * HALO), BF),
            pltpu.VMEM((n, C), BF),
            pltpu.VMEM((owners, e_rows, 128), BF),
            pltpu.VMEM((27, C, 128), F32),
            pltpu.VMEM((3, C, 128), F32),
            pltpu.VMEM((padded, 128), BF),
            pltpu.SemaphoreType.DMA((3,)),
            pltpu.SemaphoreType.DMA((2,)),
            pltpu.SemaphoreType.DMA((2,)),
            pltpu.SemaphoreType.DMA((owners, 8 + count // 8)),
            pltpu.SemaphoreType.DMA((owners, 2)),
            pltpu.SemaphoreType.DMA((stages, 8)),
            pltpu.SemaphoreType.DMA((stages, 8)),
        ]
        + sum_scratch(count, 8, C),
        compiler_params=pltpu.CompilerParams(
            vmem_limit_bytes=60 * 1024 * 1024, collective_id=0, has_side_effects=True
        ),
    )(near, nodes, dy, mask3, master)


def conv_back_kernel(count, cores, owners, near_hbm, first_hbm, conv_hbm, x_ref, mask_ref, sums_ref, stats_ref,
                     rows_ref, grads_ref,
                     grad_ref, total_s, bias_out,
                     near, ext, delta, conv, weight, dw, kept, r1, r2, r3, r4, local_sem, halo_send, halo_recv, g_send,
                     g_recv, slots, s_send, s_recv, w_own, w_slots, w_high, w_sem, w_recv, w_recv_high, early_s, factors, w_sum):
    step = pl.program_id(0)
    steps = pl.num_programs(0)
    block = (step + 1) % steps
    n = first_hbm.shape[0]
    shard = total_s.shape[0]
    padded = grads_ref.shape[-2]
    half = padded // 2
    me = my_place()
    low, high = me % 8, me // 8
    y, x, g = low // 4, (low // 2) % 2, low % 2
    highs = stages_of(count // 8)[::-1]
    nh = len(highs)
    left, right = (me + count - 1) % count, (me + 1) % count
    y_place, x_place, g_place = me + 4 - 8 * y, me + 2 - 4 * x, me + 1 - 2 * g
    top, bottom = pl.ds(0, half), pl.ds(half, half)

    locals_ = [
        pltpu.make_async_copy(first_hbm, delta, local_sem.at[0]),
        pltpu.make_async_copy(conv_hbm, conv, local_sem.at[1]),
        pltpu.make_async_copy(near_hbm, near.at[:, pl.ds(BLK, n)], local_sem.at[2]),
        pltpu.make_async_copy(grads_ref.at[:, :, :, g], kept, local_sem.at[3]),
    ]
    near_halo = [
        send(near_hbm.at[:, pl.ds(0, BLK)], near.at[:, pl.ds(BLK + n, BLK)], halo_send.at[0], halo_recv.at[0], left, cores),
        send(near_hbm.at[:, pl.ds(n - BLK, BLK)], near.at[:, pl.ds(0, BLK)], halo_send.at[1], halo_recv.at[1], right, cores),
    ]
    delta_halo = [
        send(ext.at[pl.ds(HALO, HALO)], ext.at[pl.ds(HALO + n, HALO)], halo_send.at[2], halo_recv.at[2], left, cores),
        send(ext.at[pl.ds(n, HALO)], ext.at[pl.ds(0, HALO)], halo_send.at[3], halo_recv.at[3], right, cores),
    ]

    blocks, per = n // BLK, TB // BLK

    def make_rows(i):
        at = pl.ds(pl.multiple_of(i * BLK, BLK), BLK)
        live = jnp.broadcast_to(mask_ref[i].astype(F32), (BLK, BLK)).T
        live = jnp.concatenate([live] * 3, axis=1)
        value = delta[at, :] * factors[0:1, :] + live * (factors[1:2, :] + factors[2:3, :] * conv[at, :].astype(F32))
        ext[pl.ds(pl.multiple_of(i * BLK + HALO, HALO), BLK), :] = value.astype(BF)
        return 0

    def core_copies():
        return [send(grads_ref.at[:, :, :, 1 - g], r1, g_send.at[0, 0], g_recv.at[0, 0], g_place, cores)]

    def core_add():
        def body(i, _):
            kept[i // 4, (i // 2) % 2, i % 2] = (
                kept[i // 4, (i // 2) % 2, i % 2].astype(F32) + r1[i // 4, (i // 2) % 2, i % 2].astype(F32)
            ).astype(BF)
            return 0
        lax.fori_loop(0, count // 2, body, 0)

    def quad_copies_0():
        return [
            send(kept.at[:, :, 1 - x, top], r2.at[0], g_send.at[1, 0], g_recv.at[1, 0], x_place, cores),
            send(kept.at[:, 1 - y, :, bottom], r2.at[1], g_send.at[1, 1], g_recv.at[1, 1], y_place, cores),
        ]

    def quad_add_0():
        def body(i, _):
            h, w = i // 2, i % 2
            kept[h, w, x, top] = (
                kept[h, w, x, top].astype(F32) + r2[0, h, w].astype(F32)
            ).astype(BF)
            kept[h, y, w, bottom] = (
                kept[h, y, w, bottom].astype(F32) + r2[1, h, w].astype(F32)
            ).astype(BF)
            return 0
        lax.fori_loop(0, count // 4, body, 0)

    def quad_copies_1():
        return [
            send(kept.at[:, 1 - y, x, top], r3.at[0], g_send.at[2, 0], g_recv.at[2, 0], y_place, cores),
            send(kept.at[:, y, 1 - x, bottom], r3.at[1], g_send.at[2, 1], g_recv.at[2, 1], x_place, cores),
        ]

    def quad_add_1():
        def body(h, _):
            kept[h, y, x, top] = (
                kept[h, y, x, top].astype(F32) + r3[0, h].astype(F32)
            ).astype(BF)
            kept[h, y, x, bottom] = (
                kept[h, y, x, bottom].astype(F32) + r3[1, h].astype(F32)
            ).astype(BF)
            return 0
        lax.fori_loop(0, count // 8, body, 0)

    bases = []
    base = 0
    for stride, size in highs:
        bases.append(base)
        base += (size - 1) * stride

    def high_copies(s):
        stride, size = highs[s]
        mine, partners = others(high, stride, size)
        out = []
        for k, place in partners:
            source = kept.at[pl.ds(place // stride * stride, stride), y, x]
            target = r4.at[pl.ds(bases[s] + (k - 1) * stride, stride)]
            out.append(send(source, target, g_send.at[3 + s, k], g_recv.at[3 + s, k], place * 8 + low, cores))
        return out

    def high_add(s):
        stride, size = highs[s]
        start = high // stride * stride
        def body(i, _):
            value = kept[start + i, y, x].astype(F32)
            for k in range(size - 1):
                value = value + r4[bases[s] + k * stride + i].astype(F32)
            if s == nh - 1:
                total_s[...] = value[:shard]
            else:
                kept[start + i, y, x] = value.astype(BF)
            return 0
        lax.fori_loop(0, stride, body, 0)

    plan = [(core_copies, core_add), (quad_copies_0, quad_add_0), (quad_copies_1, quad_add_1)]
    plan += [(functools.partial(high_copies, s), functools.partial(high_add, s)) for s in range(nh)]
    cuts = CUTS_SCATTER(nh)

    @pl.when(step == 0)
    def _():
        for copy in locals_:
            copy.start()
        dw[...] = jnp.zeros_like(dw)
        partners = [left, right]
        partners += [(high + h) % (count // 8) * 8 + low for h in range(1, count // 8)]
        partners += [place for _, place in others(me, 1, 8)[1]]
        greet(partners, cores)
        def beside(s):
            if s == 0:
                for copy in plan[0][0]() + near_halo:
                    copy.start()
        total = all_sum(sums_ref[...], me, count, cores, slots, s_send, s_recv, beside)
        gain_total, shift_total = total[0:1], total[1:2]
        bias_out[...] = jnp.concatenate([total[2:3, i * 128 : (i + 1) * 128] for i in range(3)], axis=0)
        early_s[...] = jnp.zeros_like(early_s)
        for i in range(3):
            early_s[i : i + 1, :] = gain_total[:, i * 128 : (i + 1) * 128]
            early_s[3 + i : 4 + i, :] = shift_total[:, i * 128 : (i + 1) * 128]
            early_s[ROW_CONV - 3 + i : ROW_CONV - 2 + i, :] = total[2:3, i * 128 : (i + 1) * 128]
        for k in range(3):
            weight[:, k * 128 : (k + 1) * 128] = rows_ref[pl.ds(ROW_CONV + k, 27, stride=3), :]
        gain = jnp.concatenate([rows_ref[i : i + 1, :] for i in range(3)], axis=1)
        live_total = stats_ref[2:3]
        average = stats_ref[0:1] / live_total
        variance = stats_ref[1:2] / live_total - average * average
        inverse = lax.rsqrt(variance + EPS)
        delta_variance = -0.5 * inverse * inverse * inverse * (gain * gain_total / inverse)
        delta_average = -gain * shift_total * inverse - 2.0 * average * delta_variance
        a = gain * inverse
        b = delta_average / live_total
        c = 2.0 * delta_variance / live_total
        for copy in locals_:
            copy.wait()

        factors[0:1, :] = a
        factors[1:2, :] = b
        factors[2:3, :] = c
        make_rows(0)
        make_rows(blocks - 1)
        lax.fori_loop(per - 1, 2 * per + 1, lambda k, _: make_rows(k), 0)
        for copy in delta_halo:
            copy.start()

    for s in range(len(plan)):
        @pl.when(step == cuts[s])
        def _(s=s):
            for copy in plan[s][0]():
                copy.wait()
            plan[s][1]()
            if s + 1 < len(plan):
                for copy in plan[s + 1][0]():
                    copy.start()

    @pl.when(step == steps - 2)
    def _():
        for copy in near_halo + delta_halo:
            copy.wait()

    start = pl.multiple_of(block * TB, TB)
    target = lax.broadcasted_iota(jnp.int32, (BLK, 2 * BLK), 0).astype(F32).astype(BF)
    one, zero = jnp.ones((), BF), jnp.zeros((), BF)
    lane = lax.broadcasted_iota(jnp.int32, (27, 2 * BLK), 1) - BLK
    places, totals, picks, comes, xs = {}, {}, {}, {}, {}
    for b in range(TB // BLK):
        near_w = near[:, pl.ds(start + b * BLK, 3 * BLK)][:, HALO : HALO + 2 * BLK]
        places[b] = jnp.where(near_w < 0, -1, near_w + lane).astype(F32).astype(BF)

    def pick(task):
        b, q = task
        picks[task] = jnp.concatenate(
            [jnp.where(places[b][j : j + 1, :] == target, one, zero) for j in range(3 * q, 3 * q + 3)], axis=0
        )

    def multiply(task):
        b, q = task
        comes[task] = nn(picks.pop(task), ext[pl.ds(start + b * BLK, 2 * BLK), :])

    def add(task):
        b, q = task
        come = comes.pop(task)
        if q == 0:
            xs[b] = x_ref[b * BLK : (b + 1) * BLK, :].astype(F32)
            totals[b] = delta[pl.ds(start + b * BLK, BLK), :]
        for i in range(3):
            j, part = 3 * q + i, come[i * BLK : (i + 1) * BLK]
            totals[b] = totals[b] + part * weight[j : j + 1, :]
            dw[j] += jnp.sum((part * xs[b]).reshape(BLK // 8, 8, C), axis=0)
        if q == 8:
            grad_ref[b * BLK : (b + 1) * BLK, :] = totals.pop(b).astype(BF)

    skew([pick, multiply, add], [(b, q) for b in range(TB // BLK) for q in range(9)])

    for k in range(per):
        i = ((block + 1) * per + 1 + k) % blocks
        make_rows(jnp.where((i == 0) | (i == blocks - 1), blocks - 2, i))

    @pl.when(step == steps - 1)
    def _():
        mine = jnp.concatenate([jnp.sum(dw[...], axis=1), jnp.zeros((5, C), F32)], axis=0)
        w_own[...] = mine.astype(BF)
        to_first = send(w_own, w_slots.at[low], w_sem.at[0], w_recv.at[low], me - low, cores)

        @pl.when(low != 0)
        def _():
            to_first.start()
            to_first.wait_send()

        @pl.when(low == 0)
        def _():
            for k in range(1, 8):
                send(w_own, w_slots.at[k], w_sem.at[0], w_recv.at[k], me + k, cores).wait_recv()
            mine_8 = mine + sum(w_slots[k].astype(F32) for k in range(1, 8))
            w_own[...] = mine_8.astype(BF)

            @pl.when(high != 0)
            def _():
                up = send(w_own, w_high.at[high], w_sem.at[0], w_recv_high.at[high], 0, cores)
                up.start()
                up.wait_send()

            @pl.when(high == 0)
            def _():
                for h in range(1, count // 8):
                    send(w_own, w_high.at[h], w_sem.at[0], w_recv_high.at[h], h * 8, cores).wait_recv()
                mine_all = mine_8 + sum(w_high[h].astype(F32) for h in range(1, count // 8))
                w_own[...] = mine_all.astype(BF)
                w_sum[...] = mine_all
                out = [send(w_own, w_high.at[0], w_sem.at[o], w_recv_high.at[0], o, cores) for o in range(1, owners)]
                for copy in out:
                    copy.start()
                for copy in out:
                    copy.wait_send()

        for o in range(owners):
            @pl.when(me == o)
            def _(o=o):
                if o == 0:
                    sums = w_sum[...]
                else:
                    send(w_own, w_high.at[0], w_sem.at[0], w_recv_high.at[0], 0, cores).wait_recv()
                    sums = w_high[0].astype(F32)
                for k in range(3):
                    early_s[pl.ds(ROW_CONV + k, 27, stride=3), :] = sums[:27, k * 128 : (k + 1) * 128]
                rows = min(shard, early_s.shape[0] - o * shard)
                total_s[0:rows, :] += early_s[o * shard : o * shard + rows, :]


def CUTS_SCATTER(nh):
    return [1, 3, 4] + [4 + 3 * (s + 1) // nh for s in range(nh)]


def convolve_back(near, delta, conv, nodes, mask3, sums, stats, rows, grads, shard, count, cores):
    n = nodes.shape[0]
    steps = n // TB
    padded = grads.shape[-2]
    highs = count // 8
    owners = -(-ROW_JOINT // shard)
    turned = pl.BlockSpec((TB, C), lambda i: ((i + 1) % steps, 0))
    anywhere = pl.BlockSpec(memory_space=pl.ANY)
    r4_rows = sum((size - 1) * stride for stride, size in stages_of(highs))
    return pl.pallas_call(
        functools.partial(conv_back_kernel, count, cores, owners),
        grid=(steps,),
        in_specs=[
            anywhere,
            anywhere,
            anywhere,
            turned,
            whole(*mask3.shape),
            whole(*sums.shape),
            whole(*stats.shape),
            whole(*rows.shape),
            anywhere,
        ],
        out_specs=[turned, whole(shard, 128), whole(3, 128)],
        out_shape=[
            jax.ShapeDtypeStruct((n, C), BF),
            jax.ShapeDtypeStruct((shard, 128), F32),
            jax.ShapeDtypeStruct((3, 128), F32),
        ],
        scratch_shapes=[
            pltpu.VMEM((27, n + 2 * BLK), jnp.int32),
            pltpu.VMEM((n + 2 * HALO, C), BF),
            pltpu.VMEM((n, C), F32),
            pltpu.VMEM((n, C), BF),
            pltpu.VMEM((27, C), F32),
            pltpu.VMEM((27, 8, C), F32),
            pltpu.VMEM((highs, 2, 2, padded, 128), BF),
            pltpu.VMEM((highs, 2, 2, padded, 128), BF),
            pltpu.VMEM((2, highs, 2, padded // 2, 128), BF),
            pltpu.VMEM((2, highs, padded // 2, 128), BF),
            pltpu.VMEM((r4_rows, padded, 128), BF),
            pltpu.SemaphoreType.DMA((4,)),
            pltpu.SemaphoreType.DMA((4,)),
            pltpu.SemaphoreType.DMA((4,)),
            pltpu.SemaphoreType.DMA((3 + len(stages_of(highs)), 8)),
            pltpu.SemaphoreType.DMA((3 + len(stages_of(highs)), 8)),
        ]
        + sum_scratch(count, 8, C)
        + [
            pltpu.VMEM((32, C), BF),
            pltpu.VMEM((8, 32, C), BF),
            pltpu.VMEM((highs, 32, C), BF),
            pltpu.SemaphoreType.DMA((max(owners, 1),)),
            pltpu.SemaphoreType.DMA((8,)),
            pltpu.SemaphoreType.DMA((highs,)),
            pltpu.VMEM((round_up(ROW_JOINT, 8), 128), F32),
            pltpu.VMEM((8, C), F32),
            pltpu.VMEM((32, C), F32),
        ],
        compiler_params=pltpu.CompilerParams(
            vmem_limit_bytes=60 * 1024 * 1024, collective_id=1, has_side_effects=True
        ),
    )(near, delta, conv, nodes, mask3, sums, stats, rows, grads)


def prepare(stats, rows, gathered, shard, flat, norm, spread, mats):
    for i in range(gathered.shape[0] * 8):
        flat[i * shard : (i + 1) * shard, :] = gathered[i // 8, (i // 4) % 2, (i // 2) % 2, i % 2].astype(F32)[:shard]
    for first, out, out_t in mats:
        height, width = out.shape
        per = width // 128
        for k in range(per):
            for r in range(0, height, C):
                piece = flat[pl.ds(first + r * per + k, C, stride=per), :]
                out[r : r + C, k * 128 : (k + 1) * 128] = piece.astype(BF)
                out_t[k * 128 : (k + 1) * 128, r : r + C] = piece.T.astype(BF)
    for i in range(ROW_CONV):
        spread[i * 128 : (i + 1) * 128, :] = jnp.broadcast_to(rows[i : i + 1, :], (128, 128)).T
    gain = jnp.concatenate([rows[i : i + 1, :] for i in range(3)], axis=1)
    shift = jnp.concatenate([rows[3 + i : 4 + i, :] for i in range(3)], axis=1)
    live_total = stats[2:3, :]
    average = stats[0:1, :] / live_total
    variance = stats[1:2, :] / live_total - average * average
    inverse = lax.rsqrt(variance + EPS)
    norm[0] = along_sublanes(inverse * gain)
    norm[1] = along_sublanes(shift - average * inverse * gain)
    norm[2] = along_sublanes(inverse)
    norm[3] = along_sublanes(average * inverse)


def mid_kernel(shard,conv_ref,nodes_ref,dyt_ref,mask_ref,stats_ref,rows_ref,gathered_ref,
    out_ref,dfirst_ref,grads_ref,bns_ref,
    flat_ref,bn_ref,vb_ref,wj_ref,wjt_ref,wo_ref,wot_ref,wh_ref,wht_ref,wf_ref,wft_ref,
    gj_ref,go_ref,gh_ref,gf_ref,vs_ref,hb_ref,first_s,second_s,qkv_s,kn_s,vn_s,a_s,o_s,ob_s,inv_s,dob_s,dqkv_s,x_s,acc_s,dx_s):
    step=pl.program_id(0)
    rep=T//128
    @pl.when(step==0)
    def _():
        for r in (gj_ref,go_ref,gh_ref,gf_ref,vs_ref,hb_ref): r[...]=jnp.zeros_like(r)
        prepare(stats_ref,rows_ref,gathered_ref,shard,flat_ref,bn_ref,vb_ref,
            ((ROW_JOINT,wj_ref,wjt_ref),(ROW_OUT,wo_ref,wot_ref),(ROW_HIDDEN,wh_ref,wht_ref),(ROW_FINAL,wf_ref,wft_ref)))
    def col(i,n=C):
        v=vb_ref[pl.ds(i*C,n),:]
        return jnp.concatenate([v]*rep,axis=1) if rep>1 else v
    def fold(x):
        r=x[:,:128]
        for k in range(1,rep): r=r+x[:,128*k:128*(k+1)]
        return r
    def wide(v): return jnp.concatenate([v]*rep,axis=1)
    firstT=nodes_ref[...].astype(F32)+(conv_ref[...]*wide(bn_ref[0])+wide(bn_ref[1]))
    first_s[...]=firstT
    def ln(x):
        m=jnp.mean(x,axis=0,keepdims=True); c=x-m
        rs=lax.rsqrt(jnp.mean(c*c,axis=0,keepdims=True)+EPS)
        return c*rs, rs
    xh1,rs1=ln(firstT)
    x1=(xh1*col(2)+col(3)).astype(BF)
    x_s[0]=x1
    scale=HD**-0.5
    c2=scale*1.4426950408889634
    live_row=jnp.concatenate([mask_ref[b].astype(F32) for b in range(rep)],axis=1)
    q=(nn(wjt_ref[0:C,:],x1)+col(4))*c2
    qkv_s[0:C,:]=q.astype(BF)
    k=nn(wjt_ref[C:2*C,:],x1)*live_row
    qkv_s[C:2*C,:]=k.astype(BF)
    kn_s[...]=k.T.astype(BF)
    v=nn(wjt_ref[2*C:,:],x1)+col(5)
    qkv_s[2*C:,:]=v.astype(BF)
    vn_s[...]=v.T.astype(BF)
    pi=lax.broadcasted_iota(jnp.int32,(BLK,BLK),0); qi=lax.broadcasted_iota(jnp.int32,(BLK,BLK),1)
    wq=jnp.where(pi<4,jnp.where((qi&3)==pi,0.0,-1e30),jnp.where(pi==4,-1e9*1.4426950408889634,0.0)).astype(BF)
    wq=jnp.concatenate([wq,wq],axis=1)
    wps=[]
    for b in range(rep):
        lv=jnp.broadcast_to(mask_ref[b].astype(F32),(BLK,BLK)).T
        wps.append(jnp.where(qi<4,jnp.where((pi&3)==qi,1.0,0.0),jnp.where(qi==4,1.0-lv,0.0)).astype(BF))
    z=jnp.zeros((HD,BLK),BF)
    def ex(part,i):
        return jnp.concatenate([part if t==i else z for t in range(4)],axis=0)
    tasks=[(b,g,hp*2) for b in range(rep) for g in range(3) for hp in range(2)]
    S={};A={}
    def f_s(t):
        b,g,h0=t; cs=slice(b*BLK,(b+1)*BLK)
        qs=[ex(qkv_s[g*128+i*32:g*128+(i+1)*32,cs],i) for i in (h0,h0+1)]
        S[t]=nn(jnp.concatenate([kn_s[cs,g*128:(g+1)*128],wps[b]],axis=1),jnp.concatenate([jnp.concatenate(qs,axis=1),wq],axis=0))
    def f_a(t):
        b,g,h0=t; cs=slice(b*BLK,(b+1)*BLK)
        s=S.pop(t)
        m=jnp.max(s,axis=0,keepdims=True)
        e=jnp.exp2(s-m)
        inv=1.0/jnp.sum(e,axis=0,keepdims=True)
        a=e.astype(BF)
        for i in range(2):
            a_s[g*4+h0+i,:,cs]=a[:,i*128:(i+1)*128]
            inv_s[g*4+h0+i:g*4+h0+i+1,cs]=inv[:,i*128:(i+1)*128]
        A[t]=(a,inv)
    def f_o(t):
        b,g,h0=t; cs=slice(b*BLK,(b+1)*BLK)
        a,inv=A.pop(t)
        for i in range(2):
            h=g*4+h0+i
            o_s[h*32:(h+1)*32,cs]=nn(qkv_s[2*C+h*32:2*C+(h+1)*32,cs],a[:,i*128:(i+1)*128])*inv[:,i*128:(i+1)*128]
    skew([f_s,f_a,f_o],tasks)
    ob=o_s[...].astype(BF)
    ob_s[...]=ob
    secondT=first_s[...]+(nn(wot_ref[...],ob)+col(6))
    second_s[...]=secondT
    xh2,rs2=ln(secondT)
    x2=(xh2*col(7)+col(8)).astype(BF)
    x_s[1]=x2
    dyTb=dyt_ref[...]
    FC=512
    c0=0.7978845608028654; c1=0.044715
    HH={};PP={}
    def g_h(f):
        fs=slice(f*FC,(f+1)*FC)
        HH[f]=(nn(wht_ref[fs,:],x2),nn(wf_ref[fs,:],dyTb))
    def g_g(f):
        fs=slice(f*FC,(f+1)*FC)
        hb=vb_ref[9*C+f*FC:9*C+(f+1)*FC,:]
        hb=jnp.concatenate([hb]*rep,axis=1)
        h,da=HH.pop(f)
        h=h+hb
        h2=h*h
        t=jnp.tanh(h*(c0+(c0*c1)*h2))
        p=0.5+0.5*t
        act=(h*p).astype(BF)
        dg=p*(1.0+h*(1.0-p)*(2*c0+(6*c0*c1)*h2))
        dpb=(da*dg).astype(BF)
        hb_ref[fs,:]+=fold(dpb.astype(F32))
        PP[f]=(act,dpb)
    def g_o(f):
        fs=slice(f*FC,(f+1)*FC)
        act,dpb=PP.pop(f)
        o=nn(wft_ref[:,fs],act)
        d=nn(wh_ref[:,fs],dpb)
        if f==0:
            acc_s[...]=o; dx_s[...]=d
        else:
            acc_s[...]+=o; dx_s[...]+=d
        gf_ref[:,fs]+=nt(dyTb,act)
        gh_ref[:,fs]+=nt(x2,dpb)
    skew([g_h,g_g,g_o],list(range(F//FC)))
    outT=second_s[...]+(acc_s[...]+col(15-2))
    out_ref[...]=outT.T.astype(BF)
    def ln_back(x,dx,gain,vi):
        xh,rs=ln(x)
        vs_ref[vi]+=fold(dx*xh)
        vs_ref[vi+1]+=fold(dx)
        dh=dx*gain
        m1=jnp.mean(dh,axis=0,keepdims=True)
        m2=jnp.mean(dh*xh,axis=0,keepdims=True)
        return rs*(dh-m1-xh*m2)
    dsec=dyt_ref[...].astype(F32)+ln_back(second_s[...],dx_s[...],col(7),0)
    second_s[...]=dsec
    dbr=dsec.astype(BF)
    vs_ref[2]+=fold(dbr.astype(F32))
    go_ref[...]+=nt(ob_s[...],dbr)
    dat=nn(wo_ref[...],dbr)
    for h in range(HEADS):
        hs=slice(h*32,(h+1)*32)
        dob_s[hs,:]=(dat[hs,:]*inv_s[h:h+1,:]).astype(BF)
    D={};G={}
    def b_d(t):
        b,g,h0=t; cs=slice(b*BLK,(b+1)*BLK)
        ds=[ex(dob_s[g*128+i*32:g*128+(i+1)*32,cs],i) for i in (h0,h0+1)]
        D[t]=nn(vn_s[cs,g*128:(g+1)*128],jnp.concatenate(ds,axis=1))
    def b_s(t):
        b,g,h0=t; cs=slice(b*BLK,(b+1)*BLK)
        dA=D.pop(t)
        out=[]
        for i in range(2):
            h=g*4+h0+i; hs=slice(h*32,(h+1)*32)
            delta=jnp.sum(dob_s[hs,cs].astype(F32)*o_s[hs,cs],axis=0,keepdims=True)
            out.append(a_s[h,:,cs]*(dA[:,i*128:(i+1)*128]-delta).astype(BF))
        G[t]=out
    def b_v(t):
        b,g,h0=t; cs=slice(b*BLK,(b+1)*BLK)
        for i in range(2):
            h=g*4+h0+i; hs=slice(h*32,(h+1)*32)
            dqkv_s[2*C+h*32:2*C+(h+1)*32,cs]=nt(dob_s[hs,cs],a_s[h,:,cs]).astype(BF)
    def b_q(t):
        b,g,h0=t; cs=slice(b*BLK,(b+1)*BLK)
        lrow=live_row[:,cs]
        out=G.pop(t)
        for i in range(2):
            h=g*4+h0+i; hs=slice(h*32,(h+1)*32); ds=out[i]
            dqkv_s[h*32:(h+1)*32,cs]=(nn(qkv_s[C+h*32:C+(h+1)*32,cs],ds)*scale).astype(BF)
            dqkv_s[C+h*32:C+(h+1)*32,cs]=(nt(qkv_s[hs,cs],ds)*(lrow*(scale/c2))).astype(BF)
    skew([b_d,b_v,b_s,b_q],tasks)
    vs_ref[3]+=fold(dqkv_s[0:C,:].astype(F32))
    vs_ref[4]+=fold(dqkv_s[2*C:,:].astype(F32))
    gj_ref[...]+=nt(x_s[0],dqkv_s[...])
    dx1=nn(wj_ref[...],dqkv_s[...])
    dfT=second_s[...]+ln_back(first_s[...],dx1,col(2),5)
    dfirst_ref[...]=dfT.T
    vs_ref[7]+=fold(dfT*(conv_ref[...]*wide(bn_ref[2])-wide(bn_ref[3])))
    vs_ref[8]+=fold(dfT)
    vs_ref[9]+=fold(dyt_ref[...].astype(F32))
    @pl.when(step==pl.num_programs(0)-1)
    def _():
        flat_ref[...]=jnp.zeros_like(flat_ref)
        bns_ref[...]=jnp.concatenate([lane_sums(vs_ref[i]) for i in (7,8,9)]+[jnp.zeros((5,C),F32)],axis=0)
        for vi,row in ((0,21),(1,24),(2,18),(3,12),(4,15),(5,6),(6,9)):
            for i in range(3):
                flat_ref[pl.ds(row+i,1),:]=jnp.sum(vs_ref[vi,i*128:(i+1)*128,:].T,axis=0,keepdims=True)
        for i in range(12):
            flat_ref[pl.ds(27+i,1),:]=jnp.sum(hb_ref[i*128:(i+1)*128,:].T,axis=0,keepdims=True)
        for first,mat in ((ROW_JOINT,gj_ref),(ROW_OUT,go_ref),(ROW_HIDDEN,gh_ref)):
            rows,cols=mat.shape
            per=cols//128
            for k in range(per):
                for r in range(0,rows,C):
                    flat_ref[pl.ds(first+r*per+k,C,stride=per),:]=mat[r:r+C,k*128:(k+1)*128]
        for k in range(3):
            flat_ref[pl.ds(ROW_FINAL+k,F,stride=3),:]=gf_ref[k*128:(k+1)*128,:].T
        for i in range(grads_ref.shape[0]*8):
            part=flat_ref[i*shard:(i+1)*shard,:]
            pad=grads_ref.shape[-2]-shard
            grads_ref[i//8,(i//4)%2,(i//2)%2,i%2]=jnp.concatenate([part,jnp.zeros((pad,128),F32)],axis=0).astype(BF)


def middle(conv,nodes,dy,mask3,stats,rows,gathered,shard):
    n=conv.shape[1]
    across=pl.BlockSpec((C,T),lambda i:(0,i))
    down=rows_of(C,T)
    flat_rows=gathered.shape[0]*8*shard
    in_specs=[across,across,across,pl.BlockSpec((T//128,1,128),lambda i:(i,0,0)),whole(*stats.shape),whole(*rows.shape),whole(*gathered.shape)]
    outs=[((n,C),BF,down),((n,C),F32,down),(gathered.shape,BF,whole(*gathered.shape)),((8,C),F32,whole(8,C))]
    mats=[]
    for shape in ((C,3*C),(C,C),(C,F),(F,C)): mats+=[(shape,BF),(shape[::-1],BF)]
    scr=[pltpu.VMEM(s,d) for s,d in [((flat_rows,128),F32),((4,C,128),F32),((ROW_CONV*128,128),F32)]+mats+[((C,3*C),F32),((C,C),F32),((C,F),F32),((C,F),F32),((10,C,128),F32),((F,128),F32),((C,T),F32),((C,T),F32),((3*C,T),BF),((T,C),BF),((T,C),BF),((HEADS,BLK,T),BF),((C,T),F32),((C,T),BF),((16,T),F32),((C,T),BF),((3*C,T),BF),((2,C,T),BF),((C,T),F32),((C,T),F32)]]
    return pl.pallas_call(functools.partial(mid_kernel,shard),grid=(n//T,),in_specs=in_specs,out_specs=[o[2] for o in outs],
      out_shape=[jax.ShapeDtypeStruct(o[0],o[1]) for o in outs],scratch_shapes=scr,
      compiler_params=VMEM)(conv,nodes,dy,mask3,stats,rows,gathered)


def shards(nodes_in, out_grad, neighbours, node_mask, master, first_moment, second_moment):
    n = nodes_in.shape[0]
    count, cores = lax.axis_size(AXES), lax.axis_size("grp")
    shard = master.shape[0] // 128
    mask3 = node_mask.reshape(n // 128, 1, 128)
    near = neighbours.T
    conv_t, conv, nodes_t, dy_t, gathered, first_rows, stats = convolve(
        near, nodes_in, out_grad, mask3, master.reshape(shard, 128), count, cores
    )
    output, delta_first, grads, norm_sums = middle(conv_t, nodes_t, dy_t, mask3, stats, first_rows, gathered, shard)
    node_grad, shard_delta, bias_total = convolve_back(
        near, delta_first, conv, nodes_in, mask3, norm_sums, stats, first_rows, grads, shard, count, cores
    )
    shard_delta = shard_delta.reshape(-1)
    position = lax.axis_index(AXES) * master.shape[0] + lax.iota(jnp.int32, master.shape[0])
    step_rate = jnp.where(position < 10 * C + F, 0.2, 0.03)
    new_first = 0.9 * first_moment + 0.1 * shard_delta
    new_second = 0.95 * second_moment + 0.05 * shard_delta * shard_delta
    first_hat = new_first / (1.0 - 0.9**STEP)
    second_hat = new_second / (1.0 - 0.95**STEP)
    new_master = master - step_rate * (first_hat / (jnp.sqrt(second_hat) + 1e-08) + 0.01 * master)
    return (
        output,
        node_grad.astype(F32),
        new_master,
        new_first,
        new_second,
        new_master.astype(BF),
        bias_total.reshape(-1),
    )


def solution(mesh):
    rows, flat = P(AXES, None), P(AXES)
    return jax.shard_map(
        shards,
        mesh=mesh,
        in_specs=(rows, rows, rows, flat, flat, flat, flat),
        out_specs=(rows, rows, flat, flat, flat, flat, P()),
        check_vma=False,
    )
```

```python
import functools

import jax
import jax.numpy as jnp
from jax import lax
from jax.experimental import pallas as pl
from jax.experimental.pallas import tpu as pltpu
from jax.sharding import PartitionSpec as P

C = 384
HEADS = 12
HD = 32
F = 1536
HALO = 64
STEP = 5
EPS = 1e-5
AXES = ("rows", "grp")
F32 = jnp.float32
BF = jnp.bfloat16

BLK = 128
T = 512
TB = 512
ROW_CONV = (10 * C + F) // 128
ROW_JOINT = ROW_CONV + 27 * C // 128
ROW_OUT = ROW_JOINT + C * 3 * C // 128
ROW_HIDDEN = ROW_OUT + C * C // 128
ROW_FINAL = ROW_HIDDEN + C * F // 128
ROW_END = ROW_FINAL + C * F // 128
VMEM = pltpu.CompilerParams(vmem_limit_bytes=60 * 1024 * 1024)


def nn(a, b):
    return jnp.dot(a, b, preferred_element_type=F32)


def nt(a, b):
    return lax.dot_general(a, b, (((1,), (1,)), ((), ())), preferred_element_type=F32)


def whole(*shape):
    return pl.BlockSpec(shape, lambda i: (0,) * len(shape), pipeline_mode=pl.Buffered(1))


def skew(stages, tasks):
    for i in range(len(tasks) + len(stages) - 1):
        for k, stage in enumerate(stages):
            if 0 <= i - k < len(tasks):
                stage(tasks[i - k])


def along_sublanes(row):
    parts = [row[:, i : i + 128] for i in range(0, row.shape[1], 128)]
    return jnp.concatenate([jnp.broadcast_to(p, (128, 128)).T for p in parts], axis=0)


def lane_sums(value):
    parts = [value[i : i + 128, :].T for i in range(0, value.shape[0], 128)]
    return jnp.concatenate([jnp.sum(p, axis=0, keepdims=True) for p in parts], axis=1)


def rows_of(width, size):
    return pl.BlockSpec((size, width), lambda i: (i, 0))


MESH = pl.DeviceIdType.MESH


def CUTS_GATHER(nh):
    return [1] * nh + [3, 7]


def round_up(value, step):
    return -(-value // step) * step


def my_place():
    return lax.axis_index("rows") * lax.axis_size("grp") + lax.axis_index("grp")


def device(place, cores):
    return (place // cores, place % cores)


def stages_of(count):
    out, stride = [], 1
    while stride < count:
        size = min(8, count // stride)
        out.append((stride, size))
        stride *= size
    return out


def others(me, stride, size):
    mine = (me // stride) % size
    return mine, [(k, me + ((mine + k) % size - mine) * stride) for k in range(1, size)]


def greet(partners, cores):
    barrier = pltpu.get_barrier_semaphore()
    for place in partners:
        pl.semaphore_signal(barrier, inc=1, device_id=device(place, cores), device_id_type=MESH)
    pl.semaphore_wait(barrier, len(partners))


def send(source, target, send_sem, recv_sem, place, cores):
    return pltpu.make_async_remote_copy(
        src_ref=source,
        dst_ref=target,
        send_sem=send_sem,
        recv_sem=recv_sem,
        device_id=device(place, cores),
        device_id_type=MESH,
    )


def all_sum(value, me, count, cores, slots, send_sems, recv_sems, beside=None):
    for s, (stride, size) in enumerate(stages_of(count)):
        mine, partners = others(me, stride, size)
        slots[s, mine] = value
        copies = [
            send(slots.at[s, mine], slots.at[s, mine], send_sems.at[s, k], recv_sems.at[s, k], place, cores)
            for k, place in partners
        ]
        for copy in copies:
            copy.start()
        if beside is not None:
            beside(s)
        for copy in copies:
            copy.wait()
        value = slots[s, 0]
        for i in range(1, size):
            value = value + slots[s, i]
    return value


def sum_scratch(count, rows, width):
    n = len(stages_of(count))
    return [
        pltpu.VMEM((n, 8, rows, width), F32),
        pltpu.SemaphoreType.DMA((n, 8)),
        pltpu.SemaphoreType.DMA((n, 8)),
    ]


def conv_kernel(count, cores, owners, near_ref, nodes_ref, dy_ref, mask_ref, master_ref,
                convt_ref, conv_ref, nodest_ref, dyt_ref, gathered_ref, first_ref, stats_ref,
                ext, extt, dy_s, early, weight, sums, own_s, local_sem, halo_send, halo_recv, e_send, e_recv, g_send,
                g_recv, slots, s_send, s_recv):
    step = pl.program_id(0)
    steps = pl.num_programs(0)
    block = (step + 1) % steps
    n = nodes_ref.shape[0]
    shard = master_ref.shape[0]
    padded = gathered_ref.shape[-2]
    half = padded // 2
    e_rows = early.shape[1]
    me = my_place()
    low, high = me % 8, me // 8
    y, x, g = low // 4, (low // 2) % 2, low % 2
    highs = stages_of(count // 8)
    left, right = (me + count - 1) % count, (me + 1) % count

    local = pltpu.make_async_copy(nodes_ref, ext.at[pl.ds(HALO, n)], local_sem.at[0])
    keep = pltpu.make_async_copy(own_s, gathered_ref.at[high, y, x, g], local_sem.at[1])
    local_dy = pltpu.make_async_copy(dy_ref, dy_s, local_sem.at[2])

    def turn_dy(k):
        at = pl.ds(pl.multiple_of(k * BLK, BLK), BLK)
        dyt_ref[:, at] = dy_s[at, :].T
        return 0

    def turn(k):
        at = pl.ds(pl.multiple_of(k * BLK, BLK), BLK)
        extt[:, at] = ext[at, :].T
        return 0
    to_left = send(nodes_ref.at[pl.ds(0, HALO)], ext.at[pl.ds(HALO + n, HALO)], halo_send.at[0], halo_recv.at[0], left, cores)
    to_right = send(nodes_ref.at[pl.ds(n - HALO, HALO)], ext.at[pl.ds(0, HALO)], halo_send.at[1], halo_recv.at[1], right, cores)

    def high_copies(s):
        stride, size = highs[s]
        mine, partners = others(high, stride, size)
        own = gathered_ref.at[pl.ds(high // stride * stride, stride), y, x, g]
        return [
            send(own, own, g_send.at[s, k], g_recv.at[s, k], place * 8 + low, cores)
            for k, place in partners
        ]

    nh = len(highs)
    y_place, x_place, g_place = me + 4 - 8 * y, me + 2 - 4 * x, me + 1 - 2 * g

    def quad_copies(t):
        top, bottom = pl.ds(0, half), pl.ds(half, half)
        if t == 0:
            a = gathered_ref.at[:, y, x, g, top]
            b = gathered_ref.at[:, y, x, g, bottom]
            to_a, to_b = y_place, x_place
        else:
            a = gathered_ref.at[:, :, x, g, top]
            b = gathered_ref.at[:, y, :, g, bottom]
            to_a, to_b = x_place, y_place
        s = nh + t
        return [send(a, a, g_send.at[s, 0], g_recv.at[s, 0], to_a, cores), send(b, b, g_send.at[s, 1], g_recv.at[s, 1], to_b, cores)]

    def core_copies():
        own = gathered_ref.at[:, :, :, g]
        return [send(own, own, g_send.at[nh + 2, 0], g_recv.at[nh + 2, 0], g_place, cores)]

    plan = [functools.partial(high_copies, s) for s in range(nh)]
    plan += [functools.partial(quad_copies, 0), functools.partial(quad_copies, 1), core_copies]
    cuts = CUTS_GATHER(nh)

    @pl.when(step == 0)
    def _():
        local.start()
        local_dy.start()
        sums[...] = jnp.zeros_like(sums)
        own = jnp.concatenate([master_ref[...], jnp.zeros((padded - shard, 128), F32)], axis=0).astype(BF)
        own_s[...] = own
        keep.start()
        wide = [h for h in range(1, count // 8)]
        partners = [left, right]
        partners += [(high + h) % (count // 8) * 8 + low for h in wide]
        partners += [place for _, place in others(me, 1, 8)[1]]
        greet(partners, cores)
        early_copies = []
        for o in range(owners):
            up = [send(early.at[o], early.at[o], e_send.at[o, 8 + h], e_recv.at[o, 0], h * 8 + o, cores) for h in wide]
            out = [
                send(early.at[o], early.at[o], e_send.at[o, k], e_recv.at[o, 1], me + k - o, cores)
                for k in range(8) if k != o
            ]
            early_copies.append((up, out))

            @pl.when(low == o)
            def _(o=o, up=up, out=out):
                @pl.when(high == 0)
                def _():
                    early[o] = own[:e_rows]
                    for copy in up:
                        copy.start()
                @pl.when(high > 0)
                def _():
                    send(early.at[o], early.at[o], e_send.at[o, 8], e_recv.at[o, 0], left, cores).wait_recv()
                for copy in out:
                    copy.start()
        to_left.start()
        to_right.start()
        keep.wait()
        for copy in plan[0]():
            copy.start()
        local.wait()
        lax.fori_loop(1, n // BLK, lambda k, _: turn(k), 0)
        for o in range(owners):
            @pl.when(low != o)
            def _():
                send(early.at[o], early.at[o], e_send.at[o, 8], e_recv.at[o, 1], left, cores).wait_recv()
        for o in range(owners):
            rows = min(shard, e_rows)
            first_ref[pl.ds(o * shard, rows), :] = early[o].astype(F32)[:rows]
        table = jnp.concatenate([first_ref[pl.ds(ROW_CONV + k, 27, stride=3), :] for k in range(3)], axis=1)
        table = jnp.concatenate([table, jnp.zeros((BLK - 27, C), F32)], axis=0).T.astype(BF)
        entry = lax.broadcasted_iota(jnp.int32, (BLK, 2 * BLK), 0)
        second = lax.broadcasted_iota(jnp.int32, (BLK, 2 * BLK), 1) // BLK
        for j in range(0, 27, 2):
            both = nn(table, jnp.where(entry == j + second, 1.0, 0.0).astype(BF))
            weight[j] = both[:, :BLK]
            if j + 1 < 27:
                weight[j + 1] = both[:, BLK:]
        for o, (up, out) in enumerate(early_copies):
            @pl.when(low == o)
            def _(up=up, out=out):
                @pl.when(high == 0)
                def _():
                    for copy in up:
                        copy.wait_send()
                for copy in out:
                    copy.wait_send()

    for s in range(len(plan) - 1):
        @pl.when(step == cuts[s])
        def _(s=s):
            for copy in plan[s]():
                copy.wait()
            for copy in plan[s + 1]():
                copy.start()

    @pl.when(step == steps - 2)
    def _():
        to_left.wait()
        to_right.wait()
        turn(0)
        turn(n // BLK)

    sub = lax.broadcasted_iota(jnp.int32, (2 * BLK, BLK), 0).astype(F32).astype(BF)
    one, zero = jnp.ones((), BF), jnp.zeros((), BF)
    pairs = [(j, j + 1) for j in range(0, 12, 2)] + [(12, 14)] + [(j, j + 1) for j in range(15, 27, 2)]
    at = pl.multiple_of(block * T, T)
    lane = lax.broadcasted_iota(jnp.int32, (27, BLK), 1)
    places, totals, picks, comes = {}, {}, {}, {}
    for b in range(T // BLK):
        near = near_ref[:, b * BLK : (b + 1) * BLK]
        places[b] = jnp.where(near < 0, -1, near + lane).astype(F32).astype(BF)

    def pick(task):
        b, q = task
        if q == 0:
            center = ext[pl.ds(at + b * BLK + HALO, BLK), :].astype(F32).T
            nodest_ref[:, b * BLK : (b + 1) * BLK] = center.astype(BF)
            totals[b] = center * weight[13]
        picks[task] = jnp.concatenate(
            [jnp.where(places[b][j : j + 1, :] == sub, one, zero) for j in pairs[q]], axis=1
        )

    def multiply(task):
        b, q = task
        comes[task] = nn(extt[:, pl.ds(at + b * BLK, 2 * BLK)], picks.pop(task))

    def add(task):
        b, q = task
        come = comes.pop(task)
        totals[b] = totals[b] + (come[:, :BLK] * weight[pairs[q][0]] + come[:, BLK:] * weight[pairs[q][1]])
        if q == len(pairs) - 1:
            total = totals.pop(b)
            convt_ref[:, b * BLK : (b + 1) * BLK] = total
            conv_ref[b * BLK : (b + 1) * BLK, :] = total.T.astype(BF)
            live = mask_ref[b].astype(F32)
            kept = total * live
            sums[0] += kept
            sums[1] += kept * total
            sums[2, 0:1] += live

    skew([pick, multiply, add], [(b, q) for b in range(T // BLK) for q in range(len(pairs))])

    @pl.when(step == steps - 1)
    def _():
        rows = [lane_sums(sums[i]) for i in range(2)]
        rows += [jnp.broadcast_to(jnp.sum(sums[2, 0:1], axis=1, keepdims=True), (1, C))]
        rows = jnp.concatenate(rows + [jnp.zeros((5, C), F32)], axis=0)
        local_dy.wait()
        cut = len(stages_of(count))

        def beside(s):
            lax.fori_loop(n // BLK * s // cut, n // BLK * (s + 1) // cut, lambda k, _: turn_dy(k), 0)

        stats_ref[...] = all_sum(rows, me, count, cores, slots, s_send, s_recv, beside)
        for copy in plan[-1]():
            copy.wait()


def convolve(near, nodes, dy, mask3, master, count, cores):
    n = nodes.shape[0]
    steps = n // T
    shard = master.shape[0]
    padded = round_up(shard, 32)
    owners = -(-ROW_JOINT // shard)
    e_rows = min(padded, round_up(ROW_JOINT, 16))
    down = pl.BlockSpec((T, C), lambda i: ((i + 1) % steps, 0))
    across = pl.BlockSpec((C, T), lambda i: (0, (i + 1) % steps))
    anywhere = pl.BlockSpec(memory_space=pl.ANY)
    stages = len(stages_of(count // 8)) + 3
    first_rows = round_up((owners - 1) * shard + e_rows, 8)
    return pl.pallas_call(
        functools.partial(conv_kernel, count, cores, owners),
        grid=(steps,),
        in_specs=[
            pl.BlockSpec((27, T), lambda i: (0, (i + 1) % steps)),
            anywhere,
            anywhere,
            pl.BlockSpec((T // BLK, 1, 128), lambda i: ((i + 1) % steps, 0, 0)),
            whole(shard, 128),
        ],
        out_specs=[across, down, across, whole(C, n), anywhere, whole(first_rows, 128), whole(8, C)],
        out_shape=[
            jax.ShapeDtypeStruct((C, n), F32),
            jax.ShapeDtypeStruct((n, C), BF),
            jax.ShapeDtypeStruct((C, n), BF),
            jax.ShapeDtypeStruct((C, n), BF),
            jax.ShapeDtypeStruct((count // 8, 2, 2, 2, padded, 128), BF),
            jax.ShapeDtypeStruct((first_rows, 128), F32),
            jax.ShapeDtypeStruct((8, C), F32),
        ],
        scratch_shapes=[
            pltpu.VMEM((n + 2 * HALO, C), BF),
            pltpu.VMEM((C, n + 2 * HALO), BF),
            pltpu.VMEM((n, C), BF),
            pltpu.VMEM((owners, e_rows, 128), BF),
            pltpu.VMEM((27, C, 128), F32),
            pltpu.VMEM((3, C, 128), F32),
            pltpu.VMEM((padded, 128), BF),
            pltpu.SemaphoreType.DMA((3,)),
            pltpu.SemaphoreType.DMA((2,)),
            pltpu.SemaphoreType.DMA((2,)),
            pltpu.SemaphoreType.DMA((owners, 8 + count // 8)),
            pltpu.SemaphoreType.DMA((owners, 2)),
            pltpu.SemaphoreType.DMA((stages, 8)),
            pltpu.SemaphoreType.DMA((stages, 8)),
        ]
        + sum_scratch(count, 8, C),
        compiler_params=pltpu.CompilerParams(
            vmem_limit_bytes=60 * 1024 * 1024, collective_id=0, has_side_effects=True
        ),
    )(near, nodes, dy, mask3, master)


def conv_back_kernel(count, cores, owners, near_hbm, first_hbm, conv_hbm, x_ref, mask_ref, sums_ref, stats_ref,
                     rows_ref, grads_ref,
                     grad_ref, total_s, bias_out,
                     near, ext, delta, conv, weight, dw, kept, r1, r2, r3, r4, local_sem, halo_send, halo_recv, g_send,
                     g_recv, slots, s_send, s_recv, w_own, w_slots, w_high, w_sem, w_recv, w_recv_high, early_s, factors, w_sum):
    step = pl.program_id(0)
    steps = pl.num_programs(0)
    block = (step + 1) % steps
    n = first_hbm.shape[0]
    shard = total_s.shape[0]
    padded = grads_ref.shape[-2]
    half = padded // 2
    me = my_place()
    low, high = me % 8, me // 8
    y, x, g = low // 4, (low // 2) % 2, low % 2
    highs = stages_of(count // 8)[::-1]
    nh = len(highs)
    left, right = (me + count - 1) % count, (me + 1) % count
    y_place, x_place, g_place = me + 4 - 8 * y, me + 2 - 4 * x, me + 1 - 2 * g
    top, bottom = pl.ds(0, half), pl.ds(half, half)

    locals_ = [
        pltpu.make_async_copy(first_hbm, delta, local_sem.at[0]),
        pltpu.make_async_copy(conv_hbm, conv, local_sem.at[1]),
        pltpu.make_async_copy(near_hbm, near.at[:, pl.ds(BLK, n)], local_sem.at[2]),
        pltpu.make_async_copy(grads_ref.at[:, :, :, g], kept, local_sem.at[3]),
    ]
    near_halo = [
        send(near_hbm.at[:, pl.ds(0, BLK)], near.at[:, pl.ds(BLK + n, BLK)], halo_send.at[0], halo_recv.at[0], left, cores),
        send(near_hbm.at[:, pl.ds(n - BLK, BLK)], near.at[:, pl.ds(0, BLK)], halo_send.at[1], halo_recv.at[1], right, cores),
    ]
    delta_halo = [
        send(ext.at[pl.ds(HALO, HALO)], ext.at[pl.ds(HALO + n, HALO)], halo_send.at[2], halo_recv.at[2], left, cores),
        send(ext.at[pl.ds(n, HALO)], ext.at[pl.ds(0, HALO)], halo_send.at[3], halo_recv.at[3], right, cores),
    ]

    blocks, per = n // BLK, TB // BLK

    def make_rows(i):
        at = pl.ds(pl.multiple_of(i * BLK, BLK), BLK)
        live = jnp.broadcast_to(mask_ref[i].astype(F32), (BLK, BLK)).T
        live = jnp.concatenate([live] * 3, axis=1)
        value = delta[at, :] * factors[0:1, :] + live * (factors[1:2, :] + factors[2:3, :] * conv[at, :].astype(F32))
        ext[pl.ds(pl.multiple_of(i * BLK + HALO, HALO), BLK), :] = value.astype(BF)
        return 0

    def core_copies():
        return [send(grads_ref.at[:, :, :, 1 - g], r1, g_send.at[0, 0], g_recv.at[0, 0], g_place, cores)]

    def core_add():
        def body(i, _):
            kept[i // 4, (i // 2) % 2, i % 2] = (
                kept[i // 4, (i // 2) % 2, i % 2].astype(F32) + r1[i // 4, (i // 2) % 2, i % 2].astype(F32)
            ).astype(BF)
            return 0
        lax.fori_loop(0, count // 2, body, 0)

    def quad_copies_0():
        return [
            send(kept.at[:, :, 1 - x, top], r2.at[0], g_send.at[1, 0], g_recv.at[1, 0], x_place, cores),
            send(kept.at[:, 1 - y, :, bottom], r2.at[1], g_send.at[1, 1], g_recv.at[1, 1], y_place, cores),
        ]

    def quad_add_0():
        def body(i, _):
            h, w = i // 2, i % 2
            kept[h, w, x, top] = (
                kept[h, w, x, top].astype(F32) + r2[0, h, w].astype(F32)
            ).astype(BF)
            kept[h, y, w, bottom] = (
                kept[h, y, w, bottom].astype(F32) + r2[1, h, w].astype(F32)
            ).astype(BF)
            return 0
        lax.fori_loop(0, count // 4, body, 0)

    def quad_copies_1():
        return [
            send(kept.at[:, 1 - y, x, top], r3.at[0], g_send.at[2, 0], g_recv.at[2, 0], y_place, cores),
            send(kept.at[:, y, 1 - x, bottom], r3.at[1], g_send.at[2, 1], g_recv.at[2, 1], x_place, cores),
        ]

    def quad_add_1():
        def body(h, _):
            kept[h, y, x, top] = (
                kept[h, y, x, top].astype(F32) + r3[0, h].astype(F32)
            ).astype(BF)
            kept[h, y, x, bottom] = (
                kept[h, y, x, bottom].astype(F32) + r3[1, h].astype(F32)
            ).astype(BF)
            return 0
        lax.fori_loop(0, count // 8, body, 0)

    bases = []
    base = 0
    for stride, size in highs:
        bases.append(base)
        base += (size - 1) * stride

    def high_copies(s):
        stride, size = highs[s]
        mine, partners = others(high, stride, size)
        out = []
        for k, place in partners:
            source = kept.at[pl.ds(place // stride * stride, stride), y, x]
            target = r4.at[pl.ds(bases[s] + (k - 1) * stride, stride)]
            out.append(send(source, target, g_send.at[3 + s, k], g_recv.at[3 + s, k], place * 8 + low, cores))
        return out

    def high_add(s):
        stride, size = highs[s]
        start = high // stride * stride
        def body(i, _):
            value = kept[start + i, y, x].astype(F32)
            for k in range(size - 1):
                value = value + r4[bases[s] + k * stride + i].astype(F32)
            if s == nh - 1:
                total_s[...] = value[:shard]
            else:
                kept[start + i, y, x] = value.astype(BF)
            return 0
        lax.fori_loop(0, stride, body, 0)

    plan = [(core_copies, core_add), (quad_copies_0, quad_add_0), (quad_copies_1, quad_add_1)]
    plan += [(functools.partial(high_copies, s), functools.partial(high_add, s)) for s in range(nh)]
    cuts = CUTS_SCATTER(nh)

    @pl.when(step == 0)
    def _():
        for copy in locals_:
            copy.start()
        dw[...] = jnp.zeros_like(dw)
        partners = [left, right]
        partners += [(high + h) % (count // 8) * 8 + low for h in range(1, count // 8)]
        partners += [place for _, place in others(me, 1, 8)[1]]
        greet(partners, cores)
        def beside(s):
            if s == 0:
                for copy in plan[0][0]() + near_halo:
                    copy.start()
        total = all_sum(sums_ref[...], me, count, cores, slots, s_send, s_recv, beside)
        gain_total, shift_total = total[0:1], total[1:2]
        bias_out[...] = jnp.concatenate([total[2:3, i * 128 : (i + 1) * 128] for i in range(3)], axis=0)
        early_s[...] = jnp.zeros_like(early_s)
        for i in range(3):
            early_s[i : i + 1, :] = gain_total[:, i * 128 : (i + 1) * 128]
            early_s[3 + i : 4 + i, :] = shift_total[:, i * 128 : (i + 1) * 128]
            early_s[ROW_CONV - 3 + i : ROW_CONV - 2 + i, :] = total[2:3, i * 128 : (i + 1) * 128]
        for k in range(3):
            weight[:, k * 128 : (k + 1) * 128] = rows_ref[pl.ds(ROW_CONV + k, 27, stride=3), :]
        gain = jnp.concatenate([rows_ref[i : i + 1, :] for i in range(3)], axis=1)
        live_total = stats_ref[2:3]
        average = stats_ref[0:1] / live_total
        variance = stats_ref[1:2] / live_total - average * average
        inverse = lax.rsqrt(variance + EPS)
        delta_variance = -0.5 * inverse * inverse * inverse * (gain * gain_total / inverse)
        delta_average = -gain * shift_total * inverse - 2.0 * average * delta_variance
        a = gain * inverse
        b = delta_average / live_total
        c = 2.0 * delta_variance / live_total
        for copy in locals_:
            copy.wait()

        factors[0:1, :] = a
        factors[1:2, :] = b
        factors[2:3, :] = c
        make_rows(0)
        make_rows(blocks - 1)
        lax.fori_loop(per - 1, 2 * per + 1, lambda k, _: make_rows(k), 0)
        for copy in delta_halo:
            copy.start()

    for s in range(len(plan)):
        @pl.when(step == cuts[s])
        def _(s=s):
            for copy in plan[s][0]():
                copy.wait()
            plan[s][1]()
            if s + 1 < len(plan):
                for copy in plan[s + 1][0]():
                    copy.start()

    @pl.when(step == steps - 2)
    def _():
        for copy in near_halo + delta_halo:
            copy.wait()

    start = pl.multiple_of(block * TB, TB)
    target = lax.broadcasted_iota(jnp.int32, (BLK, 2 * BLK), 0).astype(F32).astype(BF)
    one, zero = jnp.ones((), BF), jnp.zeros((), BF)
    lane = lax.broadcasted_iota(jnp.int32, (27, 2 * BLK), 1) - BLK
    places, totals, picks, comes, xs = {}, {}, {}, {}, {}
    for b in range(TB // BLK):
        near_w = near[:, pl.ds(start + b * BLK, 3 * BLK)][:, HALO : HALO + 2 * BLK]
        places[b] = jnp.where(near_w < 0, -1, near_w + lane).astype(F32).astype(BF)

    def pick(task):
        b, q = task
        picks[task] = jnp.concatenate(
            [jnp.where(places[b][j : j + 1, :] == target, one, zero) for j in range(3 * q, 3 * q + 3)], axis=0
        )

    def multiply(task):
        b, q = task
        comes[task] = nn(picks.pop(task), ext[pl.ds(start + b * BLK, 2 * BLK), :])

    def add(task):
        b, q = task
        come = comes.pop(task)
        if q == 0:
            xs[b] = x_ref[b * BLK : (b + 1) * BLK, :].astype(F32)
            totals[b] = delta[pl.ds(start + b * BLK, BLK), :]
        for i in range(3):
            j, part = 3 * q + i, come[i * BLK : (i + 1) * BLK]
            totals[b] = totals[b] + part * weight[j : j + 1, :]
            dw[j] += jnp.sum((part * xs[b]).reshape(BLK // 8, 8, C), axis=0)
        if q == 8:
            grad_ref[b * BLK : (b + 1) * BLK, :] = totals.pop(b).astype(BF)

    skew([pick, multiply, add], [(b, q) for b in range(TB // BLK) for q in range(9)])

    for k in range(per):
        i = ((block + 1) * per + 1 + k) % blocks
        make_rows(jnp.where((i == 0) | (i == blocks - 1), blocks - 2, i))

    @pl.when(step == steps - 1)
    def _():
        mine = jnp.concatenate([jnp.sum(dw[...], axis=1), jnp.zeros((5, C), F32)], axis=0)
        w_own[...] = mine.astype(BF)
        to_first = send(w_own, w_slots.at[low], w_sem.at[0], w_recv.at[low], me - low, cores)

        @pl.when(low != 0)
        def _():
            to_first.start()
            to_first.wait_send()

        @pl.when(low == 0)
        def _():
            for k in range(1, 8):
                send(w_own, w_slots.at[k], w_sem.at[0], w_recv.at[k], me + k, cores).wait_recv()
            mine_8 = mine + sum(w_slots[k].astype(F32) for k in range(1, 8))
            w_own[...] = mine_8.astype(BF)

            @pl.when(high != 0)
            def _():
                up = send(w_own, w_high.at[high], w_sem.at[0], w_recv_high.at[high], 0, cores)
                up.start()
                up.wait_send()

            @pl.when(high == 0)
            def _():
                for h in range(1, count // 8):
                    send(w_own, w_high.at[h], w_sem.at[0], w_recv_high.at[h], h * 8, cores).wait_recv()
                mine_all = mine_8 + sum(w_high[h].astype(F32) for h in range(1, count // 8))
                w_own[...] = mine_all.astype(BF)
                w_sum[...] = mine_all
                out = [send(w_own, w_high.at[0], w_sem.at[o], w_recv_high.at[0], o, cores) for o in range(1, owners)]
                for copy in out:
                    copy.start()
                for copy in out:
                    copy.wait_send()

        for o in range(owners):
            @pl.when(me == o)
            def _(o=o):
                if o == 0:
                    sums = w_sum[...]
                else:
                    send(w_own, w_high.at[0], w_sem.at[0], w_recv_high.at[0], 0, cores).wait_recv()
                    sums = w_high[0].astype(F32)
                for k in range(3):
                    early_s[pl.ds(ROW_CONV + k, 27, stride=3), :] = sums[:27, k * 128 : (k + 1) * 128]
                rows = min(shard, early_s.shape[0] - o * shard)
                total_s[0:rows, :] += early_s[o * shard : o * shard + rows, :]


def CUTS_SCATTER(nh):
    return [1, 3, 4] + [4 + 3 * (s + 1) // nh for s in range(nh)]


def convolve_back(near, delta, conv, nodes, mask3, sums, stats, rows, grads, shard, count, cores):
    n = nodes.shape[0]
    steps = n // TB
    padded = grads.shape[-2]
    highs = count // 8
    owners = -(-ROW_JOINT // shard)
    turned = pl.BlockSpec((TB, C), lambda i: ((i + 1) % steps, 0))
    anywhere = pl.BlockSpec(memory_space=pl.ANY)
    r4_rows = sum((size - 1) * stride for stride, size in stages_of(highs))
    return pl.pallas_call(
        functools.partial(conv_back_kernel, count, cores, owners),
        grid=(steps,),
        in_specs=[
            anywhere,
            anywhere,
            anywhere,
            turned,
            whole(*mask3.shape),
            whole(*sums.shape),
            whole(*stats.shape),
            whole(*rows.shape),
            anywhere,
        ],
        out_specs=[turned, whole(shard, 128), whole(3, 128)],
        out_shape=[
            jax.ShapeDtypeStruct((n, C), BF),
            jax.ShapeDtypeStruct((shard, 128), F32),
            jax.ShapeDtypeStruct((3, 128), F32),
        ],
        scratch_shapes=[
            pltpu.VMEM((27, n + 2 * BLK), jnp.int32),
            pltpu.VMEM((n + 2 * HALO, C), BF),
            pltpu.VMEM((n, C), F32),
            pltpu.VMEM((n, C), BF),
            pltpu.VMEM((27, C), F32),
            pltpu.VMEM((27, 8, C), F32),
            pltpu.VMEM((highs, 2, 2, padded, 128), BF),
            pltpu.VMEM((highs, 2, 2, padded, 128), BF),
            pltpu.VMEM((2, highs, 2, padded // 2, 128), BF),
            pltpu.VMEM((2, highs, padded // 2, 128), BF),
            pltpu.VMEM((r4_rows, padded, 128), BF),
            pltpu.SemaphoreType.DMA((4,)),
            pltpu.SemaphoreType.DMA((4,)),
            pltpu.SemaphoreType.DMA((4,)),
            pltpu.SemaphoreType.DMA((3 + len(stages_of(highs)), 8)),
            pltpu.SemaphoreType.DMA((3 + len(stages_of(highs)), 8)),
        ]
        + sum_scratch(count, 8, C)
        + [
            pltpu.VMEM((32, C), BF),
            pltpu.VMEM((8, 32, C), BF),
            pltpu.VMEM((highs, 32, C), BF),
            pltpu.SemaphoreType.DMA((max(owners, 1),)),
            pltpu.SemaphoreType.DMA((8,)),
            pltpu.SemaphoreType.DMA((highs,)),
            pltpu.VMEM((round_up(ROW_JOINT, 8), 128), F32),
            pltpu.VMEM((8, C), F32),
            pltpu.VMEM((32, C), F32),
        ],
        compiler_params=pltpu.CompilerParams(
            vmem_limit_bytes=60 * 1024 * 1024, collective_id=1, has_side_effects=True
        ),
    )(near, delta, conv, nodes, mask3, sums, stats, rows, grads)


def prepare(stats, rows, gathered, shard, flat, norm, spread, mats):
    for i in range(gathered.shape[0] * 8):
        flat[i * shard : (i + 1) * shard, :] = gathered[i // 8, (i // 4) % 2, (i // 2) % 2, i % 2].astype(F32)[:shard]
    for first, out, out_t in mats:
        height, width = out.shape
        per = width // 128
        for k in range(per):
            for r in range(0, height, C):
                piece = flat[pl.ds(first + r * per + k, C, stride=per), :]
                out[r : r + C, k * 128 : (k + 1) * 128] = piece.astype(BF)
                out_t[k * 128 : (k + 1) * 128, r : r + C] = piece.T.astype(BF)
    for i in range(ROW_CONV):
        spread[i * 128 : (i + 1) * 128, :] = jnp.broadcast_to(rows[i : i + 1, :], (128, 128)).T
    gain = jnp.concatenate([rows[i : i + 1, :] for i in range(3)], axis=1)
    shift = jnp.concatenate([rows[3 + i : 4 + i, :] for i in range(3)], axis=1)
    live_total = stats[2:3, :]
    average = stats[0:1, :] / live_total
    variance = stats[1:2, :] / live_total - average * average
    inverse = lax.rsqrt(variance + EPS)
    norm[0] = along_sublanes(inverse * gain)
    norm[1] = along_sublanes(shift - average * inverse * gain)
    norm[2] = along_sublanes(inverse)
    norm[3] = along_sublanes(average * inverse)


def mid_kernel(shard,conv_ref,nodes_ref,dyt_ref,mask_ref,stats_ref,rows_ref,gathered_ref,
    out_ref,dfirst_ref,grads_ref,bns_ref,
    flat_ref,bn_ref,vb_ref,wj_ref,wjt_ref,wo_ref,wot_ref,wh_ref,wht_ref,wf_ref,wft_ref,
    gj_ref,go_ref,gh_ref,gf_ref,vs_ref,hb_ref,first_s,second_s,qkv_s,kn_s,vn_s,a_s,o_s,ob_s,inv_s,dob_s,dqkv_s,x_s,acc_s,dx_s):
    step=pl.program_id(0)
    rep=T//128
    @pl.when(step==0)
    def _():
        for r in (gj_ref,go_ref,gh_ref,gf_ref,vs_ref,hb_ref): r[...]=jnp.zeros_like(r)
        prepare(stats_ref,rows_ref,gathered_ref,shard,flat_ref,bn_ref,vb_ref,
            ((ROW_JOINT,wj_ref,wjt_ref),(ROW_OUT,wo_ref,wot_ref),(ROW_HIDDEN,wh_ref,wht_ref),(ROW_FINAL,wf_ref,wft_ref)))
    def col(i,n=C):
        v=vb_ref[pl.ds(i*C,n),:]
        return jnp.concatenate([v]*rep,axis=1) if rep>1 else v
    def fold(x):
        r=x[:,:128]
        for k in range(1,rep): r=r+x[:,128*k:128*(k+1)]
        return r
    def wide(v): return jnp.concatenate([v]*rep,axis=1)
    firstT=nodes_ref[...].astype(F32)+(conv_ref[...]*wide(bn_ref[0])+wide(bn_ref[1]))
    first_s[...]=firstT
    def ln(x):
        m=jnp.mean(x,axis=0,keepdims=True); c=x-m
        rs=lax.rsqrt(jnp.mean(c*c,axis=0,keepdims=True)+EPS)
        return c*rs, rs
    xh1,rs1=ln(firstT)
    x1=(xh1*col(2)+col(3)).astype(BF)
    x_s[0]=x1
    scale=HD**-0.5
    c2=scale*1.4426950408889634
    live_row=jnp.concatenate([mask_ref[b].astype(F32) for b in range(rep)],axis=1)
    q=(nn(wjt_ref[0:C,:],x1)+col(4))*c2
    qkv_s[0:C,:]=q.astype(BF)
    k=nn(wjt_ref[C:2*C,:],x1)*live_row
    qkv_s[C:2*C,:]=k.astype(BF)
    kn_s[...]=k.T.astype(BF)
    v=nn(wjt_ref[2*C:,:],x1)+col(5)
    qkv_s[2*C:,:]=v.astype(BF)
    vn_s[...]=v.T.astype(BF)
    pi=lax.broadcasted_iota(jnp.int32,(BLK,BLK),0); qi=lax.broadcasted_iota(jnp.int32,(BLK,BLK),1)
    wq=jnp.where(pi<4,jnp.where((qi&3)==pi,0.0,-1e30),jnp.where(pi==4,-1e9*1.4426950408889634,0.0)).astype(BF)
    wq=jnp.concatenate([wq,wq],axis=1)
    wps=[]
    for b in range(rep):
        lv=jnp.broadcast_to(mask_ref[b].astype(F32),(BLK,BLK)).T
        wps.append(jnp.where(qi<4,jnp.where((pi&3)==qi,1.0,0.0),jnp.where(qi==4,1.0-lv,0.0)).astype(BF))
    z=jnp.zeros((HD,BLK),BF)
    def ex(part,i):
        return jnp.concatenate([part if t==i else z for t in range(4)],axis=0)
    tasks=[(b,g,hp*2) for b in range(rep) for g in range(3) for hp in range(2)]
    S={};A={}
    def f_s(t):
        b,g,h0=t; cs=slice(b*BLK,(b+1)*BLK)
        qs=[ex(qkv_s[g*128+i*32:g*128+(i+1)*32,cs],i) for i in (h0,h0+1)]
        S[t]=nn(jnp.concatenate([kn_s[cs,g*128:(g+1)*128],wps[b]],axis=1),jnp.concatenate([jnp.concatenate(qs,axis=1),wq],axis=0))
    def f_a(t):
        b,g,h0=t; cs=slice(b*BLK,(b+1)*BLK)
        s=S.pop(t)
        m=jnp.max(s,axis=0,keepdims=True)
        e=jnp.exp2(s-m)
        inv=1.0/jnp.sum(e,axis=0,keepdims=True)
        a=e.astype(BF)
        for i in range(2):
            a_s[g*4+h0+i,:,cs]=a[:,i*128:(i+1)*128]
            inv_s[g*4+h0+i:g*4+h0+i+1,cs]=inv[:,i*128:(i+1)*128]
        A[t]=(a,inv)
    def f_o(t):
        b,g,h0=t; cs=slice(b*BLK,(b+1)*BLK)
        a,inv=A.pop(t)
        for i in range(2):
            h=g*4+h0+i
            o_s[h*32:(h+1)*32,cs]=nn(qkv_s[2*C+h*32:2*C+(h+1)*32,cs],a[:,i*128:(i+1)*128])*inv[:,i*128:(i+1)*128]
    skew([f_s,f_a,f_o],tasks)
    ob=o_s[...].astype(BF)
    ob_s[...]=ob
    secondT=first_s[...]+(nn(wot_ref[...],ob)+col(6))
    second_s[...]=secondT
    xh2,rs2=ln(secondT)
    x2=(xh2*col(7)+col(8)).astype(BF)
    x_s[1]=x2
    dyTb=dyt_ref[...]
    FC=512
    c0=0.7978845608028654; c1=0.044715
    HH={};PP={}
    def g_h(f):
        fs=slice(f*FC,(f+1)*FC)
        HH[f]=(nn(wht_ref[fs,:],x2),nn(wf_ref[fs,:],dyTb))
    def g_g(f):
        fs=slice(f*FC,(f+1)*FC)
        hb=vb_ref[9*C+f*FC:9*C+(f+1)*FC,:]
        hb=jnp.concatenate([hb]*rep,axis=1)
        h,da=HH.pop(f)
        h=h+hb
        h2=h*h
        t=jnp.tanh(h*(c0+(c0*c1)*h2))
        p=0.5+0.5*t
        act=(h*p).astype(BF)
        dg=p*(1.0+h*(1.0-p)*(2*c0+(6*c0*c1)*h2))
        dpb=(da*dg).astype(BF)
        hb_ref[fs,:]+=fold(dpb.astype(F32))
        PP[f]=(act,dpb)
    def g_o(f):
        fs=slice(f*FC,(f+1)*FC)
        act,dpb=PP.pop(f)
        o=nn(wft_ref[:,fs],act)
        d=nn(wh_ref[:,fs],dpb)
        if f==0:
            acc_s[...]=o; dx_s[...]=d
        else:
            acc_s[...]+=o; dx_s[...]+=d
        gf_ref[:,fs]+=nt(dyTb,act)
        gh_ref[:,fs]+=nt(x2,dpb)
    skew([g_h,g_g,g_o],list(range(F//FC)))
    outT=second_s[...]+(acc_s[...]+col(15-2))
    out_ref[...]=outT.T.astype(BF)
    def ln_back(x,dx,gain,vi):
        xh,rs=ln(x)
        vs_ref[vi]+=fold(dx*xh)
        vs_ref[vi+1]+=fold(dx)
        dh=dx*gain
        m1=jnp.mean(dh,axis=0,keepdims=True)
        m2=jnp.mean(dh*xh,axis=0,keepdims=True)
        return rs*(dh-m1-xh*m2)
    dsec=dyt_ref[...].astype(F32)+ln_back(second_s[...],dx_s[...],col(7),0)
    second_s[...]=dsec
    dbr=dsec.astype(BF)
    vs_ref[2]+=fold(dbr.astype(F32))
    go_ref[...]+=nt(ob_s[...],dbr)
    dat=nn(wo_ref[...],dbr)
    for h in range(HEADS):
        hs=slice(h*32,(h+1)*32)
        dob_s[hs,:]=(dat[hs,:]*inv_s[h:h+1,:]).astype(BF)
    D={};G={}
    def b_d(t):
        b,g,h0=t; cs=slice(b*BLK,(b+1)*BLK)
        ds=[ex(dob_s[g*128+i*32:g*128+(i+1)*32,cs],i) for i in (h0,h0+1)]
        D[t]=nn(vn_s[cs,g*128:(g+1)*128],jnp.concatenate(ds,axis=1))
    def b_s(t):
        b,g,h0=t; cs=slice(b*BLK,(b+1)*BLK)
        dA=D.pop(t)
        out=[]
        for i in range(2):
            h=g*4+h0+i; hs=slice(h*32,(h+1)*32)
            delta=jnp.sum(dob_s[hs,cs].astype(F32)*o_s[hs,cs],axis=0,keepdims=True)
            out.append(a_s[h,:,cs]*(dA[:,i*128:(i+1)*128]-delta).astype(BF))
        G[t]=out
    def b_v(t):
        b,g,h0=t; cs=slice(b*BLK,(b+1)*BLK)
        for i in range(2):
            h=g*4+h0+i; hs=slice(h*32,(h+1)*32)
            dqkv_s[2*C+h*32:2*C+(h+1)*32,cs]=nt(dob_s[hs,cs],a_s[h,:,cs]).astype(BF)
    def b_q(t):
        b,g,h0=t; cs=slice(b*BLK,(b+1)*BLK)
        lrow=live_row[:,cs]
        out=G.pop(t)
        for i in range(2):
            h=g*4+h0+i; hs=slice(h*32,(h+1)*32); ds=out[i]
            dqkv_s[h*32:(h+1)*32,cs]=(nn(qkv_s[C+h*32:C+(h+1)*32,cs],ds)*scale).astype(BF)
            dqkv_s[C+h*32:C+(h+1)*32,cs]=(nt(qkv_s[hs,cs],ds)*(lrow*(scale/c2))).astype(BF)
    skew([b_d,b_v,b_s,b_q],tasks)
    vs_ref[3]+=fold(dqkv_s[0:C,:].astype(F32))
    vs_ref[4]+=fold(dqkv_s[2*C:,:].astype(F32))
    gj_ref[...]+=nt(x_s[0],dqkv_s[...])
    dx1=nn(wj_ref[...],dqkv_s[...])
    dfT=second_s[...]+ln_back(first_s[...],dx1,col(2),5)
    dfirst_ref[...]=dfT.T
    vs_ref[7]+=fold(dfT*(conv_ref[...]*wide(bn_ref[2])-wide(bn_ref[3])))
    vs_ref[8]+=fold(dfT)
    vs_ref[9]+=fold(dyt_ref[...].astype(F32))
    @pl.when(step==pl.num_programs(0)-1)
    def _():
        flat_ref[...]=jnp.zeros_like(flat_ref)
        bns_ref[...]=jnp.concatenate([lane_sums(vs_ref[i]) for i in (7,8,9)]+[jnp.zeros((5,C),F32)],axis=0)
        for vi,row in ((0,21),(1,24),(2,18),(3,12),(4,15),(5,6),(6,9)):
            for i in range(3):
                flat_ref[pl.ds(row+i,1),:]=jnp.sum(vs_ref[vi,i*128:(i+1)*128,:].T,axis=0,keepdims=True)
        for i in range(12):
            flat_ref[pl.ds(27+i,1),:]=jnp.sum(hb_ref[i*128:(i+1)*128,:].T,axis=0,keepdims=True)
        for first,mat in ((ROW_JOINT,gj_ref),(ROW_OUT,go_ref),(ROW_HIDDEN,gh_ref)):
            rows,cols=mat.shape
            per=cols//128
            for k in range(per):
                for r in range(0,rows,C):
                    flat_ref[pl.ds(first+r*per+k,C,stride=per),:]=mat[r:r+C,k*128:(k+1)*128]
        for k in range(3):
            flat_ref[pl.ds(ROW_FINAL+k,F,stride=3),:]=gf_ref[k*128:(k+1)*128,:].T
        for i in range(grads_ref.shape[0]*8):
            part=flat_ref[i*shard:(i+1)*shard,:]
            pad=grads_ref.shape[-2]-shard
            grads_ref[i//8,(i//4)%2,(i//2)%2,i%2]=jnp.concatenate([part,jnp.zeros((pad,128),F32)],axis=0).astype(BF)


def middle(conv,nodes,dy,mask3,stats,rows,gathered,shard):
    n=conv.shape[1]
    across=pl.BlockSpec((C,T),lambda i:(0,i))
    down=rows_of(C,T)
    flat_rows=gathered.shape[0]*8*shard
    in_specs=[across,across,across,pl.BlockSpec((T//128,1,128),lambda i:(i,0,0)),whole(*stats.shape),whole(*rows.shape),whole(*gathered.shape)]
    outs=[((n,C),BF,down),((n,C),F32,down),(gathered.shape,BF,whole(*gathered.shape)),((8,C),F32,whole(8,C))]
    mats=[]
    for shape in ((C,3*C),(C,C),(C,F),(F,C)): mats+=[(shape,BF),(shape[::-1],BF)]
    scr=[pltpu.VMEM(s,d) for s,d in [((flat_rows,128),F32),((4,C,128),F32),((ROW_CONV*128,128),F32)]+mats+[((C,3*C),F32),((C,C),F32),((C,F),F32),((C,F),F32),((10,C,128),F32),((F,128),F32),((C,T),F32),((C,T),F32),((3*C,T),BF),((T,C),BF),((T,C),BF),((HEADS,BLK,T),BF),((C,T),F32),((C,T),BF),((16,T),F32),((C,T),BF),((3*C,T),BF),((2,C,T),BF),((C,T),F32),((C,T),F32)]]
    return pl.pallas_call(functools.partial(mid_kernel,shard),grid=(n//T,),in_specs=in_specs,out_specs=[o[2] for o in outs],
      out_shape=[jax.ShapeDtypeStruct(o[0],o[1]) for o in outs],scratch_shapes=scr,
      compiler_params=VMEM)(conv,nodes,dy,mask3,stats,rows,gathered)


def shards(nodes_in, out_grad, neighbours, node_mask, master, first_moment, second_moment):
    n = nodes_in.shape[0]
    count, cores = lax.axis_size(AXES), lax.axis_size("grp")
    shard = master.shape[0] // 128
    mask3 = node_mask.reshape(n // 128, 1, 128)
    near = neighbours.T
    conv_t, conv, nodes_t, dy_t, gathered, first_rows, stats = convolve(
        near, nodes_in, out_grad, mask3, master.reshape(shard, 128), count, cores
    )
    output, delta_first, grads, norm_sums = middle(conv_t, nodes_t, dy_t, mask3, stats, first_rows, gathered, shard)
    node_grad, shard_delta, bias_total = convolve_back(
        near, delta_first, conv, nodes_in, mask3, norm_sums, stats, first_rows, grads, shard, count, cores
    )
    shard_delta = shard_delta.reshape(-1)
    position = lax.axis_index(AXES) * master.shape[0] + lax.iota(jnp.int32, master.shape[0])
    step_rate = jnp.where(position < 10 * C + F, 0.2, 0.03)
    new_first = 0.9 * first_moment + 0.1 * shard_delta
    new_second = 0.95 * second_moment + 0.05 * shard_delta * shard_delta
    first_hat = new_first / (1.0 - 0.9**STEP)
    second_hat = new_second / (1.0 - 0.95**STEP)
    new_master = master - step_rate * (first_hat / (jnp.sqrt(second_hat) + 1e-08) + 0.01 * master)
    return (
        output,
        node_grad.astype(F32),
        new_master,
        new_first,
        new_second,
        new_master.astype(BF),
        bias_total.reshape(-1),
    )


def solution(mesh):
    rows, flat = P(AXES, None), P(AXES)
    return jax.shard_map(
        shards,
        mesh=mesh,
        in_specs=(rows, rows, rows, flat, flat, flat, flat),
        out_specs=(rows, rows, flat, flat, flat, flat, P()),
        check_vma=False,
    )
```
